128 devices in a mesh: frame: 8 (over x_lo, z), space: 16 (over y, x_hi, core).
Axes of the slice: x: 4 (x_hi: 2, x_lo: 2; x = x_hi * 2 + x_lo), y: 4, z: 4, core: 2. Of those that a mesh axis runs over, the one named last changes fastest.
Arguments:
- latents: float32 [8, 1024, 128], P('frame', 'space'), may hold values from -6 to 6
- fresh_noise: float32 [2, 1024, 128], P(None, 'space'), may hold values from -6 to 6
- level_index: int32 [8], replicated, may hold values from 0 to 47, as said below
- plan: int32 [48], replicated, may hold values from 1 to 999, as said below
- frame_ids: int32 [10], replicated, may hold values from 5003 to 5030, as said below
- in_weight: bfloat16 [128, 3072], replicated, may hold values from -0.5 to 0.5
- cond_gain: float32 [2, 3072], replicated, may hold values from 0.1 to 1.9
- norm_gain: float32 [3072], replicated, may hold values from 0.1 to 1.9
- qkv_weight: bfloat16 [3, 3072, 3072], P(None, None, 'space'), may hold values from -0.109375 to 0.109375
- qk_gain: float32 [2, 64], replicated, may hold values from 0.5 to 4
- out_weight: bfloat16 [3072, 3072], replicated, may hold values from -0.109375 to 0.109375
- final_gain: float32 [3072], replicated, may hold values from 0.1 to 1.9
- final_weight: bfloat16 [3072, 128], replicated, may hold values from -0.109375 to 0.109375
Outputs:
- estimates: float32 [2, 8, 1024, 128], P(None, 'frame', 'space')
- queue: float32 [8, 1024, 128], P('frame', 'space')
The draws below stay inside these ranges and needn't reach their ends.
Inputs may be any that keep to these rules, and one draw needn't show every extreme that they name: `level_index`: strictly rising along the slots, from 0 in the first slot to 47 in the last. `plan`: strictly rising, from 1 to 999. `frame_ids`: strictly rising, in steps of 1 to 3, the last one 5000 + 3 * 10.
All inputs are finite; a program needn't handle non-finite values.
Results may differ from the reference program's by a relative error of at most 0.0095.
Values may be sent and summed in bfloat16 or wider, within the bound.
No kernel may reach another device: no remote copies, remote signals or barrier semaphores. Data moves between devices by JAX's collectives and lax.ppermute only.
A program may use at most 128 MiB of HBM per device.

```python
import math
import jax
import jax.numpy as jnp
from jax import lax

D = 3072
HEAD = 64
P_SIZE = 128
TABLE = 48
STEPS = 2
SLOTS = 8
GROUP = 1024


def rising_between(key, first, last, count):
    inner = jax.random.permutation(key, last - first - 1)[:count - 2] + first + 1
    middle = jnp.sort(inner.astype(jnp.int32))
    return jnp.concatenate([jnp.array([first], jnp.int32), middle, jnp.array([last], jnp.int32)]).astype(jnp.int32)


def draw_level_index(key, part):
    key = jax.random.fold_in(key, 11)
    return rising_between(key, 0, TABLE - 1, SLOTS)


def draw_plan(key, part):
    key = jax.random.fold_in(key, 12)
    return rising_between(key, 1, 999, TABLE)


def draw_frame_ids(key, part):
    key = jax.random.fold_in(key, 13)
    steps = jax.random.randint(key, (SLOTS + STEPS,), 1, 4)
    sums = jnp.cumsum(steps)
    top = 5000 + 3 * (SLOTS + STEPS)
    return (top - sums[-1] + sums).astype(jnp.int32)


def draw_qk_gain(key, part):
    key = jax.random.fold_in(key, 14)
    return jax.random.uniform(key, (2, HEAD), jnp.float32, 0.5, 1.5)


def level_of(rng, dims, cuts, least, top_value):
    level, own = 1.0, jax.random.fold_in(rng, 6)
    for dim, blocks in cuts:
        heights = jnp.exp(jax.random.uniform(jax.random.fold_in(own, dim), (blocks,), jnp.float32, least / len(cuts), top_value / len(cuts)))
        level = level * jnp.repeat(heights, dims[dim] // blocks).reshape([-1 if axis == dim else 1 for axis in range(len(dims))])
    return level


def noise(stream_key, extent, scale, bound, pieces=(), kind=jnp.bfloat16):
    loudness = level_of(stream_key, extent, pieces, -0.22, 0.18) if pieces else 1.0
    drawn = jax.random.normal(stream_key, extent, jnp.float32) * scale * loudness
    return jnp.minimum(jnp.maximum(drawn, -bound), bound).astype(kind)


def setup_inputs(seed: int = 0) -> dict:
    arg_keys = jax.random.split(jax.random.key(seed), 14)
    return {
        "latents": noise(arg_keys[0], (SLOTS, GROUP, P_SIZE), 1.0, 6.0, ((0, 8), (1, 16)), jnp.float32),
        "fresh_noise": noise(arg_keys[1], (STEPS, GROUP, P_SIZE), 1.0, 6.0, ((1, 16),), jnp.float32),
        "level_index": draw_level_index(jax.random.fold_in(arg_keys[13], 71), 0),
        "plan": draw_plan(jax.random.fold_in(arg_keys[13], 71), 0),
        "frame_ids": draw_frame_ids(jax.random.fold_in(arg_keys[13], 71), 0),
        "in_weight": noise(arg_keys[5], (P_SIZE, D), P_SIZE ** -0.5, 0.5),
        "cond_gain": jnp.clip(1.0 + 0.18 * jax.random.normal(arg_keys[6], (2, D), jnp.float32), 0.1, 1.9),
        "norm_gain": jnp.clip(1.0 + 0.18 * jax.random.normal(arg_keys[7], (D,), jnp.float32), 0.1, 1.9),
        "qkv_weight": noise(arg_keys[8], (3, D, D), D ** -0.5, 0.109375, ((2, 16),)),
        "qk_gain": draw_qk_gain(jax.random.fold_in(arg_keys[13], 71), 0),
        "out_weight": noise(arg_keys[10], (D, D), D ** -0.5, 0.109375),
        "final_gain": jnp.clip(1.0 + 0.18 * jax.random.normal(arg_keys[11], (D,), jnp.float32), 0.1, 1.9),
        "final_weight": noise(arg_keys[12], (D, P_SIZE), D ** -0.5, 0.109375),
    }


def waves(stamp, width):
    half = width // 2
    freqs = jnp.exp(-math.log(10000.0) * jnp.arange(half, dtype=jnp.float32) / half)
    angle = stamp * freqs
    return jnp.concatenate([jnp.cos(angle), jnp.sin(angle)])

def rms_scale(values, gain):
    return values * lax.rsqrt(lax.optimization_barrier(jnp.mean(values * values, axis=-1, keepdims=True)) + 1e-06) * gain

def embed(latent_b, stamp, frame_id, in_weight, cond_gain, norm_gain):
    width = in_weight.shape[1]
    hidden = jnp.dot(latent_b, in_weight, preferred_element_type=jnp.float32)
    hidden = hidden + cond_gain[0] * waves(stamp, width) + cond_gain[1] * waves(frame_id, width)
    return (hidden, rms_scale(hidden, norm_gain).astype(jnp.bfloat16))

def project_heads(normed, weight, gain_row, factor, width):
    rows = normed.shape[0]
    raw = jnp.dot(normed, weight, preferred_element_type=jnp.float32).reshape(rows, -1, width)
    return (rms_scale(raw, gain_row) * factor).astype(jnp.bfloat16)

def attend(query, key, value):
    rows = query.shape[0]
    size = min(512, rows)
    blocks = query.reshape(rows // size, size, query.shape[1], query.shape[2])
    key_f = key.astype(jnp.float32)
    value_f = value.astype(jnp.float32)

    def one_block(block):
        scores = jnp.einsum('qhd,khd->hqk', block.astype(jnp.float32), key_f)
        weights = jax.nn.softmax(scores, axis=-1).astype(jnp.bfloat16)
        return jnp.einsum('hqk,khd->qhd', weights.astype(jnp.float32), value_f).astype(jnp.bfloat16)
    return lax.map(one_block, blocks).reshape(rows, -1)

def reference(latents, fresh_noise, level_index, plan, frame_ids, in_weight, cond_gain, norm_gain, qkv_weight, qk_gain, out_weight, final_gain, final_weight):
    slots = latents.shape[0]
    stamps = plan[level_index].astype(jnp.float32)
    sigmas = stamps / 1000.0
    sigma_next = jnp.concatenate([jnp.zeros((1,), jnp.float32), sigmas[:-1]])
    scale = 1.0 / math.sqrt(HEAD)
    states = [latents[slot] for slot in range(slots)]
    outputs = []
    for step in range(STEPS):
        hiddens, queries, keys, values = ([], [], [], [])
        for slot in range(slots):
            latent_b = states[slot].astype(jnp.bfloat16)
            hidden, normed = embed(latent_b, stamps[slot], frame_ids[slot + step].astype(jnp.float32), in_weight, cond_gain, norm_gain)
            hiddens.append(hidden)
            queries.append(project_heads(normed, qkv_weight[0], qk_gain[0], scale, HEAD))
            keys.append(project_heads(normed, qkv_weight[1], qk_gain[1], 1.0, HEAD))
            rows = normed.shape[0]
            values.append(jnp.dot(normed, qkv_weight[2], preferred_element_type=jnp.float32).astype(jnp.bfloat16).reshape(rows, -1, HEAD))
        renewed = []
        step_estimates = []
        for slot in range(slots):
            if slot > 0:
                key_all = jnp.concatenate([keys[slot], keys[slot - 1]], axis=0)
                value_all = jnp.concatenate([values[slot], values[slot - 1]], axis=0)
            else:
                key_all, value_all = (keys[slot], values[slot])
            attended = attend(queries[slot], key_all, value_all)
            mixed = hiddens[slot] + jnp.dot(attended, out_weight, preferred_element_type=jnp.float32)
            velocity = jnp.dot(rms_scale(mixed, final_gain).astype(jnp.bfloat16), final_weight, preferred_element_type=jnp.float32)
            step_estimates.append(states[slot] - sigmas[slot] * velocity)
            renewed.append(states[slot] + (sigma_next[slot] - sigmas[slot]) * velocity)
        outputs.append(jnp.stack(step_estimates))
        states = renewed[1:] + [fresh_noise[step]]
    return (jnp.stack(outputs), jnp.stack(states))
```

```python
import functools
import math

import jax
import jax.numpy as jnp
from jax import lax
from jax.experimental import pallas as pl
from jax.experimental.pallas import tpu as pltpu
from jax.sharding import Mesh
from jax.sharding import PartitionSpec as P

HEAD = 64
STEPS = 2
FEAT = 128
WIDE = 256
CHIPS = 8
TOK = 64
COLS = 192
PACK = 48
PAY = 3 * COLS + PACK + 2 * TOK
HEADS = CHIPS * 3
GROUPS = HEADS // 4
KEYS = 2048
ONE = 136
EPS = 1e-06
SAFE = 60.0

BF = jnp.bfloat16
F32 = jnp.float32
VMEM = pl.BlockSpec(memory_space=pltpu.VMEM)
SMEM = pl.BlockSpec(memory_space=pltpu.SMEM)
ANY = pl.BlockSpec(memory_space=pl.ANY)


def dot(a, b):
    return jnp.dot(a, b, preferred_element_type=F32)


def dot_t(a, b):
    return lax.dot_general(a, b, (((1,), (1,)), ((), ())), preferred_element_type=F32)


def halves(x):
    high = x.astype(BF)
    return high, (x - high.astype(F32)).astype(BF)


def lanes(shape):
    return lax.broadcasted_iota(jnp.int32, shape, len(shape) - 1)


def rows(shape):
    return lax.broadcasted_iota(jnp.int32, shape, len(shape) - 2)


def fold_kernel(qkv_ref, in_ref, cond_ref, gain_ref, x_ref, prev_ref, pay_ref, gram_hi_ref, gram_lo_ref):
    gain = gain_ref[...]
    cond = cond_ref[...]
    embed = in_ref[...]
    emb_hi, emb_lo = halves(embed.astype(F32) * gain)
    cg_hi, cg_lo = halves(jnp.concatenate([cond, jnp.zeros_like(cond)], axis=0) * gain)
    left = jnp.concatenate([emb_hi, emb_lo, cg_hi, cg_lo], axis=0)
    packed = jnp.zeros((PACK, FEAT), F32)
    for j in range(3):
        full = dot(left, qkv_ref[j])
        mat = full[0:128] + full[128:256]
        bias = full[256:264] + full[272:280]
        high = bias.astype(BF).astype(F32)
        bias = jnp.where(rows(bias.shape) < 4, high, bias - high)
        mat_t = jnp.transpose(mat).astype(BF)
        bias = jnp.concatenate([bias, jnp.zeros((120, COLS), F32)], axis=0)
        bias_t = jnp.transpose(bias)
        for i in range(4):
            part = bias_t[PACK * i : PACK * (i + 1)]
            shift = 8 * (4 * j + i)
            packed = packed + (pltpu.roll(part, shift, 1) if shift else part)
        for chip in range(CHIPS):
            pay_ref[chip, COLS * j : COLS * (j + 1)] = mat_t
    packed = packed.astype(BF)
    for chip in range(CHIPS):
        pay_ref[chip, 3 * COLS : 3 * COLS + PACK] = packed
        pay_ref[chip, 3 * COLS + PACK : PAY - TOK] = x_ref[...]
        pay_ref[chip, PAY - TOK : PAY] = prev_ref[...]
    c_hi, c_lo = halves(cond)
    four = rows(cond.shape) < 4
    c_hi = jnp.where(four, c_hi.astype(F32), 0.0).astype(BF)
    c_lo = jnp.where(four, c_lo.astype(F32), 0.0).astype(BF)
    none = jnp.zeros((120, embed.shape[1]), BF)
    l_hi = jnp.concatenate([embed, jnp.concatenate([c_hi, none], axis=0)], axis=0)
    l_lo = jnp.concatenate([jnp.zeros_like(embed), jnp.concatenate([c_lo, none], axis=0)], axis=0)
    gram = dot_t(l_hi, l_hi) + dot_t(l_hi, l_lo) + dot_t(l_lo, l_hi)
    g_hi, g_lo = halves(gram)
    gram_hi_ref[...] = g_hi
    gram_lo_ref[...] = g_lo


def fold(qkv, in_weight, cond, gain, x, prev):
    return pl.pallas_call(
        fold_kernel,
        out_shape=(
            jax.ShapeDtypeStruct((CHIPS, PAY, FEAT), BF),
            jax.ShapeDtypeStruct((WIDE, WIDE), BF),
            jax.ShapeDtypeStruct((WIDE, WIDE), BF),
        ),
        in_specs=[VMEM] * 6,
        out_specs=(VMEM,) * 3,
        compiler_params=pltpu.CompilerParams(vmem_limit_bytes=40 * 2**20),
        name="fold",
    )(qkv, in_weight, cond, gain, x, prev)


def attend_kernel(
    step,
    place_ref,
    safe_ref,
    pay_ref,
    mine_ref,
    other_ref,
    gram_hi_ref,
    gram_lo_ref,
    qk_ref,
    out_w_ref,
    part_ref,
    part_other_ref,
    xk_ref,
    xkt_ref,
    val_ref,
    aq_ref,
    ak_ref,
    av_ref,
    rk_ref,
    p_ref,
    s_ref,
    acc_ref,
    w_ref,
    sem,
):
    chip, core = place_ref[0], place_ref[1]
    copies = []
    for m in range(CHIPS):
        begin = pl.multiple_of((2 * m + core) * COLS, COLS)
        copies.append(pltpu.make_async_copy(out_w_ref.at[pl.ds(begin, COLS)], w_ref.at[pl.ds(m * COLS, COLS)], sem))
    for copy in copies:
        copy.start()

    half = CHIPS * TOK
    for group in range(2):
        for side, ref in enumerate((mine_ref, other_ref)):
            base = (2 * group + side) * half
            block = ref[:, TOK * group : TOK * (group + 1), :].reshape(half, FEAT)
            xk_ref[base : base + half, 0:FEAT] = block
        lane = lanes((KEYS // 2, FEAT))
        mark = jnp.logical_or(lane == 2 * step + group, lane == 4 + 2 * step + group)
        xk_ref[group * KEYS // 2 : (group + 1) * KEYS // 2, FEAT:WIDE] = mark.astype(F32).astype(BF)
    xkt_ref[0:FEAT, :] = jnp.transpose(xk_ref[:, 0:FEAT])
    row = rows((FEAT, KEYS))
    group = (lanes((FEAT, KEYS)) >= KEYS // 2).astype(jnp.int32)
    mark = jnp.logical_or(row == 2 * step + group, row == 4 + 2 * step + group)
    xkt_ref[FEAT:WIDE, :] = mark.astype(F32).astype(BF)

    xkt = xkt_ref[...]
    square = dot(gram_hi_ref[...], xkt) + dot(gram_lo_ref[...], xkt)
    m_row = jnp.sum(square * xkt.astype(F32), axis=0, keepdims=True) * (1.0 / 3072.0) + EPS
    r_col = jnp.transpose(jnp.broadcast_to(lax.rsqrt(m_row), (8, KEYS)))[:, 0:1]
    val = xk_ref[...].astype(F32) * r_col
    val_ref[...] = jnp.where(lanes((KEYS, WIDE)) == ONE, 1.0, val).astype(BF)

    lane = lanes((PACK, FEAT))
    for m in range(CHIPS):
        packed = pay_ref[m, 3 * COLS : 3 * COLS + PACK, :].astype(F32)
        for j, ref in enumerate((aq_ref, ak_ref, av_ref)):
            ref[m * COLS : (m + 1) * COLS, 0:FEAT] = pay_ref[m, j * COLS : (j + 1) * COLS, :]
            for i in range(4):
                shift = 8 * (4 * j + i)
                part = pltpu.roll(packed, FEAT - shift, 1) if shift else packed
                part = jnp.where(lane < 8, part, 0.0)
                ref[m * COLS + i * PACK : m * COLS + (i + 1) * PACK, FEAT:WIDE] = part.astype(BF)

    xq = jnp.concatenate([mine_ref[chip, 0:TOK, :], other_ref[chip, 0:TOK, :]], axis=0)
    lane = lanes((2 * TOK, FEAT))
    mark = jnp.logical_or(lane == 2 * step, lane == 4 + 2 * step)
    xq = jnp.concatenate([xq, mark.astype(F32).astype(BF)], axis=1)
    square = dot(xq, gram_hi_ref[...]) + dot(xq, gram_lo_ref[...])
    m_q = jnp.sum(square * xq.astype(F32), axis=1, keepdims=True) * (1.0 / 3072.0) + EPS
    ones = (rows((WIDE, WIDE)) // HEAD == lanes((WIDE, WIDE)) // HEAD).astype(F32).astype(BF)
    head_of = lanes((2 * TOK, WIDE)) // HEAD

    def one_group(g, fast):
        begin = pl.multiple_of(g * WIDE, WIDE)
        ak = ak_ref[pl.ds(begin, WIDE), :]
        u = dot(ak, xkt_ref[...])
        u = jnp.sum((u * u).reshape(4, HEAD, KEYS), axis=1)
        rk = lax.rsqrt(u * (1.0 / HEAD) + EPS * m_row)
        q = dot_t(xq, aq_ref[pl.ds(begin, WIDE), :])
        sq_hi, sq_lo = halves(q * q)
        mean = (dot(sq_hi, ones) + dot(sq_lo, ones)) * (1.0 / HEAD)
        q = q * lax.rsqrt(mean + EPS * m_q) * qk_ref[...]
        q = jnp.concatenate([jnp.where(head_of == h, q, 0.0) for h in range(4)], axis=0)
        carried = dot(q.astype(BF), ak).astype(BF)
        if fast:
            for h in range(4):
                s = dot(carried[128 * h : 128 * (h + 1)], xkt_ref[...])
                p_ref[128 * h : 128 * (h + 1), :] = jnp.exp2(s * rk[h : h + 1]).astype(BF)
        else:
            for h in range(4):
                s_ref[...] = dot(carried[128 * h : 128 * (h + 1)], xkt_ref[...]) * rk[h : h + 1]
                s = s_ref[...]
                s = s - jnp.max(s, axis=1, keepdims=True)
                p_ref[128 * h : 128 * (h + 1), :] = jnp.exp2(s).astype(BF)
        z = dot(p_ref[...], val_ref[...])
        z = (z * (1.0 / z[:, ONE : ONE + 1])).astype(BF)
        o = dot_t(z, av_ref[pl.ds(begin, WIDE), :])
        picked = jnp.where(head_of == 0, o[0:128], 0.0)
        for h in range(1, 4):
            picked = jnp.where(head_of == h, o[128 * h : 128 * (h + 1)], picked)
        acc_ref[g] = picked.astype(BF)

    @pl.when(safe_ref[0] == 1)
    def _():
        def body(g, carry):
            one_group(g, True)
            return carry

        lax.fori_loop(0, GROUPS, body, 0)

    @pl.when(safe_ref[0] != 1)
    def _():
        def body(g, carry):
            one_group(g, False)
            return carry

        lax.fori_loop(0, GROUPS, body, 0)

    for copy in copies:
        copy.wait()
    o = jnp.concatenate([acc_ref[g] for g in range(GROUPS)], axis=1)
    y = dot(o, w_ref[...])
    part_ref[...] = y[0:TOK]
    part_other_ref[...] = y[TOK:]


def attend(step, place, safe, pay, mine, other, gram_hi, gram_lo, qk, out_weight):
    width = out_weight.shape[1]
    part = jax.ShapeDtypeStruct((TOK, width), F32)
    half = HEADS * HEAD
    return pl.pallas_call(
        functools.partial(attend_kernel, step),
        out_shape=(part, part),
        in_specs=[SMEM, SMEM] + [VMEM] * 6 + [ANY],
        out_specs=(VMEM, VMEM),
        scratch_shapes=[
            pltpu.VMEM((KEYS, WIDE), BF),
            pltpu.VMEM((WIDE, KEYS), BF),
            pltpu.VMEM((KEYS, WIDE), BF),
            pltpu.VMEM((half, WIDE), BF),
            pltpu.VMEM((half, WIDE), BF),
            pltpu.VMEM((half, WIDE), BF),
            pltpu.VMEM((HEADS, KEYS), F32),
            pltpu.VMEM((512, KEYS), BF),
            pltpu.VMEM((128, KEYS), F32),
            pltpu.VMEM((GROUPS, 2 * TOK, WIDE), BF),
            pltpu.VMEM((half, width), BF),
            pltpu.SemaphoreType.DMA,
        ],
        compiler_params=pltpu.CompilerParams(vmem_limit_bytes=56 * 2**20),
        name="attend",
    )(place, safe, pay, mine, other, gram_hi, gram_lo, qk, out_weight)


def finish_kernel(step, sig_ref, state_ref, in_ref, cond_ref, part_ref, got_ref, gain_ref, final_ref, est_ref, new_ref):
    state = state_ref[...]
    y = dot(state.astype(BF), in_ref[...]) + cond_ref[2 * step : 2 * step + 1, :]
    y = y + part_ref[...] + got_ref[...]
    scale = lax.rsqrt(jnp.mean(y * y, axis=1, keepdims=True) + EPS)
    velocity = dot((y * scale * gain_ref[...]).astype(BF), final_ref[...])
    est_ref[...] = state - sig_ref[0] * velocity
    new_ref[...] = state + sig_ref[1] * velocity


def finish(step, sig, state, in_weight, cond, part, got, gain, final_weight):
    out = jax.ShapeDtypeStruct(state.shape, F32)
    return pl.pallas_call(
        functools.partial(finish_kernel, step),
        out_shape=(out, out),
        in_specs=[SMEM] + [VMEM] * 7,
        out_specs=(VMEM, VMEM),
        compiler_params=pltpu.CompilerParams(vmem_limit_bytes=32 * 2**20),
        name="finish",
    )(sig, state, in_weight, cond, part, got, gain, final_weight)


def passed_along(x, by):
    peers = lax.axis_size("frame")
    pairs = [(i, i + by) for i in range(peers) if 0 <= i + by < peers]
    return lax.ppermute(x, "frame", pairs)


def swapped(x):
    return lax.ppermute(x, "core", [(0, 1), (1, 0)])


def spread(x):
    return lax.all_to_all(x, ("y", "far"), 0, 0, tiled=True)


def waves(stamp, width):
    half = width // 2
    freqs = jnp.exp(-math.log(10000.0) * jnp.arange(half, dtype=F32) / half)
    angle = stamp * freqs
    return jnp.concatenate([jnp.cos(angle), jnp.sin(angle)])


def pick(table, where):
    return jnp.sum(jnp.where(jnp.arange(table.shape[0]) == where, table, 0))


def shards(
    latents,
    fresh_noise,
    level_index,
    plan,
    frame_ids,
    in_weight,
    cond_gain,
    norm_gain,
    qkv_weight,
    qk_gain,
    out_weight,
    final_gain,
    final_weight,
):
    slot = lax.axis_index("frame")
    count = lax.axis_size("frame")
    width = in_weight.shape[1]
    state = latents[0]
    x = state.astype(BF)
    prev = jnp.where(slot == 0, x, passed_along(x, 1))

    before = jnp.maximum(slot - 1, 0)
    stamp_now = pick(plan, pick(level_index, slot)).astype(F32)
    stamp_prev = pick(plan, pick(level_index, before)).astype(F32)
    sigma = stamp_now / 1000.0
    sigma_next = jnp.where(slot > 0, stamp_prev / 1000.0, jnp.float32(0.0))
    sig = jnp.stack([sigma, sigma_next - sigma])
    wave_now = cond_gain[0] * waves(stamp_now, width)
    wave_prev = cond_gain[0] * waves(stamp_prev, width)
    conds = []
    for step in range(STEPS):
        id_now = pick(frame_ids, slot + step).astype(F32)
        id_prev = pick(frame_ids, before + step).astype(F32)
        conds.append(wave_now + cond_gain[1] * waves(id_now, width))
        conds.append(wave_prev + cond_gain[1] * waves(id_prev, width))
    cond = jnp.stack(conds + conds)

    product = qk_gain[0] * qk_gain[1]
    safe = (HEAD**0.5 * jnp.max(jnp.abs(product)) <= SAFE).astype(jnp.int32)[None]
    qk = jnp.tile(product * (math.log2(math.e) / math.sqrt(HEAD)), 4)[None]
    place = jnp.stack([lax.axis_index(("y", "far")), lax.axis_index("core")]).astype(jnp.int32)

    sent, gram_hi, gram_lo = fold(qkv_weight, in_weight, cond, norm_gain[None], x, prev)
    pay = spread(sent)
    mine = pay[:, PAY - 2 * TOK :, :]
    results = []
    for step in range(STEPS):
        other = swapped(mine)
        part, part_other = attend(step, place, safe, pay, mine, other, gram_hi, gram_lo, qk, out_weight)
        got = swapped(part_other)
        estimate, renewed = finish(step, sig, state, in_weight, cond, part, got, final_gain[None], final_weight)
        results.append(estimate)
        state = jnp.where(slot == count - 1, fresh_noise[step], passed_along(renewed, -1))
        if step + 1 < STEPS:
            x = state.astype(BF)
            prev = jnp.where(slot == 0, x, renewed.astype(BF))
            both = jnp.concatenate([x, prev], axis=0)
            mine = spread(jnp.broadcast_to(both[None], (CHIPS,) + both.shape))
    return (jnp.stack(results)[:, None], state[None])


def solution(mesh):
    split = Mesh(mesh.devices.reshape(8, 4, 2, 2), ("frame", "y", "far", "core"))
    space = ("y", "far", "core")
    in_specs = (
        P("frame", space, None),
        P(None, space, None),
        P(),
        P(),
        P(),
        P(),
        P(),
        P(),
        P(None, None, space),
        P(),
        P(),
        P(),
        P(),
    )
    out_specs = (P(None, "frame", space, None), P("frame", space, None))
    return jax.shard_map(shards, mesh=split, in_specs=in_specs, out_specs=out_specs, check_vma=False)
```

```python
import functools
import math

import jax
import jax.numpy as jnp
from jax import lax
from jax.experimental import pallas as pl
from jax.experimental.pallas import tpu as pltpu
from jax.sharding import Mesh
from jax.sharding import PartitionSpec as P

HEAD = 64
STEPS = 2
FEAT = 128
WIDE = 256
CHIPS = 8
TOK = 64
COLS = 192
PACK = 48
PAY = 3 * COLS + PACK + 2 * TOK
HEADS = CHIPS * 3
GROUPS = HEADS // 4
KEYS = 2048
ONE = 136
EPS = 1e-06
SAFE = 60.0

BF = jnp.bfloat16
F32 = jnp.float32
VMEM = pl.BlockSpec(memory_space=pltpu.VMEM)
SMEM = pl.BlockSpec(memory_space=pltpu.SMEM)
ANY = pl.BlockSpec(memory_space=pl.ANY)


def dot(a, b):
    return jnp.dot(a, b, preferred_element_type=F32)


def dot_t(a, b):
    return lax.dot_general(a, b, (((1,), (1,)), ((), ())), preferred_element_type=F32)


def halves(x):
    high = x.astype(BF)
    return high, (x - high.astype(F32)).astype(BF)


def in_vmem(x):
    return pltpu.with_memory_space_constraint(x, pltpu.VMEM)


def lanes(shape):
    return lax.broadcasted_iota(jnp.int32, shape, len(shape) - 1)


def rows(shape):
    return lax.broadcasted_iota(jnp.int32, shape, len(shape) - 2)


def fold_kernel(
    level_ref,
    plan_ref,
    ids_ref,
    freq_ref,
    qkv_ref,
    in_ref,
    cond_gain_ref,
    gain_ref,
    qk_gain_ref,
    state_ref,
    pay_ref,
    gram_hi_ref,
    gram_lo_ref,
    cond_ref,
    qk_ref,
    safe_ref,
    sig_ref,
    w_ref,
    sems,
):
    copies = [pltpu.make_async_copy(qkv_ref.at[j], w_ref.at[j], sems.at[j]) for j in range(3)]
    for copy in copies:
        copy.start()

    slot = lax.axis_index("frame")
    before = jnp.maximum(slot - 1, 0)
    stamp_now = plan_ref[level_ref[slot]].astype(F32)
    stamp_prev = plan_ref[level_ref[before]].astype(F32)
    sigma = stamp_now / 1000.0
    sig_ref[0] = sigma
    sig_ref[1] = jnp.where(slot > 0, stamp_prev / 1000.0, 0.0) - sigma

    product = qk_gain_ref[0:1, :] * qk_gain_ref[1:2, :]
    safe_ref[0] = (HEAD**0.5 * jnp.max(jnp.abs(product)) <= SAFE).astype(jnp.int32)
    product = product * (math.log2(math.e) / math.sqrt(HEAD))
    qk_ref[...] = jnp.concatenate([product] * 4, axis=1)

    row = rows((8, freq_ref.shape[1]))
    stamp = jnp.where(row % 2 == 0, stamp_now, stamp_prev)
    ident = jnp.zeros_like(stamp)
    for step in range(STEPS):
        now = ids_ref[slot + step].astype(F32)
        prev = ids_ref[before + step].astype(F32)
        ident = jnp.where((row // 2) % 2 == step, jnp.where(row % 2 == 0, now, prev), ident)
    freq = freq_ref[...]
    wave_stamp = jnp.concatenate([jnp.cos(stamp * freq), jnp.sin(stamp * freq)], axis=1)
    wave_ident = jnp.concatenate([jnp.cos(ident * freq), jnp.sin(ident * freq)], axis=1)
    cond = cond_gain_ref[0:1, :] * wave_stamp + cond_gain_ref[1:2, :] * wave_ident
    cond_ref[...] = cond

    embed = in_ref[...]
    c_hi, c_lo = halves(cond)
    four = rows(cond.shape) < 4
    c_hi = jnp.where(four, c_hi.astype(F32), 0.0).astype(BF)
    c_lo = jnp.where(four, c_lo.astype(F32), 0.0).astype(BF)
    none = jnp.zeros((120, embed.shape[1]), BF)
    l_hi = jnp.concatenate([embed, jnp.concatenate([c_hi, none], axis=0)], axis=0)
    l_lo = jnp.concatenate([jnp.zeros_like(embed), jnp.concatenate([c_lo, none], axis=0)], axis=0)
    gram = dot_t(l_hi, l_hi) + dot_t(l_hi, l_lo) + dot_t(l_lo, l_hi)
    g_hi, g_lo = halves(gram)
    gram_hi_ref[...] = g_hi
    gram_lo_ref[...] = g_lo

    gain = gain_ref[...]
    emb_hi, emb_lo = halves(embed.astype(F32) * gain)
    cg_hi, cg_lo = halves(cond * gain)
    none = jnp.zeros((112, embed.shape[1]), BF)
    right = jnp.concatenate([emb_hi, jnp.concatenate([cg_hi, cg_lo], axis=0), none], axis=0)
    packed = jnp.zeros((PACK, FEAT), F32)
    for j in range(3):
        copies[j].wait()
        full = dot_t(w_ref[j], right)
        mat = (full[:, 0:FEAT] + dot_t(w_ref[j], emb_lo)).astype(BF)
        bias = full[:, FEAT:WIDE]
        bias = bias + pltpu.roll(bias, FEAT - 8, 1)
        bias = jnp.where(lanes(bias.shape) < 8, bias, 0.0)
        high = bias.astype(BF).astype(F32)
        bias = jnp.where(lanes(bias.shape) < 4, high, bias - high)
        for i in range(4):
            part = bias[PACK * i : PACK * (i + 1)]
            shift = 8 * (4 * j + i)
            packed = packed + (pltpu.roll(part, shift, 1) if shift else part)
        for chip in range(CHIPS):
            pay_ref[chip, COLS * j : COLS * (j + 1)] = mat
    packed = packed.astype(BF)
    x = state_ref[0].astype(BF)
    for chip in range(CHIPS):
        pay_ref[chip, 3 * COLS : 3 * COLS + PACK] = packed
        pay_ref[chip, 3 * COLS + PACK : PAY - TOK] = x
        pay_ref[chip, PAY - TOK : PAY] = x


def fold(level_index, plan, frame_ids, freq, qkv, in_weight, cond_gain, gain, qk_gain, latents):
    width = in_weight.shape[1]
    return pl.pallas_call(
        fold_kernel,
        out_shape=(
            pltpu.VMEM((CHIPS, PAY, FEAT), BF),
            pltpu.VMEM((WIDE, WIDE), BF),
            pltpu.VMEM((WIDE, WIDE), BF),
            pltpu.VMEM((8, width), F32),
            pltpu.VMEM((1, WIDE), F32),
            jax.ShapeDtypeStruct((1,), jnp.int32),
            jax.ShapeDtypeStruct((2,), F32),
        ),
        in_specs=[SMEM] * 3 + [VMEM, ANY] + [VMEM] * 5,
        out_specs=(VMEM,) * 5 + (SMEM,) * 2,
        scratch_shapes=[pltpu.VMEM(qkv.shape, BF), pltpu.SemaphoreType.DMA((3,))],
        compiler_params=pltpu.CompilerParams(vmem_limit_bytes=40 * 2**20),
        name="fold",
    )(level_index, plan, frame_ids, freq, qkv, in_weight, cond_gain, gain, qk_gain, latents)


def attend_kernel(
    step,
    safe_ref,
    pay_ref,
    mine_ref,
    other_ref,
    gram_hi_ref,
    gram_lo_ref,
    qk_ref,
    out_w_ref,
    part_ref,
    part_other_ref,
    xk_ref,
    xkt_ref,
    val_ref,
    aq_ref,
    ak_ref,
    av_ref,
    rk_ref,
    p_ref,
    s_ref,
    qc_ref,
    z_ref,
    w_ref,
    sem,
):
    chip, core = lax.axis_index(("y", "far")), lax.axis_index("core")
    first = lax.axis_index("frame") == 0
    copies = []
    for m in range(CHIPS):
        begin = pl.multiple_of((2 * m + core) * COLS, COLS)
        copies.append(pltpu.make_async_copy(out_w_ref.at[pl.ds(begin, COLS)], w_ref.at[pl.ds(m * COLS, COLS)], sem))
    for copy in copies:
        copy.start()

    half = CHIPS * TOK
    for group in range(2):
        for side, ref in enumerate((mine_ref, other_ref)):
            base = (2 * group + side) * half
            block = ref[:, TOK * group : TOK * (group + 1), :].reshape(half, FEAT)
            if group == 1:
                block = jnp.where(first, ref[:, 0:TOK, :].reshape(half, FEAT), block)
            xk_ref[base : base + half, 0:FEAT] = block
        lane = lanes((KEYS // 2, FEAT))
        mark = jnp.logical_or(lane == 2 * step + group, lane == 4 + 2 * step + group)
        xk_ref[group * KEYS // 2 : (group + 1) * KEYS // 2, FEAT:WIDE] = mark.astype(F32).astype(BF)
    xkt_ref[0:FEAT, :] = jnp.transpose(xk_ref[:, 0:FEAT])
    row = rows((FEAT, KEYS))
    group = (lanes((FEAT, KEYS)) >= KEYS // 2).astype(jnp.int32)
    mark = jnp.logical_or(row == 2 * step + group, row == 4 + 2 * step + group)
    xkt_ref[FEAT:WIDE, :] = mark.astype(F32).astype(BF)

    xkt = xkt_ref[...]
    square = dot(gram_hi_ref[...], xkt) + dot(gram_lo_ref[...], xkt)
    m_row = jnp.sum(square * xkt.astype(F32), axis=0, keepdims=True) * (1.0 / 3072.0) + EPS
    r_col = jnp.transpose(jnp.broadcast_to(lax.rsqrt(m_row), (8, KEYS)))[:, 0:1]
    val = xk_ref[...].astype(F32) * r_col
    val_ref[...] = jnp.where(lanes((KEYS, WIDE)) == ONE, 1.0, val).astype(BF)

    lane = lanes((PACK, FEAT))
    for m in range(CHIPS):
        packed = pay_ref[m, 3 * COLS : 3 * COLS + PACK, :].astype(F32)
        for j, ref in enumerate((aq_ref, ak_ref, av_ref)):
            ref[m * COLS : (m + 1) * COLS, 0:FEAT] = pay_ref[m, j * COLS : (j + 1) * COLS, :]
            for i in range(4):
                shift = 8 * (4 * j + i)
                part = pltpu.roll(packed, FEAT - shift, 1) if shift else packed
                part = jnp.where(lane < 8, part, 0.0)
                ref[m * COLS + i * PACK : m * COLS + (i + 1) * PACK, FEAT:WIDE] = part.astype(BF)

    xq = jnp.concatenate([mine_ref[chip, 0:TOK, :], other_ref[chip, 0:TOK, :]], axis=0)
    lane = lanes((2 * TOK, FEAT))
    mark = jnp.logical_or(lane == 2 * step, lane == 4 + 2 * step)
    xq = jnp.concatenate([xq, mark.astype(F32).astype(BF)], axis=1)
    square = dot(xq, gram_hi_ref[...]) + dot(xq, gram_lo_ref[...])
    m_q = jnp.sum(square * xq.astype(F32), axis=1, keepdims=True) * (1.0 / 3072.0) + EPS
    ones = (rows((WIDE, WIDE)) // HEAD == lanes((WIDE, WIDE)) // HEAD).astype(F32).astype(BF)
    head_of = lanes((2 * TOK, WIDE)) // HEAD

    def norms(g, carry):
        begin = pl.multiple_of(g * WIDE, WIDE)
        u = dot(ak_ref[pl.ds(begin, WIDE), :], xkt_ref[...])
        u = jnp.sum((u * u).reshape(4, HEAD, KEYS), axis=1)
        rk = lax.rsqrt(u * (1.0 / HEAD) + EPS * m_row)
        rk_ref[g] = jnp.concatenate([rk, rk], axis=0)
        return carry

    lax.fori_loop(0, GROUPS, norms, 0, unroll=True)

    for g in range(GROUPS):
        span = slice(g * WIDE, (g + 1) * WIDE)
        q = dot_t(xq, aq_ref[span, :])
        sq_hi, sq_lo = halves(q * q)
        mean = (dot(sq_hi, ones) + dot(sq_lo, ones)) * (1.0 / HEAD)
        q = q * lax.rsqrt(mean + EPS * m_q) * qk_ref[...]
        q = jnp.concatenate([jnp.where(head_of == h, q, 0.0) for h in range(4)], axis=0)
        qc_ref[g] = dot(q.astype(BF), ak_ref[span, :]).astype(BF)

    def one_group(g, fast):
        carried = qc_ref[g]
        rk = rk_ref[g]
        for h in range(4):
            span = slice(2 * TOK * h, 2 * TOK * (h + 1))
            s = dot(carried[span], xkt_ref[...]) * rk[h : h + 1]
            if not fast:
                s_ref[...] = s
                s = s_ref[...]
                s = s - jnp.max(s, axis=1, keepdims=True)
            p_ref[span, :] = jnp.exp2(s).astype(BF)
        for h in range(4):
            span = slice(2 * TOK * h, 2 * TOK * (h + 1))
            z = dot(p_ref[span, :], val_ref[...])
            z_ref[g, span] = (z * (1.0 / z[:, ONE : ONE + 1])).astype(BF)

    @pl.when(safe_ref[0] == 1)
    def _():
        def body(g, carry):
            one_group(g, True)
            return carry

        lax.fori_loop(0, GROUPS, body, 0, unroll=3)

    @pl.when(safe_ref[0] != 1)
    def _():
        def body(g, carry):
            one_group(g, False)
            return carry

        lax.fori_loop(0, GROUPS, body, 0)

    outs = []
    for g in range(GROUPS):
        o = dot_t(z_ref[g], av_ref[g * WIDE : (g + 1) * WIDE, :])
        picked = jnp.where(head_of == 0, o[0:128], 0.0)
        for h in range(1, 4):
            picked = jnp.where(head_of == h, o[128 * h : 128 * (h + 1)], picked)
        outs.append(picked.astype(BF))
    for copy in copies:
        copy.wait()
    y = dot(jnp.concatenate(outs, axis=1), w_ref[...])
    part_ref[...] = y[0:TOK]
    part_other_ref[...] = y[TOK:].astype(BF)


def attend(step, safe, pay, mine, other, gram_hi, gram_lo, qk, out_weight):
    width = out_weight.shape[1]
    half = HEADS * HEAD
    return pl.pallas_call(
        functools.partial(attend_kernel, step),
        out_shape=(pltpu.VMEM((TOK, width), F32), pltpu.VMEM((TOK, width), BF)),
        in_specs=[SMEM] + [VMEM] * 6 + [ANY],
        out_specs=(VMEM, VMEM),
        scratch_shapes=[
            pltpu.VMEM((KEYS, WIDE), BF),
            pltpu.VMEM((WIDE, KEYS), BF),
            pltpu.VMEM((KEYS, WIDE), BF),
            pltpu.VMEM((half, WIDE), BF),
            pltpu.VMEM((half, WIDE), BF),
            pltpu.VMEM((half, WIDE), BF),
            pltpu.VMEM((GROUPS, 8, KEYS), F32),
            pltpu.VMEM((512, KEYS), BF),
            pltpu.VMEM((128, KEYS), F32),
            pltpu.VMEM((GROUPS, 512, WIDE), BF),
            pltpu.VMEM((GROUPS, 512, WIDE), BF),
            pltpu.VMEM((half, width), BF),
            pltpu.SemaphoreType.DMA,
        ],
        compiler_params=pltpu.CompilerParams(vmem_limit_bytes=56 * 2**20),
        name="attend",
    )(safe, *[in_vmem(v) for v in (pay, mine, other, gram_hi, gram_lo, qk)], out_weight)


def finish_kernel(
    step, sig_ref, state_ref, in_ref, cond_ref, part_ref, got_ref, gain_ref, final_ref, fresh_ref, est_ref, sent_ref, prev_ref
):
    state = state_ref[...]
    y = dot(state.astype(BF), in_ref[...]) + cond_ref[2 * step : 2 * step + 1, :]
    y = y + part_ref[...] + got_ref[...].astype(F32)
    scale = lax.rsqrt(jnp.mean(y * y, axis=1, keepdims=True) + EPS)
    velocity = dot((y * scale * gain_ref[...]).astype(BF), final_ref[...])
    est_ref[...] = state - sig_ref[0] * velocity
    renewed = state + sig_ref[1] * velocity
    sent_ref[...] = jnp.where(lax.axis_index("frame") == 0, fresh_ref[step], renewed)
    prev_ref[...] = renewed.astype(BF)


def finish(step, sig, state, in_weight, cond, part, got, gain, final_weight, fresh):
    out = jax.ShapeDtypeStruct(state.shape, F32)
    return pl.pallas_call(
        functools.partial(finish_kernel, step),
        out_shape=(out, out, jax.ShapeDtypeStruct(state.shape, BF)),
        in_specs=[SMEM] + [VMEM] * 8,
        out_specs=(VMEM,) * 3,
        compiler_params=pltpu.CompilerParams(vmem_limit_bytes=32 * 2**20),
        name="finish",
    )(sig, state, in_weight, in_vmem(cond), in_vmem(part), in_vmem(got), gain, final_weight, fresh)


def passed_along(x, by):
    peers = lax.axis_size("frame")
    return lax.ppermute(x, "frame", [(i, (i + by) % peers) for i in range(peers)])


def swapped(x):
    return lax.ppermute(x, "core", [(0, 1), (1, 0)])


def spread(x):
    return lax.all_to_all(x, ("y", "far"), 0, 0, tiled=True)


def shards(
    latents,
    fresh_noise,
    level_index,
    plan,
    frame_ids,
    in_weight,
    cond_gain,
    norm_gain,
    qkv_weight,
    qk_gain,
    out_weight,
    final_gain,
    final_weight,
):
    half = in_weight.shape[1] // 2
    freq = jnp.exp(-math.log(10000.0) * jnp.arange(half, dtype=F32) / half)
    state = latents[0]
    prev = passed_along(state, 1).astype(BF)
    sent, gram_hi, gram_lo, cond, qk, safe, sig = fold(
        level_index,
        plan,
        frame_ids,
        freq[None],
        jnp.swapaxes(qkv_weight, 1, 2),
        in_weight,
        cond_gain,
        norm_gain[None],
        qk_gain,
        latents,
    )
    pay = spread(sent.at[:, PAY - TOK :, :].set(prev[None]))
    mine = pay[:, PAY - 2 * TOK :, :]
    results = []
    for step in range(STEPS):
        other = swapped(mine)
        part, part_other = attend(step, safe, pay, mine, other, gram_hi, gram_lo, qk, out_weight)
        got = swapped(part_other)
        estimate, out, prev = finish(
            step, sig, state, in_weight, cond, part, got, final_gain[None], final_weight, fresh_noise
        )
        results.append(estimate)
        state = passed_along(out, -1)
        if step + 1 < STEPS:
            both = jnp.concatenate([state.astype(BF), prev], axis=0)
            mine = spread(jnp.broadcast_to(both[None], (CHIPS,) + both.shape))
    return (jnp.stack(results)[:, None], state[None])


def solution(mesh):
    split = Mesh(mesh.devices.reshape(8, 4, 2, 2), ("frame", "y", "far", "core"))
    space = ("y", "far", "core")
    in_specs = (
        P("frame", space, None),
        P(None, space, None),
        P(),
        P(),
        P(),
        P(),
        P(),
        P(),
        P(None, None, space),
        P(),
        P(),
        P(),
        P(),
    )
    out_specs = (P(None, "frame", space, None), P("frame", space, None))
    return jax.shard_map(shards, mesh=split, in_specs=in_specs, out_specs=out_specs, check_vma=False)
```

```python
import functools
import math

import jax
import jax.numpy as jnp
import numpy as np
from jax import lax
from jax.experimental import pallas as pl
from jax.experimental.pallas import tpu as pltpu
from jax.sharding import Mesh
from jax.sharding import PartitionSpec as P

HEAD = 64
STEPS = 2
FEAT = 128
WIDE = 256
CHIPS = 8
TOK = 64
COLS = 192
PACK = 48
PAY = 3 * COLS + PACK + 2 * TOK
HEADS = CHIPS * 3
GROUPS = HEADS // 4
KEYS = 2048
ONE = 136
EPS = 1e-06
SAFE = 60.0

BF = jnp.bfloat16
F32 = jnp.float32
VMEM = pl.BlockSpec(memory_space=pltpu.VMEM)
SMEM = pl.BlockSpec(memory_space=pltpu.SMEM)
ANY = pl.BlockSpec(memory_space=pl.ANY)


def dot(a, b):
    return jnp.dot(a, b, preferred_element_type=F32)


def dot_t(a, b):
    return lax.dot_general(a, b, (((1,), (1,)), ((), ())), preferred_element_type=F32)


def halves(x):
    high = x.astype(BF)
    return high, (x - high.astype(F32)).astype(BF)


def in_vmem(x):
    return pltpu.with_memory_space_constraint(x, pltpu.VMEM)


def in_hbm(x):
    return pltpu.with_memory_space_constraint(x, pltpu.HBM)


def lanes(shape):
    return lax.broadcasted_iota(jnp.int32, shape, len(shape) - 1)


def rows(shape):
    return lax.broadcasted_iota(jnp.int32, shape, len(shape) - 2)


def fold_kernel(
    level_hbm,
    plan_hbm,
    ids_hbm,
    freq_hbm,
    qkv_hbm,
    in_hbm,
    cond_gain_hbm,
    gain_hbm,
    qk_gain_hbm,
    state_hbm,
    pay_ref,
    gram_hi_ref,
    gram_lo_ref,
    cond_ref,
    qk_ref,
    safe_ref,
    sig_ref,
    level_ref,
    plan_ref,
    ids_ref,
    freq_ref,
    w_ref,
    in_ref,
    cond_gain_ref,
    gain_ref,
    qk_gain_ref,
    state_ref,
    sems,
):
    pairs = (
        (level_hbm, level_ref),
        (plan_hbm, plan_ref),
        (ids_hbm, ids_ref),
        (freq_hbm, freq_ref),
        (in_hbm, in_ref),
        (qkv_hbm, w_ref),
        (cond_gain_hbm, cond_gain_ref),
        (gain_hbm, gain_ref),
        (qk_gain_hbm, qk_gain_ref),
        (state_hbm, state_ref),
    )
    copies = [pltpu.make_async_copy(src, dst, sems.at[i]) for i, (src, dst) in enumerate(pairs)]
    for copy in copies:
        copy.start()
    for i in (0, 1, 2, 3):
        copies[i].wait()

    slot = lax.axis_index("frame")
    before = jnp.maximum(slot - 1, 0)
    stamp_now = plan_ref[level_ref[slot]].astype(F32)
    stamp_prev = plan_ref[level_ref[before]].astype(F32)
    sigma = stamp_now / 1000.0
    sig_ref[0] = sigma
    sig_ref[1] = jnp.where(slot > 0, stamp_prev / 1000.0, 0.0) - sigma

    freq = freq_ref[...]
    row = rows((8, freq.shape[1]))
    angle = jnp.where(row == 0, stamp_now, stamp_prev)
    for step in range(STEPS):
        angle = jnp.where(row == 2 + 2 * step, ids_ref[slot + step].astype(F32), angle)
        angle = jnp.where(row == 3 + 2 * step, ids_ref[before + step].astype(F32), angle)
    angle = angle * freq
    wave = jnp.concatenate([jnp.cos(angle), jnp.sin(angle)], axis=1)

    for i in (4, 6, 7, 8, 9):
        copies[i].wait()
    product = qk_gain_ref[0:1, :] * qk_gain_ref[1:2, :]
    safe_ref[0] = (HEAD**0.5 * jnp.max(jnp.abs(product)) <= SAFE).astype(jnp.int32)
    product = product * (math.log2(math.e) / math.sqrt(HEAD))
    qk_ref[...] = jnp.concatenate([product] * 4, axis=1)

    stamps = cond_gain_ref[0:1, :] * wave
    idents = cond_gain_ref[1:2, :] * wave
    cond = jnp.concatenate([stamps[0:2] + idents[2:4], stamps[0:2] + idents[4:6]], axis=0)
    cond = jnp.concatenate([cond, jnp.zeros_like(cond)], axis=0)
    cond_ref[...] = cond

    embed = in_ref[...]
    none = jnp.zeros((112, embed.shape[1]), BF)
    c_hi, c_lo = halves(cond)
    left = jnp.concatenate([embed, jnp.concatenate([c_hi, c_lo], axis=0), none], axis=0)
    gram = dot_t(left, left)
    lane, row = lanes(gram.shape), rows(gram.shape)
    gram = jnp.where(lane < FEAT + 8, gram + jnp.where(lane >= FEAT, pltpu.roll(gram, WIDE - 8, 1), 0.0), 0.0)
    gram = jnp.where(row < FEAT + 8, gram + jnp.where(row >= FEAT, pltpu.roll(gram, WIDE - 8, 0), 0.0), 0.0)
    g_hi, g_lo = halves(gram)
    gram_hi_ref[...] = g_hi
    gram_lo_ref[...] = g_lo

    gain = gain_ref[...]
    emb = (embed.astype(F32) * gain).astype(BF)
    cg_hi, cg_lo = halves(cond * gain)
    right = jnp.concatenate([emb, jnp.concatenate([cg_hi, cg_lo], axis=0), none], axis=0)
    copies[5].wait()
    full = dot_t(w_ref[...].reshape(3 * COLS, embed.shape[1]), right)
    mat = full[:, 0:FEAT].astype(BF)
    bias = full[:, FEAT:WIDE]
    bias = bias + pltpu.roll(bias, FEAT - 8, 1)
    lane = lanes(bias.shape)
    bias = jnp.where(lane < 4, bias, 0.0)
    high = bias.astype(BF).astype(F32)
    bias = high + pltpu.roll(bias - high, 4, 1)
    packed = bias[0:PACK]
    for i in range(1, 12):
        packed = packed + pltpu.roll(bias[PACK * i : PACK * (i + 1)], 8 * i, 1)
    packed = packed.astype(BF)
    x = state_ref[0].astype(BF)
    for chip in range(CHIPS):
        pay_ref[chip, 0 : 3 * COLS] = mat
        pay_ref[chip, 3 * COLS : 3 * COLS + PACK] = packed
        pay_ref[chip, 3 * COLS + PACK : PAY - TOK] = x
        pay_ref[chip, PAY - TOK : PAY] = x


def fold(level_index, plan, frame_ids, freq, qkv, in_weight, cond_gain, gain, qk_gain, latents):
    width = in_weight.shape[1]
    args = (level_index, plan, frame_ids, freq, qkv, in_weight, cond_gain, gain, qk_gain, latents)
    return pl.pallas_call(
        fold_kernel,
        out_shape=(
            pltpu.VMEM((CHIPS, PAY, FEAT), BF),
            pltpu.VMEM((WIDE, WIDE), BF),
            pltpu.VMEM((WIDE, WIDE), BF),
            pltpu.VMEM((8, width), F32),
            pltpu.VMEM((1, WIDE), F32),
            jax.ShapeDtypeStruct((1,), jnp.int32),
            jax.ShapeDtypeStruct((2,), F32),
        ),
        in_specs=[ANY] * len(args),
        out_specs=(VMEM,) * 5 + (SMEM,) * 2,
        scratch_shapes=[pltpu.SMEM(v.shape, v.dtype) for v in args[:3]]
        + [pltpu.VMEM(v.shape, v.dtype) for v in args[3:]]
        + [pltpu.SemaphoreType.DMA((len(args),))],
        compiler_params=pltpu.CompilerParams(vmem_limit_bytes=40 * 2**20),
        name="fold",
    )(*[in_hbm(v) for v in args])


def enter_kernel(prev_ref, pay_ref, out_ref):
    prev = prev_ref[...].astype(BF)
    for chip in range(CHIPS):
        out_ref[chip, PAY - TOK : PAY] = prev


def enter(prev, pay):
    return pl.pallas_call(
        enter_kernel,
        out_shape=pltpu.VMEM(pay.shape, pay.dtype),
        in_specs=[VMEM, VMEM],
        out_specs=VMEM,
        input_output_aliases={1: 0},
        name="enter",
    )(in_vmem(prev), in_vmem(pay))


def attend_kernel(
    step,
    safe_ref,
    pay_ref,
    mine_ref,
    other_ref,
    gram_hi_ref,
    gram_lo_ref,
    qk_ref,
    out_w_ref,
    part_ref,
    part_other_ref,
    xk_ref,
    xkt_ref,
    val_ref,
    aq_ref,
    ak_ref,
    av_ref,
    rk_ref,
    p_ref,
    s_ref,
    qc_ref,
    z_ref,
    w_ref,
    sem,
):
    chip, core = lax.axis_index(("y", "far")), lax.axis_index("core")
    first = lax.axis_index("frame") == 0
    copies = []
    for m in range(CHIPS):
        begin = pl.multiple_of((2 * m + core) * COLS, COLS)
        copies.append(pltpu.make_async_copy(out_w_ref.at[pl.ds(begin, COLS)], w_ref.at[pl.ds(m * COLS, COLS)], sem))
    for copy in copies:
        copy.start()

    half = CHIPS * TOK
    for group in range(2):
        for side, ref in enumerate((mine_ref, other_ref)):
            base = (2 * group + side) * half
            block = ref[:, TOK * group : TOK * (group + 1), :].reshape(half, FEAT)
            if group == 1:
                block = jnp.where(first, ref[:, 0:TOK, :].reshape(half, FEAT), block)
            xk_ref[base : base + half, 0:FEAT] = block
        lane = lanes((KEYS // 2, FEAT))
        mark = jnp.logical_or(lane == 2 * step + group, lane == 4 + 2 * step + group)
        xk_ref[group * KEYS // 2 : (group + 1) * KEYS // 2, FEAT:WIDE] = mark.astype(F32).astype(BF)
    xkt_ref[0:FEAT, :] = jnp.transpose(xk_ref[:, 0:FEAT])
    row = rows((FEAT, KEYS))
    group = (lanes((FEAT, KEYS)) >= KEYS // 2).astype(jnp.int32)
    mark = jnp.logical_or(row == 2 * step + group, row == 4 + 2 * step + group)
    xkt_ref[FEAT:WIDE, :] = mark.astype(F32).astype(BF)

    xkt = xkt_ref[...]
    square = dot(gram_hi_ref[...], xkt) + dot(gram_lo_ref[...], xkt)
    m_row = jnp.sum(square * xkt.astype(F32), axis=0, keepdims=True) * (1.0 / 3072.0) + EPS
    r_col = jnp.transpose(jnp.broadcast_to(lax.rsqrt(m_row), (8, KEYS)))[:, 0:1]
    val = xk_ref[...].astype(F32) * r_col
    val_ref[...] = jnp.where(lanes((KEYS, WIDE)) == ONE, 1.0, val).astype(BF)

    lane = lanes((PACK, FEAT))
    for m in range(CHIPS):
        packed = pay_ref[m, 3 * COLS : 3 * COLS + PACK, :].astype(F32)
        for j, ref in enumerate((aq_ref, ak_ref, av_ref)):
            ref[m * COLS : (m + 1) * COLS, 0:FEAT] = pay_ref[m, j * COLS : (j + 1) * COLS, :]
            for i in range(4):
                shift = 8 * (4 * j + i)
                part = pltpu.roll(packed, FEAT - shift, 1) if shift else packed
                part = jnp.where(lane < 8, part, 0.0)
                ref[m * COLS + i * PACK : m * COLS + (i + 1) * PACK, FEAT:WIDE] = part.astype(BF)

    xq = jnp.concatenate([mine_ref[chip, 0:TOK, :], other_ref[chip, 0:TOK, :]], axis=0)
    row = rows((FEAT, 2 * TOK))
    mark = jnp.logical_or(row == 2 * step, row == 4 + 2 * step)
    xqt = jnp.concatenate([jnp.transpose(xq), mark.astype(F32).astype(BF)], axis=0)
    square = dot(gram_hi_ref[...], xqt) + dot(gram_lo_ref[...], xqt)
    m_q = jnp.sum(square * xqt.astype(F32), axis=0, keepdims=True) * (1.0 / 3072.0) + EPS
    head_of = lanes((2 * TOK, WIDE)) // HEAD

    def norms(g, carry):
        begin = pl.multiple_of(g * WIDE, WIDE)
        u = dot(ak_ref[pl.ds(begin, WIDE), :], xkt_ref[...])
        u = jnp.sum((u * u).reshape(4, HEAD, KEYS), axis=1)
        rk = lax.rsqrt(u * (1.0 / HEAD) + EPS * m_row)
        rk_ref[g] = jnp.concatenate([rk, rk], axis=0)
        return carry

    lax.fori_loop(0, GROUPS, norms, 0, unroll=True)

    q = dot(aq_ref[...], xqt).reshape(HEADS, HEAD, 2 * TOK)
    q = q * lax.rsqrt(jnp.sum(q * q, axis=1, keepdims=True) * (1.0 / HEAD) + EPS * m_q[None])
    q = q.reshape(HEADS * HEAD, 2 * TOK)
    for g in range(GROUPS):
        span = slice(g * WIDE, (g + 1) * WIDE)
        some = jnp.transpose(q[span]) * qk_ref[...]
        some = jnp.concatenate([jnp.where(head_of == h, some, 0.0) for h in range(4)], axis=0)
        qc_ref[g] = dot(some.astype(BF), ak_ref[span, :]).astype(BF)

    def one_group(g, fast):
        carried = qc_ref[g]
        rk = rk_ref[g]
        for h in range(4):
            span = slice(2 * TOK * h, 2 * TOK * (h + 1))
            s = dot(carried[span], xkt_ref[...]) * rk[h : h + 1]
            if not fast:
                s_ref[...] = s
                s = s_ref[...]
                s = s - jnp.max(s, axis=1, keepdims=True)
            p_ref[span, :] = jnp.exp2(s).astype(BF)
        for h in range(4):
            span = slice(2 * TOK * h, 2 * TOK * (h + 1))
            z = dot(p_ref[span, :], val_ref[...])
            z_ref[g, span] = (z * (1.0 / z[:, ONE : ONE + 1])).astype(BF)

    @pl.when(safe_ref[0] == 1)
    def _():
        def body(g, carry):
            one_group(g, True)
            return carry

        lax.fori_loop(0, GROUPS, body, 0, unroll=3)

    @pl.when(safe_ref[0] != 1)
    def _():
        def body(g, carry):
            one_group(g, False)
            return carry

        lax.fori_loop(0, GROUPS, body, 0)

    outs = []
    for g in range(GROUPS):
        o = dot_t(z_ref[g], av_ref[g * WIDE : (g + 1) * WIDE, :])
        picked = jnp.where(head_of == 0, o[0:128], 0.0)
        for h in range(1, 4):
            picked = jnp.where(head_of == h, o[128 * h : 128 * (h + 1)], picked)
        outs.append(picked.astype(BF))
    for copy in copies:
        copy.wait()
    y = dot(jnp.concatenate(outs, axis=1), w_ref[...])
    part_ref[...] = y[0:TOK]
    part_other_ref[...] = y[TOK:].astype(BF)


def attend(step, safe, pay, mine, other, gram_hi, gram_lo, qk, out_weight):
    width = out_weight.shape[1]
    half = HEADS * HEAD
    return pl.pallas_call(
        functools.partial(attend_kernel, step),
        out_shape=(pltpu.VMEM((TOK, width), F32), pltpu.VMEM((TOK, width), BF)),
        in_specs=[SMEM] + [VMEM] * 6 + [ANY],
        out_specs=(VMEM, VMEM),
        scratch_shapes=[
            pltpu.VMEM((KEYS, WIDE), BF),
            pltpu.VMEM((WIDE, KEYS), BF),
            pltpu.VMEM((KEYS, WIDE), BF),
            pltpu.VMEM((half, WIDE), BF),
            pltpu.VMEM((half, WIDE), BF),
            pltpu.VMEM((half, WIDE), BF),
            pltpu.VMEM((GROUPS, 8, KEYS), F32),
            pltpu.VMEM((512, KEYS), BF),
            pltpu.VMEM((128, KEYS), F32),
            pltpu.VMEM((GROUPS, 512, WIDE), BF),
            pltpu.VMEM((GROUPS, 512, WIDE), BF),
            pltpu.VMEM((half, width), BF),
            pltpu.SemaphoreType.DMA,
        ],
        compiler_params=pltpu.CompilerParams(vmem_limit_bytes=56 * 2**20),
        name="attend",
    )(safe, *[in_vmem(v) for v in (pay, mine, other, gram_hi, gram_lo, qk)], out_weight)


def finish_kernel(
    step, sig_ref, state_ref, in_ref, cond_ref, part_ref, got_ref, gain_ref, final_ref, fresh_ref, est_ref, sent_ref, prev_ref
):
    state = state_ref[...]
    y = dot(state.astype(BF), in_ref[...]) + cond_ref[2 * step : 2 * step + 1, :]
    y = y + part_ref[...] + got_ref[...].astype(F32)
    scale = lax.rsqrt(jnp.mean(y * y, axis=1, keepdims=True) + EPS)
    velocity = dot((y * scale * gain_ref[...]).astype(BF), final_ref[...])
    est_ref[...] = state - sig_ref[0] * velocity
    renewed = state + sig_ref[1] * velocity
    sent_ref[...] = jnp.where(lax.axis_index("frame") == 0, fresh_ref[step], renewed)
    prev_ref[...] = renewed.astype(BF)


def finish(step, sig, state, in_weight, cond, part, got, gain, final_weight, fresh):
    out = jax.ShapeDtypeStruct(state.shape, F32)
    return pl.pallas_call(
        functools.partial(finish_kernel, step),
        out_shape=(out, out, jax.ShapeDtypeStruct(state.shape, BF)),
        in_specs=[SMEM] + [VMEM] * 8,
        out_specs=(VMEM,) * 3,
        compiler_params=pltpu.CompilerParams(vmem_limit_bytes=32 * 2**20),
        name="finish",
    )(sig, state, in_weight, in_vmem(cond), in_vmem(part), in_vmem(got), gain, final_weight, fresh)


def passed_along(x, by):
    peers = lax.axis_size("frame")
    return lax.ppermute(x, "frame", [(i, (i + by) % peers) for i in range(peers)])


def swapped(x):
    return lax.ppermute(x, "core", [(0, 1), (1, 0)])


def spread(x):
    return lax.all_to_all(x, ("y", "far"), 0, 0, tiled=True)


def shards(
    latents,
    fresh_noise,
    level_index,
    plan,
    frame_ids,
    in_weight,
    cond_gain,
    norm_gain,
    qkv_weight,
    qk_gain,
    out_weight,
    final_gain,
    final_weight,
):
    half = in_weight.shape[1] // 2
    freq = jnp.asarray(np.exp(-math.log(10000.0) * np.arange(half, dtype=np.float32) / half), F32)
    state = latents[0]
    prev = passed_along(state, 1)
    sent, gram_hi, gram_lo, cond, qk, safe, sig = fold(
        level_index,
        plan,
        frame_ids,
        freq[None],
        jnp.swapaxes(qkv_weight, 1, 2),
        in_weight,
        cond_gain,
        norm_gain[None],
        qk_gain,
        latents,
    )
    pay = spread(enter(prev, sent))
    mine = pay[:, PAY - 2 * TOK :, :]
    results = []
    for step in range(STEPS):
        other = swapped(mine)
        part, part_other = attend(step, safe, pay, mine, other, gram_hi, gram_lo, qk, out_weight)
        got = swapped(part_other)
        estimate, out, prev = finish(
            step, sig, state, in_weight, cond, part, got, final_gain[None], final_weight, fresh_noise
        )
        results.append(estimate)
        state = passed_along(out, -1)
        if step + 1 < STEPS:
            both = jnp.concatenate([state.astype(BF), prev], axis=0)
            mine = spread(jnp.broadcast_to(both[None], (CHIPS,) + both.shape))
    return (jnp.stack(results)[:, None], state[None])


def solution(mesh):
    split = Mesh(mesh.devices.reshape(8, 4, 2, 2), ("frame", "y", "far", "core"))
    space = ("y", "far", "core")
    in_specs = (
        P("frame", space, None),
        P(None, space, None),
        P(),
        P(),
        P(),
        P(),
        P(),
        P(),
        P(None, None, space),
        P(),
        P(),
        P(),
        P(),
    )
    out_specs = (P(None, "frame", space, None), P("frame", space, None))
    return jax.shard_map(shards, mesh=split, in_specs=in_specs, out_specs=out_specs, check_vma=False)
```

```python
import functools
import math

import jax
import jax.numpy as jnp
import numpy as np
from jax import lax
from jax.experimental import pallas as pl
from jax.experimental.pallas import tpu as pltpu
from jax.sharding import Mesh
from jax.sharding import PartitionSpec as P

HEAD = 64
STEPS = 2
FEAT = 128
WIDE = 256
CHIPS = 8
TOK = 64
COLS = 192
PACK = 48
PAY = 3 * COLS + PACK + 2 * TOK
HEADS = CHIPS * 3
GROUPS = HEADS // 4
SIDE = 1024
ONE = 136
EPS = 1e-06
SAFE = 60.0

BF = jnp.bfloat16
F32 = jnp.float32
VMEM = pl.BlockSpec(memory_space=pltpu.VMEM)
SMEM = pl.BlockSpec(memory_space=pltpu.SMEM)
ANY = pl.BlockSpec(memory_space=pl.ANY)


def dot(a, b):
    return jnp.dot(a, b, preferred_element_type=F32)


def dot_t(a, b):
    return lax.dot_general(a, b, (((1,), (1,)), ((), ())), preferred_element_type=F32)


def halves(x):
    high = x.astype(BF)
    return high, (x - high.astype(F32)).astype(BF)


def in_vmem(x):
    return pltpu.with_memory_space_constraint(x, pltpu.VMEM)


def cost(products, bytes_moved=0):
    return pl.CostEstimate(flops=2 * products, transcendentals=0, bytes_accessed=bytes_moved)


def in_hbm(x):
    return pltpu.with_memory_space_constraint(x, pltpu.HBM)


def lanes(shape):
    return lax.broadcasted_iota(jnp.int32, shape, len(shape) - 1)


def rows(shape):
    return lax.broadcasted_iota(jnp.int32, shape, len(shape) - 2)


def fold_kernel(
    level_hbm,
    plan_hbm,
    ids_hbm,
    freq_hbm,
    qkv_hbm,
    in_hbm,
    cond_gain_hbm,
    gain_hbm,
    qk_gain_hbm,
    state_hbm,
    pay_ref,
    gram_hi_ref,
    gram_lo_ref,
    cond_ref,
    qk_ref,
    safe_ref,
    sig_ref,
    level_ref,
    plan_ref,
    ids_ref,
    freq_ref,
    w_ref,
    in_ref,
    cond_gain_ref,
    gain_ref,
    qk_gain_ref,
    state_ref,
    sems,
):
    pairs = (
        (level_hbm, level_ref),
        (plan_hbm, plan_ref),
        (ids_hbm, ids_ref),
        (freq_hbm, freq_ref),
        (in_hbm, in_ref),
        (qkv_hbm, w_ref),
        (cond_gain_hbm, cond_gain_ref),
        (gain_hbm, gain_ref),
        (qk_gain_hbm, qk_gain_ref),
        (state_hbm, state_ref),
    )
    copies = [pltpu.make_async_copy(src, dst, sems.at[i]) for i, (src, dst) in enumerate(pairs)]
    for copy in copies:
        copy.start()
    for i in (0, 1, 2, 3):
        copies[i].wait()

    slot = lax.axis_index("frame")
    before = jnp.maximum(slot - 1, 0)
    stamp_now = plan_ref[level_ref[slot]].astype(F32)
    stamp_prev = plan_ref[level_ref[before]].astype(F32)
    sigma = stamp_now / 1000.0
    sig_ref[0] = sigma
    sig_ref[1] = jnp.where(slot > 0, stamp_prev / 1000.0, 0.0) - sigma

    freq = freq_ref[...]
    row = rows((8, freq.shape[1]))
    angle = jnp.where(row == 0, stamp_now, stamp_prev)
    for step in range(STEPS):
        angle = jnp.where(row == 2 + 2 * step, ids_ref[slot + step].astype(F32), angle)
        angle = jnp.where(row == 3 + 2 * step, ids_ref[before + step].astype(F32), angle)
    angle = angle * freq
    wave = jnp.concatenate([jnp.cos(angle), jnp.sin(angle)], axis=1)

    for i in (4, 6, 7, 8, 9):
        copies[i].wait()
    product = qk_gain_ref[0:1, :] * qk_gain_ref[1:2, :]
    safe_ref[0] = (HEAD**0.5 * jnp.max(jnp.abs(product)) <= SAFE).astype(jnp.int32)
    product = product * (math.log2(math.e) / math.sqrt(HEAD))
    qk_ref[...] = jnp.concatenate([product] * 4, axis=1)

    stamps = cond_gain_ref[0:1, :] * wave
    idents = cond_gain_ref[1:2, :] * wave
    cond = jnp.concatenate([stamps[0:2] + idents[2:4], stamps[0:2] + idents[4:6]], axis=0)
    cond = jnp.concatenate([cond, jnp.zeros_like(cond)], axis=0)
    cond_ref[...] = cond

    embed = in_ref[...]
    none = jnp.zeros((112, embed.shape[1]), BF)
    c_hi, c_lo = halves(cond)
    left = jnp.concatenate([embed, jnp.concatenate([c_hi, c_lo], axis=0), none], axis=0)
    gram = dot_t(left, left)
    lane, row = lanes(gram.shape), rows(gram.shape)
    gram = jnp.where(lane < FEAT + 8, gram + jnp.where(lane >= FEAT, pltpu.roll(gram, WIDE - 8, 1), 0.0), 0.0)
    gram = jnp.where(row < FEAT + 8, gram + jnp.where(row >= FEAT, pltpu.roll(gram, WIDE - 8, 0), 0.0), 0.0)
    g_hi, g_lo = halves(gram)
    gram_hi_ref[...] = g_hi
    gram_lo_ref[...] = g_lo

    gain = gain_ref[...]
    emb = (embed.astype(F32) * gain).astype(BF)
    cg_hi, cg_lo = halves(cond * gain)
    right = jnp.concatenate([emb, jnp.concatenate([cg_hi, cg_lo], axis=0), none], axis=0)
    copies[5].wait()
    full = dot_t(w_ref[...].reshape(3 * COLS, embed.shape[1]), right)
    mat = full[:, 0:FEAT].astype(BF)
    bias = full[:, FEAT:WIDE]
    bias = bias + pltpu.roll(bias, FEAT - 8, 1)
    lane = lanes(bias.shape)
    bias = jnp.where(lane < 4, bias, 0.0)
    high = bias.astype(BF).astype(F32)
    bias = high + pltpu.roll(bias - high, 4, 1)
    packed = bias[0:PACK]
    for i in range(1, 12):
        packed = packed + pltpu.roll(bias[PACK * i : PACK * (i + 1)], 8 * i, 1)
    packed = packed.astype(BF)
    x = state_ref[0].astype(BF)
    for chip in range(CHIPS):
        pay_ref[chip, 0 : 3 * COLS] = mat
        pay_ref[chip, 3 * COLS : 3 * COLS + PACK] = packed
        pay_ref[chip, 3 * COLS + PACK : PAY - TOK] = x
        pay_ref[chip, PAY - TOK : PAY] = x


def fold(level_index, plan, frame_ids, freq, qkv, in_weight, cond_gain, gain, qk_gain, latents):
    width = in_weight.shape[1]
    args = (level_index, plan, frame_ids, freq, qkv, in_weight, cond_gain, gain, qk_gain, latents)
    return pl.pallas_call(
        fold_kernel,
        out_shape=(
            pltpu.VMEM((CHIPS, PAY, FEAT), BF),
            pltpu.VMEM((WIDE, WIDE), BF),
            pltpu.VMEM((WIDE, WIDE), BF),
            pltpu.VMEM((8, width), F32),
            pltpu.VMEM((1, WIDE), F32),
            jax.ShapeDtypeStruct((1,), jnp.int32),
            jax.ShapeDtypeStruct((2,), F32),
        ),
        in_specs=[ANY] * len(args),
        out_specs=(VMEM,) * 5 + (SMEM,) * 2,
        scratch_shapes=[pltpu.SMEM(v.shape, v.dtype) for v in args[:3]]
        + [pltpu.VMEM(v.shape, v.dtype) for v in args[3:]]
        + [pltpu.SemaphoreType.DMA((len(args),))],
        compiler_params=pltpu.CompilerParams(vmem_limit_bytes=40 * 2**20),
        name="fold",
    )(*[in_hbm(v) for v in args])


def enter_kernel(prev_ref, pay_ref, out_ref):
    prev = prev_ref[...].astype(BF)
    for chip in range(CHIPS):
        out_ref[chip, PAY - TOK : PAY] = prev


def enter(prev, pay):
    return pl.pallas_call(
        enter_kernel,
        out_shape=pltpu.VMEM(pay.shape, pay.dtype),
        in_specs=[VMEM, VMEM],
        out_specs=VMEM,
        input_output_aliases={1: 0},
        name="enter",
    )(in_vmem(prev), in_vmem(pay))


def unpack(pay_ref, ref, j):
    lane = lanes((PACK, FEAT))
    for m in range(CHIPS):
        packed = pay_ref[m, 3 * COLS : 3 * COLS + PACK, :].astype(F32)
        ref[m * COLS : (m + 1) * COLS, 0:FEAT] = pay_ref[m, j * COLS : (j + 1) * COLS, :]
        for i in range(4):
            shift = 8 * (4 * j + i)
            part = pltpu.roll(packed, FEAT - shift, 1) if shift else packed
            part = jnp.where(lane < 8, part, 0.0)
            ref[m * COLS + i * PACK : m * COLS + (i + 1) * PACK, FEAT:WIDE] = part.astype(BF)


def prepare(step, first, block_ref, gram_hi_ref, gram_lo_ref, ak_ref, xkt_ref, val_ref, rk_ref):
    half = CHIPS * TOK
    own = block_ref[:, 0:TOK, :].reshape(half, FEAT)
    prev = block_ref[:, TOK : 2 * TOK, :].reshape(half, FEAT)
    prev = jnp.where(first, own, prev)
    x = jnp.concatenate([own, prev], axis=0)
    group = (rows((SIDE, FEAT)) >= half).astype(jnp.int32)
    lane = lanes((SIDE, FEAT))
    mark = jnp.logical_or(lane == 2 * step + group, lane == 4 + 2 * step + group)
    xk = jnp.concatenate([x, mark.astype(F32).astype(BF)], axis=1)
    group = (lanes((FEAT, SIDE)) >= half).astype(jnp.int32)
    row = rows((FEAT, SIDE))
    mark = jnp.logical_or(row == 2 * step + group, row == 4 + 2 * step + group)
    xkt_ref[0:FEAT, :] = jnp.transpose(x)
    xkt_ref[FEAT:WIDE, :] = mark.astype(F32).astype(BF)
    xkt = xkt_ref[...]
    square = dot(gram_hi_ref[...], xkt) + dot(gram_lo_ref[...], xkt)
    m_row = jnp.sum(square * xkt.astype(F32), axis=0, keepdims=True) * (1.0 / 3072.0) + EPS
    r_col = jnp.transpose(jnp.broadcast_to(lax.rsqrt(m_row), (8, SIDE)))[:, 0:1]
    val = jnp.where(lanes((SIDE, WIDE)) == ONE, 1.0, xk.astype(F32) * r_col)
    val_ref[...] = val.astype(BF)
    for g in range(GROUPS):
        u = dot(ak_ref[g * WIDE : (g + 1) * WIDE, :], xkt_ref[...])
        u = jnp.sum((u * u).reshape(4, HEAD, SIDE), axis=1)
        rk = lax.rsqrt(u * (1.0 / HEAD) + EPS * m_row)
        rk_ref[g] = jnp.concatenate([rk, rk], axis=0)


def prepare_kernel(step, pay_ref, block_ref, gram_hi_ref, gram_lo_ref, ak_ref, xkt_ref, val_ref, rk_ref):
    unpack(pay_ref, ak_ref, 1)
    first = lax.axis_index("frame") == 0
    prepare(step, first, block_ref, gram_hi_ref, gram_lo_ref, ak_ref, xkt_ref, val_ref, rk_ref)


def side_shapes():
    return [
        pltpu.VMEM((WIDE, SIDE), BF),
        pltpu.VMEM((SIDE, WIDE), BF),
        pltpu.VMEM((GROUPS, 8, SIDE), F32),
    ]


def prepared(step, pay, block, gram_hi, gram_lo):
    return pl.pallas_call(
        functools.partial(prepare_kernel, step),
        out_shape=[pltpu.VMEM((HEADS * HEAD, WIDE), BF)] + side_shapes(),
        in_specs=[VMEM] * 4,
        out_specs=[VMEM] * 4,
        compiler_params=pltpu.CompilerParams(vmem_limit_bytes=24 * 2**20),
        cost_estimate=cost(HEADS * HEAD * WIDE * SIDE, 2 * CHIPS * PAY * FEAT),
        name="prepare",
    )(*[in_vmem(v) for v in (pay, block, gram_hi, gram_lo)])


def attend_kernel(
    step,
    safe_ref,
    pay_ref,
    mine_ref,
    other_ref,
    gram_hi_ref,
    gram_lo_ref,
    qk_ref,
    ak_ref,
    xkt_a_ref,
    val_a_ref,
    rk_a_ref,
    out_w_ref,
    part_ref,
    part_other_ref,
    xkt_b_ref,
    val_b_ref,
    rk_b_ref,
    aq_ref,
    av_ref,
    p_ref,
    s_ref,
    qc_ref,
    z_ref,
    w_ref,
    sem,
):
    chip, core = lax.axis_index(("y", "far")), lax.axis_index("core")
    first = lax.axis_index("frame") == 0
    copies = []
    for m in range(CHIPS):
        begin = pl.multiple_of((2 * m + core) * COLS, COLS)
        copies.append(pltpu.make_async_copy(out_w_ref.at[pl.ds(begin, COLS)], w_ref.at[pl.ds(m * COLS, COLS)], sem))
    for copy in copies:
        copy.start()
    sides = ((xkt_a_ref, val_a_ref, rk_a_ref), (xkt_b_ref, val_b_ref, rk_b_ref))
    spans = (slice(0, SIDE), slice(SIDE, 2 * SIDE))
    prepare(step, first, other_ref, gram_hi_ref, gram_lo_ref, ak_ref, *sides[1])

    unpack(pay_ref, aq_ref, 0)
    unpack(pay_ref, av_ref, 2)
    xq = jnp.concatenate([mine_ref[chip, 0:TOK, :], other_ref[chip, 0:TOK, :]], axis=0)
    row = rows((FEAT, 2 * TOK))
    mark = jnp.logical_or(row == 2 * step, row == 4 + 2 * step)
    xqt = jnp.concatenate([jnp.transpose(xq), mark.astype(F32).astype(BF)], axis=0)
    square = dot(gram_hi_ref[...], xqt) + dot(gram_lo_ref[...], xqt)
    m_q = jnp.sum(square * xqt.astype(F32), axis=0, keepdims=True) * (1.0 / 3072.0) + EPS
    head_of = lanes((2 * TOK, WIDE)) // HEAD

    q = dot(aq_ref[...], xqt).reshape(HEADS, HEAD, 2 * TOK)
    q = q * lax.rsqrt(jnp.sum(q * q, axis=1, keepdims=True) * (1.0 / HEAD) + EPS * m_q[None])
    q = q.reshape(HEADS * HEAD, 2 * TOK)
    for g in range(GROUPS):
        span = slice(g * WIDE, (g + 1) * WIDE)
        some = jnp.transpose(q[span]) * qk_ref[...]
        some = jnp.concatenate([jnp.where(head_of == h, some, 0.0) for h in range(4)], axis=0)
        qc_ref[g] = dot(some.astype(BF), ak_ref[span, :]).astype(BF)

    def weigh(g):
        for h in range(4):
            span = slice(2 * TOK * h, 2 * TOK * (h + 1))
            for (xkt_ref, _, rk_ref), keys in zip(sides, spans):
                s = dot(qc_ref[g, span], xkt_ref[...]) * rk_ref[g, h : h + 1, :]
                p_ref[span, keys] = jnp.exp2(s).astype(BF)

    def weigh_wide(g):
        for h in range(4):
            span = slice(2 * TOK * h, 2 * TOK * (h + 1))
            for (xkt_ref, _, rk_ref), keys in zip(sides, spans):
                s_ref[:, keys] = dot(qc_ref[g, span], xkt_ref[...]) * rk_ref[g, h : h + 1, :]
            s = s_ref[...]
            p_ref[span, :] = jnp.exp2(s - jnp.max(s, axis=1, keepdims=True)).astype(BF)

    def collect(g):
        for h in range(4):
            span = slice(2 * TOK * h, 2 * TOK * (h + 1))
            z = dot(p_ref[span, spans[0]], val_a_ref[...]) + dot(p_ref[span, spans[1]], val_b_ref[...])
            z_ref[g, span] = (z * (1.0 / z[:, ONE : ONE + 1])).astype(BF)

    @pl.when(safe_ref[0] == 1)
    def _():
        def body(i, carry):
            for k in range(3):
                weigh(3 * i + k)
                collect(3 * i + k)
            return carry

        lax.fori_loop(0, GROUPS // 3, body, 0)

    @pl.when(safe_ref[0] != 1)
    def _():
        def body(g, carry):
            weigh_wide(g)
            collect(g)
            return carry

        lax.fori_loop(0, GROUPS, body, 0)

    outs = []
    for g in range(GROUPS):
        o = dot_t(z_ref[g], av_ref[g * WIDE : (g + 1) * WIDE, :])
        picked = jnp.where(head_of == 0, o[0:128], 0.0)
        for h in range(1, 4):
            picked = jnp.where(head_of == h, o[128 * h : 128 * (h + 1)], picked)
        outs.append(picked.astype(BF))
    for copy in copies:
        copy.wait()
    y = dot(jnp.concatenate(outs, axis=1), w_ref[...])
    part_ref[...] = y[0:TOK]
    part_other_ref[...] = y[TOK:].astype(BF)


def attend(step, safe, pay, mine, other, gram_hi, gram_lo, qk, ready, out_weight):
    width = out_weight.shape[1]
    half = HEADS * HEAD
    held = [in_vmem(v) for v in (pay, mine, other, gram_hi, gram_lo, qk, *ready)]
    return pl.pallas_call(
        functools.partial(attend_kernel, step),
        out_shape=(pltpu.VMEM((TOK, width), F32), pltpu.VMEM((TOK, width), BF)),
        in_specs=[SMEM] + [VMEM] * len(held) + [ANY],
        out_specs=(VMEM, VMEM),
        scratch_shapes=side_shapes()
        + [
            pltpu.VMEM((half, WIDE), BF),
            pltpu.VMEM((half, WIDE), BF),
            pltpu.VMEM((8 * TOK, 2 * SIDE), BF),
            pltpu.VMEM((2 * TOK, 2 * SIDE), F32),
            pltpu.VMEM((GROUPS, 8 * TOK, WIDE), BF),
            pltpu.VMEM((GROUPS, 8 * TOK, WIDE), BF),
            pltpu.VMEM((half, width), BF),
            pltpu.SemaphoreType.DMA,
        ],
        compiler_params=pltpu.CompilerParams(vmem_limit_bytes=48 * 2**20),
        cost_estimate=cost(HEADS * 2 * TOK * WIDE * 4 * SIDE),
        name="attend",
    )(safe, *held, out_weight)


def finish_kernel(
    step, sig_ref, state_ref, in_ref, cond_ref, part_ref, got_ref, gain_ref, final_ref, fresh_ref, est_ref, sent_ref, prev_ref
):
    state = state_ref[...]
    y = dot(state.astype(BF), in_ref[...]) + cond_ref[2 * step : 2 * step + 1, :]
    y = y + part_ref[...] + got_ref[...].astype(F32)
    scale = lax.rsqrt(jnp.mean(y * y, axis=1, keepdims=True) + EPS)
    velocity = dot((y * scale * gain_ref[...]).astype(BF), final_ref[...])
    est_ref[...] = state - sig_ref[0] * velocity
    renewed = state + sig_ref[1] * velocity
    sent_ref[...] = jnp.where(lax.axis_index("frame") == 0, fresh_ref[step], renewed)
    prev_ref[...] = renewed.astype(BF)


def finish(step, sig, state, in_weight, cond, part, got, gain, final_weight, fresh):
    out = jax.ShapeDtypeStruct(state.shape, F32)
    return pl.pallas_call(
        functools.partial(finish_kernel, step),
        out_shape=(out, out, jax.ShapeDtypeStruct(state.shape, BF)),
        in_specs=[SMEM] + [VMEM] * 8,
        out_specs=(VMEM,) * 3,
        compiler_params=pltpu.CompilerParams(vmem_limit_bytes=32 * 2**20),
        name="finish",
    )(sig, *[in_vmem(v) for v in (state, in_weight, cond, part, got, gain, final_weight, fresh)])


def passed_along(x, by):
    peers = lax.axis_size("frame")
    return lax.ppermute(x, "frame", [(i, (i + by) % peers) for i in range(peers)])


def swapped(x):
    return lax.ppermute(x, "core", [(0, 1), (1, 0)])


def spread(x):
    return lax.all_to_all(x, ("y", "far"), 0, 0, tiled=True)


def shards(
    latents,
    fresh_noise,
    level_index,
    plan,
    frame_ids,
    in_weight,
    cond_gain,
    norm_gain,
    qkv_weight,
    qk_gain,
    out_weight,
    final_gain,
    final_weight,
):
    half = in_weight.shape[1] // 2
    freq = jnp.asarray(np.exp(-math.log(10000.0) * np.arange(half, dtype=np.float32) / half), F32)
    state = latents[0]
    prev = passed_along(state, 1)
    sent, gram_hi, gram_lo, cond, qk, safe, sig = fold(
        level_index,
        plan,
        frame_ids,
        freq[None],
        jnp.swapaxes(qkv_weight, 1, 2),
        in_weight,
        cond_gain,
        norm_gain[None],
        qk_gain,
        latents,
    )
    pay = spread(enter(prev, sent))
    mine = pay[:, PAY - 2 * TOK :, :]
    results = []
    for step in range(STEPS):
        other = swapped(mine)
        ready = prepared(step, pay, mine, gram_hi, gram_lo)
        part, part_other = attend(step, safe, pay, mine, other, gram_hi, gram_lo, qk, ready, out_weight)
        got = swapped(part_other)
        estimate, out, prev = finish(
            step, sig, state, in_weight, cond, part, got, final_gain[None], final_weight, fresh_noise
        )
        results.append(estimate)
        state = passed_along(out, -1)
        if step + 1 < STEPS:
            both = jnp.concatenate([state.astype(BF), prev], axis=0)
            mine = spread(jnp.broadcast_to(both[None], (CHIPS,) + both.shape))
    return (jnp.stack(results)[:, None], state[None])


def solution(mesh):
    split = Mesh(mesh.devices.reshape(8, 4, 2, 2), ("frame", "y", "far", "core"))
    space = ("y", "far", "core")
    in_specs = (
        P("frame", space, None),
        P(None, space, None),
        P(),
        P(),
        P(),
        P(),
        P(),
        P(),
        P(None, None, space),
        P(),
        P(),
        P(),
        P(),
    )
    out_specs = (P(None, "frame", space, None), P("frame", space, None))
    return jax.shard_map(shards, mesh=split, in_specs=in_specs, out_specs=out_specs, check_vma=False)
```

```python
import functools
import math

import jax
import jax.numpy as jnp
import numpy as np
from jax import lax
from jax.experimental import pallas as pl
from jax.experimental.pallas import tpu as pltpu
from jax.sharding import Mesh
from jax.sharding import PartitionSpec as P

HEAD = 64
STEPS = 2
FEAT = 128
WIDE = 256
CHIPS = 8
TOK = 64
COLS = 192
PACK = 48
PAY = 3 * COLS + PACK + TOK
HEADS = CHIPS * 3
GROUPS = HEADS // 4
SIDE = CHIPS * TOK
ONE = 136
EPS = 1e-06
SAFE = 60.0

BF = jnp.bfloat16
F32 = jnp.float32
VMEM = pl.BlockSpec(memory_space=pltpu.VMEM)
SMEM = pl.BlockSpec(memory_space=pltpu.SMEM)
ANY = pl.BlockSpec(memory_space=pl.ANY)


def dot(a, b):
    return jnp.dot(a, b, preferred_element_type=F32)


def dot_t(a, b):
    return lax.dot_general(a, b, (((1,), (1,)), ((), ())), preferred_element_type=F32)


def halves(x):
    high = x.astype(BF)
    return high, (x - high.astype(F32)).astype(BF)


def in_vmem(x):
    return pltpu.with_memory_space_constraint(x, pltpu.VMEM)


def cost(products, bytes_moved=0):
    return pl.CostEstimate(flops=2 * products, transcendentals=0, bytes_accessed=bytes_moved)


def in_hbm(x):
    return pltpu.with_memory_space_constraint(x, pltpu.HBM)


def lanes(shape):
    return lax.broadcasted_iota(jnp.int32, shape, len(shape) - 1)


def rows(shape):
    return lax.broadcasted_iota(jnp.int32, shape, len(shape) - 2)


def slot_of(step):
    count = lax.axis_size("frame")
    return lax.rem(lax.axis_index("frame") + count - step, count)


def fold_kernel(
    level_hbm,
    plan_hbm,
    ids_hbm,
    freq_hbm,
    qkv_hbm,
    in_hbm,
    cond_gain_hbm,
    gain_hbm,
    qk_gain_hbm,
    state_hbm,
    pay_ref,
    gram_hi_ref,
    gram_lo_ref,
    cond_ref,
    qk_ref,
    safe_ref,
    sig_ref,
    level_ref,
    plan_ref,
    ids_ref,
    freq_ref,
    w_ref,
    in_ref,
    cond_gain_ref,
    gain_ref,
    qk_gain_ref,
    state_ref,
    sems,
):
    pairs = (
        (level_hbm, level_ref),
        (plan_hbm, plan_ref),
        (ids_hbm, ids_ref),
        (freq_hbm, freq_ref),
        (in_hbm, in_ref),
        (qkv_hbm, w_ref),
        (cond_gain_hbm, cond_gain_ref),
        (gain_hbm, gain_ref),
        (qk_gain_hbm, qk_gain_ref),
        (state_hbm, state_ref),
    )
    copies = [pltpu.make_async_copy(src, dst, sems.at[i]) for i, (src, dst) in enumerate(pairs)]
    for copy in copies:
        copy.start()
    for i in (0, 1, 2, 3):
        copies[i].wait()

    freq = freq_ref[...]
    row = rows((8, freq.shape[1]))
    angle = jnp.zeros((8, freq.shape[1]), F32)
    for step in range(STEPS):
        slot = slot_of(step)
        before = jnp.maximum(slot - 1, 0)
        stamp_now = plan_ref[level_ref[slot]].astype(F32)
        stamp_prev = plan_ref[level_ref[before]].astype(F32)
        sigma = stamp_now / 1000.0
        sig_ref[2 * step] = sigma
        sig_ref[2 * step + 1] = jnp.where(slot > 0, stamp_prev / 1000.0, 0.0) - sigma
        angle = jnp.where(row == 2 * step, stamp_now, angle)
        angle = jnp.where(row == 2 * step + 1, stamp_prev, angle)
        angle = jnp.where(row == 2 * step + 4, ids_ref[slot + step].astype(F32), angle)
        angle = jnp.where(row == 2 * step + 5, ids_ref[before + step].astype(F32), angle)
    angle = angle * freq
    wave = jnp.concatenate([jnp.cos(angle), jnp.sin(angle)], axis=1)

    for i in (4, 6, 7, 8, 9):
        copies[i].wait()
    product = qk_gain_ref[0:1, :] * qk_gain_ref[1:2, :]
    safe_ref[0] = (HEAD**0.5 * jnp.max(jnp.abs(product)) <= SAFE).astype(jnp.int32)
    product = product * (math.log2(math.e) / math.sqrt(HEAD))
    qk_ref[...] = jnp.concatenate([product] * 4, axis=1)

    cond = cond_gain_ref[0:1, :] * wave[0:4] + cond_gain_ref[1:2, :] * wave[4:8]
    cond = jnp.concatenate([cond, jnp.zeros_like(cond)], axis=0)
    cond_ref[...] = cond

    embed = in_ref[...]
    none = jnp.zeros((112, embed.shape[1]), BF)
    c_hi, c_lo = halves(cond)
    left = jnp.concatenate([embed, jnp.concatenate([c_hi, c_lo], axis=0), none], axis=0)
    gram = dot_t(left, left)
    lane, row = lanes(gram.shape), rows(gram.shape)
    gram = jnp.where(lane < FEAT + 8, gram + jnp.where(lane >= FEAT, pltpu.roll(gram, WIDE - 8, 1), 0.0), 0.0)
    gram = jnp.where(row < FEAT + 8, gram + jnp.where(row >= FEAT, pltpu.roll(gram, WIDE - 8, 0), 0.0), 0.0)
    g_hi, g_lo = halves(gram)
    gram_hi_ref[...] = g_hi
    gram_lo_ref[...] = g_lo

    gain = gain_ref[...]
    emb = (embed.astype(F32) * gain).astype(BF)
    cg_hi, cg_lo = halves(cond * gain)
    right = jnp.concatenate([emb, jnp.concatenate([cg_hi, cg_lo], axis=0), none], axis=0)
    copies[5].wait()
    full = dot_t(w_ref[...].reshape(3 * COLS, embed.shape[1]), right)
    mat = full[:, 0:FEAT].astype(BF)
    bias = full[:, FEAT:WIDE]
    bias = bias + pltpu.roll(bias, FEAT - 8, 1)
    lane = lanes(bias.shape)
    bias = jnp.where(lane < 4, bias, 0.0)
    high = bias.astype(BF).astype(F32)
    bias = high + pltpu.roll(bias - high, 4, 1)
    packed = bias[0:PACK]
    for i in range(1, 12):
        packed = packed + pltpu.roll(bias[PACK * i : PACK * (i + 1)], 8 * i, 1)
    packed = packed.astype(BF)
    x = state_ref[0].astype(BF)
    for chip in range(CHIPS):
        pay_ref[chip, 0 : 3 * COLS] = mat
        pay_ref[chip, 3 * COLS : 3 * COLS + PACK] = packed
        pay_ref[chip, PAY - TOK : PAY] = x


def fold(level_index, plan, frame_ids, freq, qkv, in_weight, cond_gain, gain, qk_gain, latents):
    width = in_weight.shape[1]
    args = (level_index, plan, frame_ids, freq, qkv, in_weight, cond_gain, gain, qk_gain, latents)
    return pl.pallas_call(
        fold_kernel,
        out_shape=(
            pltpu.VMEM((CHIPS, PAY, FEAT), BF),
            pltpu.VMEM((WIDE, WIDE), BF),
            pltpu.VMEM((WIDE, WIDE), BF),
            pltpu.VMEM((8, width), F32),
            pltpu.VMEM((1, WIDE), F32),
            jax.ShapeDtypeStruct((1,), jnp.int32),
            jax.ShapeDtypeStruct((2 * STEPS,), F32),
        ),
        in_specs=[ANY] * len(args),
        out_specs=(VMEM,) * 5 + (SMEM,) * 2,
        scratch_shapes=[pltpu.SMEM(v.shape, v.dtype) for v in args[:3]]
        + [pltpu.VMEM(v.shape, v.dtype) for v in args[3:]]
        + [pltpu.SemaphoreType.DMA((len(args),))],
        compiler_params=pltpu.CompilerParams(vmem_limit_bytes=40 * 2**20),
        name="fold",
    )(*[in_hbm(v) for v in args])


def unpack(pay_ref, ref, j):
    lane = lanes((PACK, FEAT))
    for m in range(CHIPS):
        packed = pay_ref[m, 3 * COLS : 3 * COLS + PACK, :].astype(F32)
        ref[m * COLS : (m + 1) * COLS, 0:FEAT] = pay_ref[m, j * COLS : (j + 1) * COLS, :]
        for i in range(4):
            shift = 8 * (4 * j + i)
            part = pltpu.roll(packed, FEAT - shift, 1) if shift else packed
            part = jnp.where(lane < 8, part, 0.0)
            ref[m * COLS + i * PACK : m * COLS + (i + 1) * PACK, FEAT:WIDE] = part.astype(BF)


def prepare(step, group, block_ref, gram_hi_ref, gram_lo_ref, ak_ref, xkt_ref, val_ref, rk_ref):
    x = block_ref[...].reshape(SIDE, FEAT)
    lane = lanes((SIDE, FEAT))
    mark = jnp.logical_or(lane == 2 * step + group, lane == 4 + 2 * step + group)
    xk = jnp.concatenate([x, mark.astype(F32).astype(BF)], axis=1)
    row = rows((FEAT, SIDE))
    mark = jnp.logical_or(row == 2 * step + group, row == 4 + 2 * step + group)
    xkt_ref[0:FEAT, :] = jnp.transpose(x)
    xkt_ref[FEAT:WIDE, :] = mark.astype(F32).astype(BF)
    xkt = xkt_ref[...]
    square = dot(gram_hi_ref[...], xkt) + dot(gram_lo_ref[...], xkt)
    m_row = jnp.sum(square * xkt.astype(F32), axis=0, keepdims=True) * (1.0 / 3072.0) + EPS
    r_col = jnp.transpose(jnp.broadcast_to(lax.rsqrt(m_row), (8, SIDE)))[:, 0:1]
    val = jnp.where(lanes((SIDE, WIDE)) == ONE, 1.0, xk.astype(F32) * r_col)
    if group == 1:
        val = jnp.where(slot_of(step) == 0, 0.0, val)
    val_ref[...] = val.astype(BF)
    for g in range(GROUPS):
        u = dot(ak_ref[g * WIDE : (g + 1) * WIDE, :], xkt_ref[...])
        u = jnp.sum((u * u).reshape(4, HEAD, SIDE), axis=1)
        rk = lax.rsqrt(u * (1.0 / HEAD) + EPS * m_row)
        rk_ref[g] = jnp.concatenate([rk, rk], axis=0)


def prepare_own_kernel(step, pay_ref, block_ref, gram_hi_ref, gram_lo_ref, ak_ref, xkt_ref, val_ref, rk_ref):
    unpack(pay_ref, ak_ref, 1)
    prepare(step, 0, block_ref, gram_hi_ref, gram_lo_ref, ak_ref, xkt_ref, val_ref, rk_ref)


def prepare_prev_kernel(step, ak_ref, block_ref, gram_hi_ref, gram_lo_ref, xkt_ref, val_ref, rk_ref):
    prepare(step, 1, block_ref, gram_hi_ref, gram_lo_ref, ak_ref, xkt_ref, val_ref, rk_ref)


def side_shapes():
    return [
        pltpu.VMEM((WIDE, SIDE), BF),
        pltpu.VMEM((SIDE, WIDE), BF),
        pltpu.VMEM((GROUPS, 8, SIDE), F32),
    ]


def prepared(step, group, source, block, gram):
    shapes = side_shapes()
    if group == 0:
        shapes = [pltpu.VMEM((HEADS * HEAD, WIDE), BF)] + shapes
    return pl.pallas_call(
        functools.partial(prepare_own_kernel if group == 0 else prepare_prev_kernel, step),
        out_shape=shapes,
        in_specs=[VMEM] * 4,
        out_specs=[VMEM] * len(shapes),
        compiler_params=pltpu.CompilerParams(vmem_limit_bytes=24 * 2**20),
        cost_estimate=cost(HEADS * HEAD * WIDE * SIDE, 2 * CHIPS * PAY * FEAT),
        name="prepare",
    )(*[in_vmem(v) for v in (source, block, *gram)])


def weigh(g, qc_ref, sides, p_ref):
    for h in range(4):
        span = slice(2 * TOK * h, 2 * TOK * (h + 1))
        for i, (xkt_ref, _, rk_ref) in enumerate(sides):
            s = dot(qc_ref[g, span], xkt_ref[...]) * rk_ref[g, h : h + 1, :]
            p_ref[span, SIDE * i : SIDE * (i + 1)] = jnp.exp2(s).astype(BF)


def collect(g, h, sides, p_ref):
    span = slice(2 * TOK * h, 2 * TOK * (h + 1))
    z = dot(p_ref[span, 0:SIDE], sides[0][1][...])
    for i in range(1, len(sides)):
        z = z + dot(p_ref[span, SIDE * i : SIDE * (i + 1)], sides[i][1][...])
    return z


def own_kernel(
    step,
    safe_ref,
    pay_ref,
    mine_ref,
    other_ref,
    gram_hi_ref,
    gram_lo_ref,
    qk_ref,
    ak_ref,
    xkt_a_ref,
    val_a_ref,
    rk_a_ref,
    sum_ref,
    qc_ref,
    xkt_b_ref,
    val_b_ref,
    rk_b_ref,
    aq_ref,
    p_ref,
):
    chip = lax.axis_index(("y", "far"))
    sides = ((xkt_a_ref, val_a_ref, rk_a_ref), (xkt_b_ref, val_b_ref, rk_b_ref))
    prepare(step, 0, other_ref, gram_hi_ref, gram_lo_ref, ak_ref, *sides[1])

    unpack(pay_ref, aq_ref, 0)
    xq = jnp.concatenate([mine_ref[chip], other_ref[chip]], axis=0)
    row = rows((FEAT, 2 * TOK))
    mark = jnp.logical_or(row == 2 * step, row == 4 + 2 * step)
    xqt = jnp.concatenate([jnp.transpose(xq), mark.astype(F32).astype(BF)], axis=0)
    square = dot(gram_hi_ref[...], xqt) + dot(gram_lo_ref[...], xqt)
    m_q = jnp.sum(square * xqt.astype(F32), axis=0, keepdims=True) * (1.0 / 3072.0) + EPS
    head_of = lanes((2 * TOK, WIDE)) // HEAD

    q = dot(aq_ref[...], xqt).reshape(HEADS, HEAD, 2 * TOK)
    q = q * lax.rsqrt(jnp.sum(q * q, axis=1, keepdims=True) * (1.0 / HEAD) + EPS * m_q[None])
    q = q.reshape(HEADS * HEAD, 2 * TOK)
    for g in range(GROUPS):
        span = slice(g * WIDE, (g + 1) * WIDE)
        some = jnp.transpose(q[span]) * qk_ref[...]
        some = jnp.concatenate([jnp.where(head_of == h, some, 0.0) for h in range(4)], axis=0)
        qc_ref[g] = dot(some.astype(BF), ak_ref[span, :]).astype(BF)

    @pl.when(safe_ref[0] == 1)
    def _():
        def body(i, carry):
            for k in range(3):
                g = 3 * i + k
                weigh(g, qc_ref, sides, p_ref)
                for h in range(4):
                    sum_ref[g, 2 * TOK * h : 2 * TOK * (h + 1)] = collect(g, h, sides, p_ref)
            return carry

        lax.fori_loop(0, GROUPS // 3, body, 0)


def attend_own(step, safe, pay, mine, other, gram, qk, ready):
    group = (GROUPS, 8 * TOK, WIDE)
    held = [in_vmem(v) for v in (pay, mine, other, *gram, qk, *ready)]
    return pl.pallas_call(
        functools.partial(own_kernel, step),
        out_shape=[pltpu.VMEM(group, F32), pltpu.VMEM(group, BF)] + side_shapes(),
        in_specs=[SMEM] + [VMEM] * len(held),
        out_specs=[VMEM] * 5,
        scratch_shapes=[pltpu.VMEM((HEADS * HEAD, WIDE), BF), pltpu.VMEM((8 * TOK, 2 * SIDE), BF)],
        compiler_params=pltpu.CompilerParams(vmem_limit_bytes=32 * 2**20),
        cost_estimate=cost(HEADS * 2 * TOK * WIDE * 4 * SIDE),
        name="attend_own",
    )(safe, *held)


def prev_kernel(
    step,
    safe_ref,
    pay_ref,
    other_ref,
    gram_hi_ref,
    gram_lo_ref,
    ak_ref,
    sum_ref,
    qc_ref,
    xkt_a_ref,
    val_a_ref,
    rk_a_ref,
    xkt_b_ref,
    val_b_ref,
    rk_b_ref,
    xkt_c_ref,
    val_c_ref,
    rk_c_ref,
    out_w_ref,
    part_ref,
    part_other_ref,
    xkt_d_ref,
    val_d_ref,
    rk_d_ref,
    av_ref,
    p_ref,
    s_ref,
    z_ref,
    w_ref,
    sem,
):
    core = lax.axis_index("core")
    copies = []
    for m in range(CHIPS):
        begin = pl.multiple_of((2 * m + core) * COLS, COLS)
        copies.append(pltpu.make_async_copy(out_w_ref.at[pl.ds(begin, COLS)], w_ref.at[pl.ds(m * COLS, COLS)], sem))
    for copy in copies:
        copy.start()
    own = ((xkt_a_ref, val_a_ref, rk_a_ref), (xkt_b_ref, val_b_ref, rk_b_ref))
    prev = ((xkt_c_ref, val_c_ref, rk_c_ref), (xkt_d_ref, val_d_ref, rk_d_ref))
    prepare(step, 1, other_ref, gram_hi_ref, gram_lo_ref, ak_ref, *prev[1])
    unpack(pay_ref, av_ref, 2)

    def settle(g, h, z):
        z_ref[g, 2 * TOK * h : 2 * TOK * (h + 1)] = (z * (1.0 / z[:, ONE : ONE + 1])).astype(BF)

    @pl.when(safe_ref[0] == 1)
    def _():
        def body(i, carry):
            for k in range(3):
                g = 3 * i + k
                weigh(g, qc_ref, prev, p_ref)
                for h in range(4):
                    settle(g, h, collect(g, h, prev, p_ref) + sum_ref[g, 2 * TOK * h : 2 * TOK * (h + 1)])
            return carry

        lax.fori_loop(0, GROUPS // 3, body, 0)

    @pl.when(safe_ref[0] != 1)
    def _():
        every = own + prev
        alone = slot_of(step) == 0

        def body(g, carry):
            for h in range(4):
                span = slice(2 * TOK * h, 2 * TOK * (h + 1))
                for i, (xkt_ref, _, rk_ref) in enumerate(every):
                    s = dot(qc_ref[g, span], xkt_ref[...]) * rk_ref[g, h : h + 1, :]
                    s_ref[:, SIDE * i : SIDE * (i + 1)] = jnp.where(alone, -1e30, s) if i > 1 else s
                s = s_ref[...]
                p_ref[span, :] = jnp.exp2(s - jnp.max(s, axis=1, keepdims=True)).astype(BF)
                settle(g, h, collect(g, h, every, p_ref))
            return carry

        lax.fori_loop(0, GROUPS, body, 0)

    head_of = lanes((2 * TOK, WIDE)) // HEAD
    outs = []
    for g in range(GROUPS):
        o = dot_t(z_ref[g], av_ref[g * WIDE : (g + 1) * WIDE, :])
        picked = jnp.where(head_of == 0, o[0:128], 0.0)
        for h in range(1, 4):
            picked = jnp.where(head_of == h, o[128 * h : 128 * (h + 1)], picked)
        outs.append(picked.astype(BF))
    for copy in copies:
        copy.wait()
    y = dot(jnp.concatenate(outs, axis=1), w_ref[...])
    part_ref[...] = y[0:TOK]
    part_other_ref[...] = y[TOK:].astype(BF)


def attend_prev(step, safe, pay, other, gram, ak, begun, own, ready, out_weight):
    width = out_weight.shape[1]
    half = HEADS * HEAD
    held = [in_vmem(v) for v in (pay, other, *gram, ak, *begun, *own, *ready)]
    return pl.pallas_call(
        functools.partial(prev_kernel, step),
        out_shape=(pltpu.VMEM((TOK, width), F32), pltpu.VMEM((TOK, width), BF)),
        in_specs=[SMEM] + [VMEM] * len(held) + [ANY],
        out_specs=(VMEM, VMEM),
        scratch_shapes=side_shapes()
        + [
            pltpu.VMEM((half, WIDE), BF),
            pltpu.VMEM((8 * TOK, 4 * SIDE), BF),
            pltpu.VMEM((2 * TOK, 4 * SIDE), F32),
            pltpu.VMEM((GROUPS, 8 * TOK, WIDE), BF),
            pltpu.VMEM((half, width), BF),
            pltpu.SemaphoreType.DMA,
        ],
        compiler_params=pltpu.CompilerParams(vmem_limit_bytes=40 * 2**20),
        cost_estimate=cost(HEADS * 2 * TOK * WIDE * 4 * SIDE),
        name="attend_prev",
    )(safe, *held, out_weight)


def finish_kernel(
    step, sig_ref, state_ref, in_ref, cond_ref, part_ref, got_ref, gain_ref, final_ref, fresh_ref, est_ref, new_ref, *sent
):
    state = state_ref[...]
    y = dot(state.astype(BF), in_ref[...]) + cond_ref[2 * step : 2 * step + 1, :]
    y = y + part_ref[...] + got_ref[...].astype(F32)
    scale = lax.rsqrt(jnp.mean(y * y, axis=1, keepdims=True) + EPS)
    velocity = dot((y * scale * gain_ref[...]).astype(BF), final_ref[...])
    est_ref[...] = state - sig_ref[2 * step] * velocity
    new = jnp.where(slot_of(step) == 0, fresh_ref[step], state + sig_ref[2 * step + 1] * velocity)
    new_ref[...] = new
    for sent_ref in sent:
        for chip in range(CHIPS):
            sent_ref[chip] = new.astype(BF)


def finish(step, sig, state, in_weight, cond, part, got, gain, final_weight, fresh):
    out = jax.ShapeDtypeStruct(state.shape, F32)
    shapes = [out, out]
    if step + 1 < STEPS:
        shapes.append(pltpu.VMEM((CHIPS,) + state.shape, BF))
    return pl.pallas_call(
        functools.partial(finish_kernel, step),
        out_shape=shapes,
        in_specs=[SMEM] + [VMEM] * 8,
        out_specs=[VMEM] * len(shapes),
        compiler_params=pltpu.CompilerParams(vmem_limit_bytes=32 * 2**20),
        name="finish",
    )(sig, *[in_vmem(v) for v in (state, in_weight, cond, part, got, gain, final_weight, fresh)])


def passed_along(x, by):
    peers = lax.axis_size("frame")
    return lax.ppermute(x, "frame", [(i, (i + by) % peers) for i in range(peers)])


def swapped(x):
    return lax.ppermute(x, "core", [(0, 1), (1, 0)])


def spread(x):
    return lax.all_to_all(x, ("y", "far"), 0, 0, tiled=True)


def shards(
    latents,
    fresh_noise,
    level_index,
    plan,
    frame_ids,
    in_weight,
    cond_gain,
    norm_gain,
    qkv_weight,
    qk_gain,
    out_weight,
    final_gain,
    final_weight,
):
    half = in_weight.shape[1] // 2
    freq = jnp.asarray(np.exp(-math.log(10000.0) * np.arange(half, dtype=np.float32) / half), F32)
    state = latents[0]
    sent, gram_hi, gram_lo, cond, qk, safe, sig = fold(
        level_index,
        plan,
        frame_ids,
        freq[None],
        jnp.swapaxes(qkv_weight, 1, 2),
        in_weight,
        cond_gain,
        norm_gain[None],
        qk_gain,
        latents,
    )
    gram = (gram_hi, gram_lo)
    pay = spread(sent)
    mine = pay[:, PAY - TOK :, :]
    results = []
    for step in range(STEPS):
        other = swapped(mine)
        before = passed_along(mine, 1)
        ready = prepared(step, 0, pay, mine, gram)
        begun = attend_own(step, safe, pay, mine, other, gram, qk, ready)
        before, *begun = lax.optimization_barrier((before, *begun))
        ak, own = ready[0], (*ready[1:], *begun[2:])
        before_other = swapped(before)
        ready = prepared(step, 1, ak, before, gram)
        part, part_other = attend_prev(step, safe, pay, before_other, gram, ak, begun[:2], own, ready, out_weight)
        got = swapped(part_other)
        estimate, state, *sent = finish(
            step, sig, state, in_weight, cond, part, got, final_gain[None], final_weight, fresh_noise
        )
        results.append(estimate)
        if sent:
            mine = spread(sent[0])
    results[1] = passed_along(results[1], -1)
    state = passed_along(state, -2)
    return (jnp.stack(results)[:, None], state[None])


def solution(mesh):
    split = Mesh(mesh.devices.reshape(8, 4, 2, 2), ("frame", "y", "far", "core"))
    space = ("y", "far", "core")
    in_specs = (
        P("frame", space, None),
        P(None, space, None),
        P(),
        P(),
        P(),
        P(),
        P(),
        P(),
        P(None, None, space),
        P(),
        P(),
        P(),
        P(),
    )
    out_specs = (P(None, "frame", space, None), P("frame", space, None))
    return jax.shard_map(shards, mesh=split, in_specs=in_specs, out_specs=out_specs, check_vma=False)
```

```python
import functools
import math

import jax
import jax.numpy as jnp
import numpy as np
from jax import lax
from jax.experimental import pallas as pl
from jax.experimental.pallas import tpu as pltpu
from jax.sharding import Mesh
from jax.sharding import PartitionSpec as P

HEAD = 64
STEPS = 2
FEAT = 128
WIDE = 256
CHIPS = 8
TOK = 64
COLS = 192
PACK = 48
PAY = 3 * COLS + PACK + TOK
HEADS = CHIPS * 3
GROUPS = HEADS // 4
SIDE = CHIPS * TOK
ONE = 136
EPS = 1e-06
SAFE = 60.0

BF = jnp.bfloat16
F32 = jnp.float32
VMEM = pl.BlockSpec(memory_space=pltpu.VMEM)
SMEM = pl.BlockSpec(memory_space=pltpu.SMEM)
ANY = pl.BlockSpec(memory_space=pl.ANY)


def dot(a, b):
    return jnp.dot(a, b, preferred_element_type=F32)


def dot_t(a, b):
    return lax.dot_general(a, b, (((1,), (1,)), ((), ())), preferred_element_type=F32)


def halves(x):
    high = x.astype(BF)
    return high, (x - high.astype(F32)).astype(BF)


def in_vmem(x):
    return pltpu.with_memory_space_constraint(x, pltpu.VMEM)


def cost(products, bytes_moved=0):
    return pl.CostEstimate(flops=2 * products, transcendentals=0, bytes_accessed=bytes_moved)


def in_hbm(x):
    return pltpu.with_memory_space_constraint(x, pltpu.HBM)


def lanes(shape):
    return lax.broadcasted_iota(jnp.int32, shape, len(shape) - 1)


def rows(shape):
    return lax.broadcasted_iota(jnp.int32, shape, len(shape) - 2)


def slot_of(step):
    count = lax.axis_size("frame")
    return lax.rem(lax.axis_index("frame") + count - step, count)


def fold_kernel(
    level_hbm,
    plan_hbm,
    ids_hbm,
    freq_hbm,
    qkv_hbm,
    in_hbm,
    cond_gain_hbm,
    gain_hbm,
    qk_gain_hbm,
    state_hbm,
    pay_ref,
    gram_hi_ref,
    gram_lo_ref,
    cond_ref,
    qk_ref,
    safe_ref,
    sig_ref,
    level_ref,
    plan_ref,
    ids_ref,
    freq_ref,
    w_ref,
    in_ref,
    cond_gain_ref,
    gain_ref,
    qk_gain_ref,
    state_ref,
    sems,
):
    pairs = (
        (level_hbm, level_ref),
        (plan_hbm, plan_ref),
        (ids_hbm, ids_ref),
        (freq_hbm, freq_ref),
        (in_hbm, in_ref),
        (qkv_hbm, w_ref),
        (cond_gain_hbm, cond_gain_ref),
        (gain_hbm, gain_ref),
        (qk_gain_hbm, qk_gain_ref),
        (state_hbm, state_ref),
    )
    copies = [pltpu.make_async_copy(src, dst, sems.at[i]) for i, (src, dst) in enumerate(pairs)]
    for copy in copies:
        copy.start()
    for i in (0, 1, 2, 3):
        copies[i].wait()

    freq = freq_ref[...]
    row = rows((8, freq.shape[1]))
    angle = jnp.zeros((8, freq.shape[1]), F32)
    for step in range(STEPS):
        slot = slot_of(step)
        before = jnp.maximum(slot - 1, 0)
        stamp_now = plan_ref[level_ref[slot]].astype(F32)
        stamp_prev = plan_ref[level_ref[before]].astype(F32)
        sigma = stamp_now / 1000.0
        sig_ref[2 * step] = sigma
        sig_ref[2 * step + 1] = jnp.where(slot > 0, stamp_prev / 1000.0, 0.0) - sigma
        angle = jnp.where(row == 2 * step, stamp_now, angle)
        angle = jnp.where(row == 2 * step + 1, stamp_prev, angle)
        angle = jnp.where(row == 2 * step + 4, ids_ref[slot + step].astype(F32), angle)
        angle = jnp.where(row == 2 * step + 5, ids_ref[before + step].astype(F32), angle)
    angle = angle * freq
    wave = jnp.concatenate([jnp.cos(angle), jnp.sin(angle)], axis=1)

    for i in (4, 6, 7, 8, 9):
        copies[i].wait()
    product = qk_gain_ref[0:1, :] * qk_gain_ref[1:2, :]
    safe_ref[0] = (HEAD**0.5 * jnp.max(jnp.abs(product)) <= SAFE).astype(jnp.int32)
    product = product * (math.log2(math.e) / math.sqrt(HEAD))
    qk_ref[...] = jnp.concatenate([product] * 4, axis=1)

    cond = cond_gain_ref[0:1, :] * wave[0:4] + cond_gain_ref[1:2, :] * wave[4:8]
    cond = jnp.concatenate([cond, jnp.zeros_like(cond)], axis=0)
    cond_ref[...] = cond

    embed = in_ref[...]
    none = jnp.zeros((112, embed.shape[1]), BF)
    gain = gain_ref[...]
    emb = (embed.astype(F32) * gain).astype(BF)
    cg_hi, cg_lo = halves(cond * gain)
    right = jnp.concatenate([emb, jnp.concatenate([cg_hi, cg_lo], axis=0), none], axis=0)
    copies[5].wait()
    full = dot_t(w_ref[...].reshape(3 * COLS, embed.shape[1]), right)
    mat = full[:, 0:FEAT].astype(BF)
    bias = full[:, FEAT:WIDE]
    bias = bias + pltpu.roll(bias, FEAT - 8, 1)
    lane = lanes(bias.shape)
    bias = jnp.where(lane < 4, bias, 0.0)
    high = bias.astype(BF).astype(F32)
    bias = high + pltpu.roll(bias - high, 4, 1)
    packed = bias[0:PACK]
    for i in range(1, 12):
        packed = packed + pltpu.roll(bias[PACK * i : PACK * (i + 1)], 8 * i, 1)
    packed = packed.astype(BF)
    x = state_ref[0].astype(BF)
    for chip in range(CHIPS):
        pay_ref[chip, 0 : 3 * COLS] = mat
        pay_ref[chip, 3 * COLS : 3 * COLS + PACK] = packed
        pay_ref[chip, PAY - TOK : PAY] = x

    c_hi, c_lo = halves(cond)
    left = jnp.concatenate([embed, jnp.concatenate([c_hi, c_lo], axis=0)], axis=0)
    gram = dot_t(left, jnp.concatenate([left, none], axis=0))
    gram = jnp.concatenate([gram, jnp.zeros((112, WIDE), F32)], axis=0)
    lane, row = lanes(gram.shape), rows(gram.shape)
    gram = jnp.where(lane < FEAT + 8, gram + jnp.where(lane >= FEAT, pltpu.roll(gram, WIDE - 8, 1), 0.0), 0.0)
    gram = jnp.where(row < FEAT + 8, gram + jnp.where(row >= FEAT, pltpu.roll(gram, WIDE - 8, 0), 0.0), 0.0)
    g_hi, g_lo = halves(gram)
    gram_hi_ref[...] = g_hi
    gram_lo_ref[...] = g_lo


def fold(level_index, plan, frame_ids, freq, qkv, in_weight, cond_gain, gain, qk_gain, latents):
    width = in_weight.shape[1]
    args = (level_index, plan, frame_ids, freq, qkv, in_weight, cond_gain, gain, qk_gain, latents)
    return pl.pallas_call(
        fold_kernel,
        out_shape=(
            pltpu.VMEM((CHIPS, PAY, FEAT), BF),
            pltpu.VMEM((WIDE, WIDE), BF),
            pltpu.VMEM((WIDE, WIDE), BF),
            pltpu.VMEM((8, width), F32),
            pltpu.VMEM((1, WIDE), F32),
            jax.ShapeDtypeStruct((1,), jnp.int32),
            jax.ShapeDtypeStruct((2 * STEPS,), F32),
        ),
        in_specs=[ANY] * len(args),
        out_specs=(VMEM,) * 5 + (SMEM,) * 2,
        scratch_shapes=[pltpu.SMEM(v.shape, v.dtype) for v in args[:3]]
        + [pltpu.VMEM(v.shape, v.dtype) for v in args[3:]]
        + [pltpu.SemaphoreType.DMA((len(args),))],
        compiler_params=pltpu.CompilerParams(vmem_limit_bytes=20 * 2**20),
        name="fold",
    )(*[in_hbm(v) for v in args])


def unpack(pay_ref, ref, j):
    lane = lanes((PACK, FEAT))
    for m in range(CHIPS):
        packed = pay_ref[m, 3 * COLS : 3 * COLS + PACK, :].astype(F32)
        ref[m * COLS : (m + 1) * COLS, 0:FEAT] = pay_ref[m, j * COLS : (j + 1) * COLS, :]
        for i in range(4):
            shift = 8 * (4 * j + i)
            part = pltpu.roll(packed, FEAT - shift, 1) if shift else packed
            part = jnp.where(lane < 8, part, 0.0)
            ref[m * COLS + i * PACK : m * COLS + (i + 1) * PACK, FEAT:WIDE] = part.astype(BF)


def prepare(step, group, blocks, gram_hi_ref, gram_lo_ref, ak_ref, xkt_ref, val_ref, rk_ref):
    x = jnp.concatenate([ref[...].reshape(SIDE, FEAT) for ref in blocks], axis=0)
    count = x.shape[0]
    lane = lanes((count, FEAT))
    mark = jnp.logical_or(lane == 2 * step + group, lane == 4 + 2 * step + group)
    xk = jnp.concatenate([x, mark.astype(F32).astype(BF)], axis=1)
    row = rows((FEAT, count))
    mark = jnp.logical_or(row == 2 * step + group, row == 4 + 2 * step + group)
    xkt_ref[0:FEAT, :] = jnp.transpose(x)
    xkt_ref[FEAT:WIDE, :] = mark.astype(F32).astype(BF)
    xkt = xkt_ref[...]
    square = dot(gram_hi_ref[...], xkt) + dot(gram_lo_ref[...], xkt)
    m_row = jnp.sum(square * xkt.astype(F32), axis=0, keepdims=True) * (1.0 / 3072.0) + EPS
    r_col = jnp.transpose(jnp.broadcast_to(lax.rsqrt(m_row), (8, count)))[:, 0:1]
    val = jnp.where(lanes((count, WIDE)) == ONE, 1.0, xk.astype(F32) * r_col)
    if group == 1:
        val = jnp.where(slot_of(step) == 0, 0.0, val)
    val_ref[...] = val.astype(BF)
    for g in range(GROUPS):
        u = dot(ak_ref[g * WIDE : (g + 1) * WIDE, :], xkt_ref[...])
        u = jnp.sum((u * u).reshape(4, HEAD, count), axis=1)
        rk = lax.rsqrt(u * (1.0 / HEAD) + EPS * m_row)
        rk_ref[g] = jnp.concatenate([rk, rk], axis=0)


def prepare_kernel(step, ak_ref, block_ref, gram_hi_ref, gram_lo_ref, xkt_ref, val_ref, rk_ref):
    prepare(step, 1, (block_ref,), gram_hi_ref, gram_lo_ref, ak_ref, xkt_ref, val_ref, rk_ref)


def side_shapes(count):
    return [
        pltpu.VMEM((WIDE, count), BF),
        pltpu.VMEM((count, WIDE), BF),
        pltpu.VMEM((GROUPS, 8, count), F32),
    ]


def prepared(step, ak, block, gram):
    return pl.pallas_call(
        functools.partial(prepare_kernel, step),
        out_shape=side_shapes(SIDE),
        in_specs=[VMEM] * 4,
        out_specs=[VMEM] * 3,
        compiler_params=pltpu.CompilerParams(vmem_limit_bytes=10 * 2**20),
        cost_estimate=cost(HEADS * HEAD * WIDE * SIDE),
        name="prepare",
    )(*[in_vmem(v) for v in (ak, block, *gram)])


def columns(sides):
    begin = 0
    for side in sides:
        count = side[0].shape[1]
        yield side, slice(begin, begin + count)
        begin += count


def weigh(g, qc_ref, sides, p_ref):
    for h in range(4):
        span = slice(2 * TOK * h, 2 * TOK * (h + 1))
        for (xkt_ref, _, rk_ref), keys in columns(sides):
            s = dot(qc_ref[g, span], xkt_ref[...]) * rk_ref[g, h : h + 1, :]
            p_ref[span, keys] = jnp.exp2(s).astype(BF)


def collect(g, h, sides, p_ref):
    span = slice(2 * TOK * h, 2 * TOK * (h + 1))
    parts = [dot(p_ref[span, keys], val_ref[...]) for (_, val_ref, _), keys in columns(sides)]
    return sum(parts[1:], parts[0])


def own_kernel(step, *refs):
    refs = list(refs)
    safe_ref, pay_ref, mine_ref, other_ref, gram_hi_ref, gram_lo_ref, qk_ref = refs[:7]
    del refs[:7]
    copies = []
    if step == 0:
        out_w_ref, w_ref, sem = refs.pop(0), refs.pop(6), refs.pop()
        core = lax.axis_index("core")
        for m in range(CHIPS):
            begin = pl.multiple_of((2 * m + core) * COLS, COLS)
            copies.append(
                pltpu.make_async_copy(out_w_ref.at[pl.ds(begin, COLS)], w_ref.at[pl.ds(m * COLS, COLS)], sem)
            )
        for copy in copies:
            copy.start()
    sum_ref, qc_ref, ak_ref, xkt_ref, val_ref, rk_ref, aq_ref, p_ref = refs
    chip = lax.axis_index(("y", "far"))
    sides = ((xkt_ref, val_ref, rk_ref),)
    unpack(pay_ref, ak_ref, 1)
    prepare(step, 0, (mine_ref, other_ref), gram_hi_ref, gram_lo_ref, ak_ref, *sides[0])

    unpack(pay_ref, aq_ref, 0)
    xq = jnp.concatenate([mine_ref[chip], other_ref[chip]], axis=0)
    row = rows((FEAT, 2 * TOK))
    mark = jnp.logical_or(row == 2 * step, row == 4 + 2 * step)
    xqt = jnp.concatenate([jnp.transpose(xq), mark.astype(F32).astype(BF)], axis=0)
    square = dot(gram_hi_ref[...], xqt) + dot(gram_lo_ref[...], xqt)
    m_q = jnp.sum(square * xqt.astype(F32), axis=0, keepdims=True) * (1.0 / 3072.0) + EPS
    head_of = lanes((2 * TOK, WIDE)) // HEAD

    q = dot(aq_ref[...], xqt).reshape(HEADS, HEAD, 2 * TOK)
    q = q * lax.rsqrt(jnp.sum(q * q, axis=1, keepdims=True) * (1.0 / HEAD) + EPS * m_q[None])
    q = q.reshape(HEADS * HEAD, 2 * TOK)
    for g in range(GROUPS):
        span = slice(g * WIDE, (g + 1) * WIDE)
        some = jnp.transpose(q[span]) * qk_ref[...]
        some = jnp.concatenate([jnp.where(head_of == h, some, 0.0) for h in range(4)], axis=0)
        qc_ref[g] = dot(some.astype(BF), ak_ref[span, :]).astype(BF)

    @pl.when(safe_ref[0] == 1)
    def _():
        def body(i, carry):
            for k in range(3):
                g = 3 * i + k
                weigh(g, qc_ref, sides, p_ref)
                for h in range(4):
                    sum_ref[g, 2 * TOK * h : 2 * TOK * (h + 1)] = collect(g, h, sides, p_ref)
            return carry

        lax.fori_loop(0, GROUPS // 3, body, 0)

    for copy in copies:
        copy.wait()


def attend_own(step, safe, pay, mine, other, gram, qk, out_weight):
    group = (GROUPS, 8 * TOK, WIDE)
    half = HEADS * HEAD
    held = [in_vmem(v) for v in (pay, mine, other, *gram, qk)]
    specs = [SMEM] + [VMEM] * len(held)
    shapes = [pltpu.VMEM(group, F32), pltpu.VMEM(group, BF), pltpu.VMEM((half, WIDE), BF)] + side_shapes(2 * SIDE)
    scratch = [pltpu.VMEM((half, WIDE), BF), pltpu.VMEM((8 * TOK, 2 * SIDE), BF)]
    if step == 0:
        held.append(in_hbm(out_weight))
        specs.append(ANY)
        shapes.append(pltpu.VMEM((half, out_weight.shape[1]), BF))
        scratch.append(pltpu.SemaphoreType.DMA)
    return pl.pallas_call(
        functools.partial(own_kernel, step),
        out_shape=shapes,
        in_specs=specs,
        out_specs=[VMEM] * len(shapes),
        scratch_shapes=scratch,
        compiler_params=pltpu.CompilerParams(vmem_limit_bytes=14 * 2**20),
        cost_estimate=cost(HEADS * 2 * TOK * WIDE * 4 * SIDE),
        name="attend_own",
    )(safe, *held)


def prev_kernel(
    step,
    safe_ref,
    pay_ref,
    other_ref,
    gram_hi_ref,
    gram_lo_ref,
    sum_ref,
    qc_ref,
    ak_ref,
    xkt_a_ref,
    val_a_ref,
    rk_a_ref,
    xkt_c_ref,
    val_c_ref,
    rk_c_ref,
    w_ref,
    state_ref,
    in_ref,
    cond_ref,
    part_ref,
    part_other_ref,
    xkt_d_ref,
    val_d_ref,
    rk_d_ref,
    av_ref,
    p_ref,
    s_ref,
    z_ref,
):
    own = ((xkt_a_ref, val_a_ref, rk_a_ref),)
    prev = ((xkt_c_ref, val_c_ref, rk_c_ref), (xkt_d_ref, val_d_ref, rk_d_ref))
    prepare(step, 1, (other_ref,), gram_hi_ref, gram_lo_ref, ak_ref, *prev[1])
    unpack(pay_ref, av_ref, 2)

    def settle(g, h, z):
        z_ref[g, 2 * TOK * h : 2 * TOK * (h + 1)] = (z * (1.0 / z[:, ONE : ONE + 1])).astype(BF)

    @pl.when(safe_ref[0] == 1)
    def _():
        def body(i, carry):
            for k in range(3):
                g = 3 * i + k
                weigh(g, qc_ref, prev, p_ref)
                for h in range(4):
                    settle(g, h, collect(g, h, prev, p_ref) + sum_ref[g, 2 * TOK * h : 2 * TOK * (h + 1)])
            return carry

        lax.fori_loop(0, GROUPS // 3, body, 0)

    @pl.when(safe_ref[0] != 1)
    def _():
        every = own + prev
        alone = slot_of(step) == 0

        def body(g, carry):
            for h in range(4):
                span = slice(2 * TOK * h, 2 * TOK * (h + 1))
                for (xkt_ref, _, rk_ref), keys in columns(every):
                    s = dot(qc_ref[g, span], xkt_ref[...]) * rk_ref[g, h : h + 1, :]
                    s_ref[:, keys] = jnp.where(alone, -1e30, s) if keys.start else s
                s = s_ref[...]
                p_ref[span, :] = jnp.exp2(s - jnp.max(s, axis=1, keepdims=True)).astype(BF)
                settle(g, h, collect(g, h, every, p_ref))
            return carry

        lax.fori_loop(0, GROUPS, body, 0)

    head_of = lanes((2 * TOK, WIDE)) // HEAD
    outs = []
    for g in range(GROUPS):
        o = dot_t(z_ref[g], av_ref[g * WIDE : (g + 1) * WIDE, :])
        picked = jnp.where(head_of == 0, o[0:128], 0.0)
        for h in range(1, 4):
            picked = jnp.where(head_of == h, o[128 * h : 128 * (h + 1)], picked)
        outs.append(picked.astype(BF))
    y = dot(jnp.concatenate(outs, axis=1), w_ref[...])
    hidden = dot(state_ref[...].astype(BF), in_ref[...]) + cond_ref[2 * step : 2 * step + 1, :]
    part_ref[...] = hidden + y[0:TOK]
    part_other_ref[...] = y[TOK:].astype(BF)


def attend_prev(step, safe, pay, other, gram, begun, ready, weights, state, in_weight, cond):
    width = weights.shape[1]
    held = [in_vmem(v) for v in (pay, other, *gram, *begun, *ready, weights, state, in_weight, cond)]
    return pl.pallas_call(
        functools.partial(prev_kernel, step),
        out_shape=(pltpu.VMEM((TOK, width), F32), pltpu.VMEM((TOK, width), BF)),
        in_specs=[SMEM] + [VMEM] * len(held),
        out_specs=(VMEM, VMEM),
        scratch_shapes=side_shapes(SIDE)
        + [
            pltpu.VMEM((HEADS * HEAD, WIDE), BF),
            pltpu.VMEM((8 * TOK, 4 * SIDE), BF),
            pltpu.VMEM((2 * TOK, 4 * SIDE), F32),
            pltpu.VMEM((GROUPS, 8 * TOK, WIDE), BF),
        ],
        compiler_params=pltpu.CompilerParams(vmem_limit_bytes=16 * 2**20),
        cost_estimate=cost(HEADS * 2 * TOK * WIDE * 4 * SIDE),
        name="attend_prev",
    )(safe, *held)


def finish_kernel(step, sig_ref, state_ref, part_ref, got_ref, gain_ref, final_ref, fresh_ref, est_ref, new_ref, *sent):
    state = state_ref[...]
    y = part_ref[...] + got_ref[...].astype(F32)
    scale = lax.rsqrt(jnp.mean(y * y, axis=1, keepdims=True) + EPS)
    velocity = dot((y * scale * gain_ref[...]).astype(BF), final_ref[...])
    est_ref[...] = state - sig_ref[2 * step] * velocity
    new = jnp.where(slot_of(step) == 0, fresh_ref[step], state + sig_ref[2 * step + 1] * velocity)
    new_ref[...] = new
    for sent_ref in sent:
        for chip in range(CHIPS):
            sent_ref[chip] = new.astype(BF)


def finish(step, sig, state, part, got, gain, final_weight, fresh):
    out = jax.ShapeDtypeStruct(state.shape, F32)
    shapes = [out, out]
    if step + 1 < STEPS:
        shapes.append(pltpu.VMEM((CHIPS,) + state.shape, BF))
    return pl.pallas_call(
        functools.partial(finish_kernel, step),
        out_shape=shapes,
        in_specs=[SMEM] + [VMEM] * 6,
        out_specs=[VMEM] * len(shapes),
        compiler_params=pltpu.CompilerParams(vmem_limit_bytes=12 * 2**20),
        name="finish",
    )(sig, *[in_vmem(v) for v in (state, part, got, gain, final_weight, fresh)])


def leave_kernel(first_ref, second_ref, queue_ref, est_ref, out_ref, sems):
    pairs = ((first_ref, est_ref.at[0, 0]), (second_ref, est_ref.at[1, 0]), (queue_ref, out_ref.at[0]))
    copies = [pltpu.make_async_copy(src, dst, sems.at[i]) for i, (src, dst) in enumerate(pairs)]
    for copy in copies:
        copy.start()
    for copy in copies:
        copy.wait()


def leave(first, second, queue):
    return pl.pallas_call(
        leave_kernel,
        out_shape=(
            jax.ShapeDtypeStruct((STEPS, 1) + first.shape, F32),
            jax.ShapeDtypeStruct((1,) + queue.shape, F32),
        ),
        in_specs=[VMEM] * 3,
        out_specs=(ANY, ANY),
        scratch_shapes=[pltpu.SemaphoreType.DMA((3,))],
        name="leave",
    )(in_vmem(first), in_vmem(second), in_vmem(queue))


def passed_along(x, by):
    peers = lax.axis_size("frame")
    return lax.ppermute(x, "frame", [(i, (i + by) % peers) for i in range(peers)])


def swapped(x):
    return lax.ppermute(x, "core", [(0, 1), (1, 0)])


def spread(x):
    return lax.all_to_all(x, ("y", "far"), 0, 0, tiled=True)


def shards(
    latents,
    fresh_noise,
    level_index,
    plan,
    frame_ids,
    in_weight,
    cond_gain,
    norm_gain,
    qkv_weight,
    qk_gain,
    out_weight,
    final_gain,
    final_weight,
):
    half = in_weight.shape[1] // 2
    freq = jnp.asarray(np.exp(-math.log(10000.0) * np.arange(half, dtype=np.float32) / half), F32)
    state = latents[0]
    sent, gram_hi, gram_lo, cond, qk, safe, sig = fold(
        level_index,
        plan,
        frame_ids,
        freq[None],
        jnp.swapaxes(qkv_weight, 1, 2),
        in_weight,
        cond_gain,
        norm_gain[None],
        qk_gain,
        latents,
    )
    gram = (gram_hi, gram_lo)
    pay = spread(sent)
    mine = pay[:, PAY - TOK :, :]
    results = []
    for step in range(STEPS):
        other = swapped(mine)
        before = passed_along(mine, 1)
        begun = list(attend_own(step, safe, pay, mine, other, gram, qk, out_weight))
        if step == 0:
            weights = begun.pop()
        before, *begun = lax.optimization_barrier((before, *begun))
        before_other = swapped(before)
        ready = prepared(step, begun[2], before, gram)
        part, part_other = attend_prev(
            step, safe, pay, before_other, gram, begun, ready, weights, state, in_weight, cond
        )
        got = swapped(part_other)
        estimate, state, *sent = finish(step, sig, state, part, got, final_gain[None], final_weight, fresh_noise)
        results.append(estimate)
        if sent:
            mine = spread(sent[0])
    queue = passed_along(state, -2)
    return leave(results[0], passed_along(results[1], -1), queue)


def solution(mesh):
    split = Mesh(mesh.devices.reshape(8, 4, 2, 2), ("frame", "y", "far", "core"))
    space = ("y", "far", "core")
    in_specs = (
        P("frame", space, None),
        P(None, space, None),
        P(),
        P(),
        P(),
        P(),
        P(),
        P(),
        P(None, None, space),
        P(),
        P(),
        P(),
        P(),
    )
    out_specs = (P(None, "frame", space, None), P("frame", space, None))
    return jax.shard_map(shards, mesh=split, in_specs=in_specs, out_specs=out_specs, check_vma=False)
```

```python
import functools
import math

import jax
import jax.numpy as jnp
import numpy as np
from jax import lax
from jax.experimental import pallas as pl
from jax.experimental.pallas import tpu as pltpu
from jax.sharding import Mesh
from jax.sharding import PartitionSpec as P

HEAD = 64
STEPS = 2
FEAT = 128
WIDE = 256
CHIPS = 8
TOK = 64
COLS = 192
PACK = 48
PAY = 3 * COLS + PACK + TOK
HEADS = CHIPS * 3
GROUPS = HEADS // 4
SIDE = CHIPS * TOK
ONE = 136
EPS = 1e-06
SAFE = 60.0

BF = jnp.bfloat16
F32 = jnp.float32
VMEM = pl.BlockSpec(memory_space=pltpu.VMEM)
SMEM = pl.BlockSpec(memory_space=pltpu.SMEM)
ANY = pl.BlockSpec(memory_space=pl.ANY)


def dot(a, b):
    return jnp.dot(a, b, preferred_element_type=F32)


def dot_t(a, b):
    return lax.dot_general(a, b, (((1,), (1,)), ((), ())), preferred_element_type=F32)


def halves(x):
    high = x.astype(BF)
    return high, (x - high.astype(F32)).astype(BF)


def in_vmem(x):
    return pltpu.with_memory_space_constraint(x, pltpu.VMEM)


def cost(products, bytes_moved=0):
    return pl.CostEstimate(flops=2 * products, transcendentals=0, bytes_accessed=bytes_moved)


def in_hbm(x):
    return pltpu.with_memory_space_constraint(x, pltpu.HBM)


def lanes(shape):
    return lax.broadcasted_iota(jnp.int32, shape, len(shape) - 1)


def rows(shape):
    return lax.broadcasted_iota(jnp.int32, shape, len(shape) - 2)


def slot_of(step):
    count = lax.axis_size("frame")
    return lax.rem(lax.axis_index("frame") + count - step, count)


def fold_kernel(
    level_hbm,
    plan_hbm,
    ids_hbm,
    freq_hbm,
    qkv_hbm,
    in_hbm,
    cond_gain_hbm,
    gain_hbm,
    qk_gain_hbm,
    state_hbm,
    pay_ref,
    gram_hi_ref,
    gram_lo_ref,
    cond_ref,
    qk_ref,
    safe_ref,
    sig_ref,
    level_ref,
    plan_ref,
    ids_ref,
    freq_ref,
    w_ref,
    in_ref,
    cond_gain_ref,
    gain_ref,
    qk_gain_ref,
    state_ref,
    sems,
):
    pairs = (
        (level_hbm, level_ref),
        (plan_hbm, plan_ref),
        (ids_hbm, ids_ref),
        (freq_hbm, freq_ref),
        (in_hbm, in_ref),
        (qkv_hbm, w_ref),
        (cond_gain_hbm, cond_gain_ref),
        (gain_hbm, gain_ref),
        (qk_gain_hbm, qk_gain_ref),
        (state_hbm, state_ref),
    )
    copies = [pltpu.make_async_copy(src, dst, sems.at[i]) for i, (src, dst) in enumerate(pairs)]
    for copy in copies:
        copy.start()
    for i in (0, 1, 2, 3):
        copies[i].wait()

    freq = freq_ref[...]
    row = rows((8, freq.shape[1]))
    angle = jnp.zeros((8, freq.shape[1]), F32)
    for step in range(STEPS):
        slot = slot_of(step)
        before = jnp.maximum(slot - 1, 0)
        stamp_now = plan_ref[level_ref[slot]].astype(F32)
        stamp_prev = plan_ref[level_ref[before]].astype(F32)
        sigma = stamp_now / 1000.0
        sig_ref[2 * step] = sigma
        sig_ref[2 * step + 1] = jnp.where(slot > 0, stamp_prev / 1000.0, 0.0) - sigma
        angle = jnp.where(row == 2 * step, stamp_now, angle)
        angle = jnp.where(row == 2 * step + 1, stamp_prev, angle)
        angle = jnp.where(row == 2 * step + 4, ids_ref[slot + step].astype(F32), angle)
        angle = jnp.where(row == 2 * step + 5, ids_ref[before + step].astype(F32), angle)
    angle = angle * freq
    wave = jnp.concatenate([jnp.cos(angle), jnp.sin(angle)], axis=1)

    for i in (4, 6, 7, 8, 9):
        copies[i].wait()
    product = qk_gain_ref[0:1, :] * qk_gain_ref[1:2, :]
    safe_ref[0] = (HEAD**0.5 * jnp.max(jnp.abs(product)) <= SAFE).astype(jnp.int32)
    product = product * (math.log2(math.e) / math.sqrt(HEAD))
    qk_ref[...] = jnp.concatenate([product] * 4, axis=1)

    cond = cond_gain_ref[0:1, :] * wave[0:4] + cond_gain_ref[1:2, :] * wave[4:8]
    cond = jnp.concatenate([cond, jnp.zeros_like(cond)], axis=0)
    cond_ref[...] = cond

    embed = in_ref[...]
    none = jnp.zeros((112, embed.shape[1]), BF)
    gain = gain_ref[...]
    emb = (embed.astype(F32) * gain).astype(BF)
    cg_hi, cg_lo = halves(cond * gain)
    right = jnp.concatenate([emb, jnp.concatenate([cg_hi, cg_lo], axis=0), none], axis=0)
    copies[5].wait()
    full = dot_t(w_ref[...].reshape(3 * COLS, embed.shape[1]), right)
    mat = full[:, 0:FEAT].astype(BF)
    bias = full[:, FEAT:WIDE]
    bias = bias + pltpu.roll(bias, FEAT - 8, 1)
    lane = lanes(bias.shape)
    bias = jnp.where(lane < 4, bias, 0.0)
    high = bias.astype(BF).astype(F32)
    bias = high + pltpu.roll(bias - high, 4, 1)
    packed = bias[0:PACK]
    for i in range(1, 12):
        packed = packed + pltpu.roll(bias[PACK * i : PACK * (i + 1)], 8 * i, 1)
    packed = packed.astype(BF)
    x = state_ref[0].astype(BF)
    for chip in range(CHIPS):
        pay_ref[chip, 0 : 3 * COLS] = mat
        pay_ref[chip, 3 * COLS : 3 * COLS + PACK] = packed
        pay_ref[chip, PAY - TOK : PAY] = x

    c_hi, c_lo = halves(cond)
    left = jnp.concatenate([embed, jnp.concatenate([c_hi, c_lo], axis=0)], axis=0)
    gram = dot_t(left, jnp.concatenate([left, none], axis=0))
    gram = jnp.concatenate([gram, jnp.zeros((112, WIDE), F32)], axis=0)
    lane, row = lanes(gram.shape), rows(gram.shape)
    gram = jnp.where(lane < FEAT + 8, gram + jnp.where(lane >= FEAT, pltpu.roll(gram, WIDE - 8, 1), 0.0), 0.0)
    gram = jnp.where(row < FEAT + 8, gram + jnp.where(row >= FEAT, pltpu.roll(gram, WIDE - 8, 0), 0.0), 0.0)
    g_hi, g_lo = halves(gram)
    gram_hi_ref[...] = g_hi
    gram_lo_ref[...] = g_lo


def fold(level_index, plan, frame_ids, freq, qkv, in_weight, cond_gain, gain, qk_gain, latents):
    width = in_weight.shape[1]
    args = (level_index, plan, frame_ids, freq, qkv, in_weight, cond_gain, gain, qk_gain, latents)
    return pl.pallas_call(
        fold_kernel,
        out_shape=(
            pltpu.VMEM((CHIPS, PAY, FEAT), BF),
            pltpu.VMEM((WIDE, WIDE), BF),
            pltpu.VMEM((WIDE, WIDE), BF),
            pltpu.VMEM((8, width), F32),
            pltpu.VMEM((1, WIDE), F32),
            jax.ShapeDtypeStruct((1,), jnp.int32),
            jax.ShapeDtypeStruct((2 * STEPS,), F32),
        ),
        in_specs=[ANY] * len(args),
        out_specs=(VMEM,) * 5 + (SMEM,) * 2,
        scratch_shapes=[pltpu.SMEM(v.shape, v.dtype) for v in args[:3]]
        + [pltpu.VMEM(v.shape, v.dtype) for v in args[3:]]
        + [pltpu.SemaphoreType.DMA((len(args),))],
        compiler_params=pltpu.CompilerParams(vmem_limit_bytes=20 * 2**20),
        name="fold",
    )(*[in_hbm(v) for v in args])


def unpack(pay_ref, ref, j):
    lane = lanes((PACK, FEAT))
    for m in range(CHIPS):
        packed = pay_ref[m, 3 * COLS : 3 * COLS + PACK, :].astype(F32)
        ref[m * COLS : (m + 1) * COLS, 0:FEAT] = pay_ref[m, j * COLS : (j + 1) * COLS, :]
        for i in range(4):
            shift = 8 * (4 * j + i)
            part = pltpu.roll(packed, FEAT - shift, 1) if shift else packed
            part = jnp.where(lane < 8, part, 0.0)
            ref[m * COLS + i * PACK : m * COLS + (i + 1) * PACK, FEAT:WIDE] = part.astype(BF)


def prepare(step, group, blocks, gram_hi_ref, gram_lo_ref, ak_ref, xkt_ref, val_ref, rk_ref):
    x = jnp.concatenate([ref[...].reshape(SIDE, FEAT) for ref in blocks], axis=0)
    count = x.shape[0]
    lane = lanes((count, FEAT))
    mark = jnp.logical_or(lane == 2 * step + group, lane == 4 + 2 * step + group)
    xk = jnp.concatenate([x, mark.astype(F32).astype(BF)], axis=1)
    row = rows((FEAT, count))
    mark = jnp.logical_or(row == 2 * step + group, row == 4 + 2 * step + group)
    xkt_ref[0:FEAT, :] = jnp.transpose(x)
    xkt_ref[FEAT:WIDE, :] = mark.astype(F32).astype(BF)
    xkt = xkt_ref[...]
    square = dot(gram_hi_ref[...], xkt) + dot(gram_lo_ref[...], xkt)
    m_row = jnp.sum(square * xkt.astype(F32), axis=0, keepdims=True) * (1.0 / 3072.0) + EPS
    r_col = jnp.transpose(jnp.broadcast_to(lax.rsqrt(m_row), (8, count)))[:, 0:1]
    val = jnp.where(lanes((count, WIDE)) == ONE, 1.0, xk.astype(F32) * r_col)
    if group == 1:
        val = jnp.where(slot_of(step) == 0, 0.0, val)
    val_ref[...] = val.astype(BF)
    for g in range(GROUPS):
        u = dot(ak_ref[g * WIDE : (g + 1) * WIDE, :], xkt_ref[...])
        u = jnp.sum((u * u).reshape(4, HEAD, count), axis=1)
        rk = lax.rsqrt(u * (1.0 / HEAD) + EPS * m_row)
        rk_ref[g] = jnp.concatenate([rk, rk], axis=0)


def queries(step, tokens, pay_ref, gram_hi_ref, gram_lo_ref, qk_ref, aq_ref, ak_ref, qc_ref):
    unpack(pay_ref, aq_ref, 0)
    xq = jnp.concatenate(tokens, axis=0)
    row = rows((FEAT, 2 * TOK))
    mark = jnp.logical_or(row == 2 * step, row == 4 + 2 * step)
    xqt = jnp.concatenate([jnp.transpose(xq), mark.astype(F32).astype(BF)], axis=0)
    square = dot(gram_hi_ref[...], xqt) + dot(gram_lo_ref[...], xqt)
    m_q = jnp.sum(square * xqt.astype(F32), axis=0, keepdims=True) * (1.0 / 3072.0) + EPS
    head_of = lanes((2 * TOK, WIDE)) // HEAD

    q = dot(aq_ref[...], xqt).reshape(HEADS, HEAD, 2 * TOK)
    q = q * lax.rsqrt(jnp.sum(q * q, axis=1, keepdims=True) * (1.0 / HEAD) + EPS * m_q[None])
    q = q.reshape(HEADS * HEAD, 2 * TOK)
    for g in range(GROUPS):
        span = slice(g * WIDE, (g + 1) * WIDE)
        some = jnp.transpose(q[span]) * qk_ref[...]
        some = jnp.concatenate([jnp.where(head_of == h, some, 0.0) for h in range(4)], axis=0)
        qc_ref[g] = dot(some.astype(BF), ak_ref[span, :]).astype(BF)


def prepare_own_kernel(step, *refs):
    refs = list(refs)
    pay_ref, block_ref, gram_hi_ref, gram_lo_ref = refs[:4]
    del refs[:4]
    if step == 0:
        qk_ref, partner_ref, qc_ref, aq_ref = refs.pop(0), refs.pop(0), refs.pop(4), refs.pop()
    ak_ref, xkt_ref, val_ref, rk_ref = refs
    unpack(pay_ref, ak_ref, 1)
    prepare(step, 0, (block_ref,), gram_hi_ref, gram_lo_ref, ak_ref, xkt_ref, val_ref, rk_ref)
    if step == 0:
        chip = lax.axis_index(("y", "far"))
        tokens = (block_ref[chip], partner_ref[...].astype(BF))
        queries(step, tokens, pay_ref, gram_hi_ref, gram_lo_ref, qk_ref, aq_ref, ak_ref, qc_ref)


def prepared_own(step, pay, block, gram, qk, partner):
    half = HEADS * HEAD
    held = [in_vmem(v) for v in (pay, block, *gram)]
    shapes = [pltpu.VMEM((half, WIDE), BF)] + side_shapes(SIDE)
    scratch = []
    if step == 0:
        held += [in_vmem(qk), in_vmem(partner)]
        shapes.append(pltpu.VMEM((GROUPS, 8 * TOK, WIDE), BF))
        scratch.append(pltpu.VMEM((half, WIDE), BF))
    return pl.pallas_call(
        functools.partial(prepare_own_kernel, step),
        out_shape=shapes,
        in_specs=[VMEM] * len(held),
        out_specs=[VMEM] * len(shapes),
        scratch_shapes=scratch,
        compiler_params=pltpu.CompilerParams(vmem_limit_bytes=12 * 2**20),
        cost_estimate=cost(HEADS * HEAD * WIDE * SIDE, 2 * CHIPS * PAY * FEAT),
        name="prepare_own",
    )(*held)


def prepare_kernel(step, ak_ref, block_ref, gram_hi_ref, gram_lo_ref, xkt_ref, val_ref, rk_ref):
    prepare(step, 1, (block_ref,), gram_hi_ref, gram_lo_ref, ak_ref, xkt_ref, val_ref, rk_ref)


def side_shapes(count):
    return [
        pltpu.VMEM((WIDE, count), BF),
        pltpu.VMEM((count, WIDE), BF),
        pltpu.VMEM((GROUPS, 8, count), F32),
    ]


def prepared(step, ak, block, gram):
    return pl.pallas_call(
        functools.partial(prepare_kernel, step),
        out_shape=side_shapes(SIDE),
        in_specs=[VMEM] * 4,
        out_specs=[VMEM] * 3,
        compiler_params=pltpu.CompilerParams(vmem_limit_bytes=10 * 2**20),
        cost_estimate=cost(HEADS * HEAD * WIDE * SIDE),
        name="prepare",
    )(*[in_vmem(v) for v in (ak, block, *gram)])


def columns(sides):
    begin = 0
    for side in sides:
        count = side[0].shape[1]
        yield side, slice(begin, begin + count)
        begin += count


def weigh(g, qc_ref, sides, p_ref):
    for h in range(4):
        span = slice(2 * TOK * h, 2 * TOK * (h + 1))
        for (xkt_ref, _, rk_ref), keys in columns(sides):
            s = dot(qc_ref[g, span], xkt_ref[...]) * rk_ref[g, h : h + 1, :]
            p_ref[span, keys] = jnp.exp2(s).astype(BF)


def collect(g, h, sides, p_ref):
    span = slice(2 * TOK * h, 2 * TOK * (h + 1))
    parts = [dot(p_ref[span, keys], val_ref[...]) for (_, val_ref, _), keys in columns(sides)]
    return sum(parts[1:], parts[0])


def own_kernel(step, *refs):
    refs = list(refs)
    safe_ref, other_ref, gram_hi_ref, gram_lo_ref, ak_ref = refs[:5]
    sides = (refs[5:8],)
    del refs[:8]
    copies = []
    if step == 0:
        qc_ref, out_w_ref, w_ref, sem = refs.pop(0), refs.pop(0), refs.pop(4), refs.pop()
        core = lax.axis_index("core")
        for m in range(CHIPS):
            begin = pl.multiple_of((2 * m + core) * COLS, COLS)
            copies.append(
                pltpu.make_async_copy(out_w_ref.at[pl.ds(begin, COLS)], w_ref.at[pl.ds(m * COLS, COLS)], sem)
            )
        for copy in copies:
            copy.start()
    else:
        pay_ref, mine_ref, qk_ref, qc_ref, aq_ref = refs.pop(0), refs.pop(0), refs.pop(0), refs.pop(4), refs.pop()
    sum_ref, p_ref = refs.pop(0), refs.pop()
    sides += (tuple(refs),)
    prepare(step, 0, (other_ref,), gram_hi_ref, gram_lo_ref, ak_ref, *sides[1])
    if step > 0:
        chip = lax.axis_index(("y", "far"))
        tokens = (mine_ref[chip], other_ref[chip])
        queries(step, tokens, pay_ref, gram_hi_ref, gram_lo_ref, qk_ref, aq_ref, ak_ref, qc_ref)

    @pl.when(safe_ref[0] == 1)
    def _():
        def body(i, carry):
            for k in range(3):
                g = 3 * i + k
                weigh(g, qc_ref, sides, p_ref)
                for h in range(4):
                    sum_ref[g, 2 * TOK * h : 2 * TOK * (h + 1)] = collect(g, h, sides, p_ref)
            return carry

        lax.fori_loop(0, GROUPS // 3, body, 0)

    for copy in copies:
        copy.wait()


def attend_own(step, safe, pay, mine, other, gram, qk, ready, out_weight):
    group = (GROUPS, 8 * TOK, WIDE)
    half = HEADS * HEAD
    held = [in_vmem(v) for v in (other, *gram, *ready)]
    shapes = [pltpu.VMEM(group, F32)] + side_shapes(SIDE)
    scratch = [pltpu.VMEM((8 * TOK, 2 * SIDE), BF)]
    if step == 0:
        held.append(in_hbm(out_weight))
        shapes.append(pltpu.VMEM((half, out_weight.shape[1]), BF))
        scratch.append(pltpu.SemaphoreType.DMA)
    else:
        held += [in_vmem(v) for v in (pay, mine, qk)]
        shapes.append(pltpu.VMEM(group, BF))
        scratch.append(pltpu.VMEM((half, WIDE), BF))
    return pl.pallas_call(
        functools.partial(own_kernel, step),
        out_shape=shapes,
        in_specs=[SMEM] + [VMEM] * (len(held) - 1) + [ANY if step == 0 else VMEM],
        out_specs=[VMEM] * len(shapes),
        scratch_shapes=scratch,
        compiler_params=pltpu.CompilerParams(vmem_limit_bytes=14 * 2**20),
        cost_estimate=cost(HEADS * 2 * TOK * WIDE * 4 * SIDE),
        name="attend_own",
    )(safe, *held)


def prev_kernel(
    step,
    safe_ref,
    pay_ref,
    other_ref,
    gram_hi_ref,
    gram_lo_ref,
    sum_ref,
    qc_ref,
    ak_ref,
    xkt_a_ref,
    val_a_ref,
    rk_a_ref,
    xkt_b_ref,
    val_b_ref,
    rk_b_ref,
    xkt_c_ref,
    val_c_ref,
    rk_c_ref,
    w_ref,
    state_ref,
    in_ref,
    cond_ref,
    part_ref,
    part_other_ref,
    xkt_d_ref,
    val_d_ref,
    rk_d_ref,
    av_ref,
    p_ref,
    s_ref,
    z_ref,
):
    own = ((xkt_a_ref, val_a_ref, rk_a_ref), (xkt_b_ref, val_b_ref, rk_b_ref))
    prev = ((xkt_c_ref, val_c_ref, rk_c_ref), (xkt_d_ref, val_d_ref, rk_d_ref))
    prepare(step, 1, (other_ref,), gram_hi_ref, gram_lo_ref, ak_ref, *prev[1])
    unpack(pay_ref, av_ref, 2)

    def settle(g, h, z):
        z_ref[g, 2 * TOK * h : 2 * TOK * (h + 1)] = (z * (1.0 / z[:, ONE : ONE + 1])).astype(BF)

    @pl.when(safe_ref[0] == 1)
    def _():
        def body(i, carry):
            for k in range(3):
                g = 3 * i + k
                weigh(g, qc_ref, prev, p_ref)
                for h in range(4):
                    settle(g, h, collect(g, h, prev, p_ref) + sum_ref[g, 2 * TOK * h : 2 * TOK * (h + 1)])
            return carry

        lax.fori_loop(0, GROUPS // 3, body, 0)

    @pl.when(safe_ref[0] != 1)
    def _():
        every = own + prev
        alone = slot_of(step) == 0

        def body(g, carry):
            for h in range(4):
                span = slice(2 * TOK * h, 2 * TOK * (h + 1))
                for (xkt_ref, _, rk_ref), keys in columns(every):
                    s = dot(qc_ref[g, span], xkt_ref[...]) * rk_ref[g, h : h + 1, :]
                    s_ref[:, keys] = jnp.where(alone, -1e30, s) if keys.start >= 2 * SIDE else s
                s = s_ref[...]
                p_ref[span, :] = jnp.exp2(s - jnp.max(s, axis=1, keepdims=True)).astype(BF)
                settle(g, h, collect(g, h, every, p_ref))
            return carry

        lax.fori_loop(0, GROUPS, body, 0)

    head_of = lanes((2 * TOK, WIDE)) // HEAD
    outs = []
    for g in range(GROUPS):
        o = dot_t(z_ref[g], av_ref[g * WIDE : (g + 1) * WIDE, :])
        picked = jnp.where(head_of == 0, o[0:128], 0.0)
        for h in range(1, 4):
            picked = jnp.where(head_of == h, o[128 * h : 128 * (h + 1)], picked)
        outs.append(picked.astype(BF))
    y = dot(jnp.concatenate(outs, axis=1), w_ref[...])
    hidden = dot(state_ref[...].astype(BF), in_ref[...]) + cond_ref[2 * step : 2 * step + 1, :]
    part_ref[...] = hidden + y[0:TOK]
    part_other_ref[...] = y[TOK:].astype(BF)


def attend_prev(step, safe, pay, other, gram, begun, ready, weights, state, in_weight, cond):
    width = weights.shape[1]
    held = [in_vmem(v) for v in (pay, other, *gram, *begun, *ready, weights, state, in_weight, cond)]
    return pl.pallas_call(
        functools.partial(prev_kernel, step),
        out_shape=(pltpu.VMEM((TOK, width), F32), pltpu.VMEM((TOK, width), BF)),
        in_specs=[SMEM] + [VMEM] * len(held),
        out_specs=(VMEM, VMEM),
        scratch_shapes=side_shapes(SIDE)
        + [
            pltpu.VMEM((HEADS * HEAD, WIDE), BF),
            pltpu.VMEM((8 * TOK, 4 * SIDE), BF),
            pltpu.VMEM((2 * TOK, 4 * SIDE), F32),
            pltpu.VMEM((GROUPS, 8 * TOK, WIDE), BF),
        ],
        compiler_params=pltpu.CompilerParams(vmem_limit_bytes=16 * 2**20),
        cost_estimate=cost(HEADS * 2 * TOK * WIDE * 4 * SIDE),
        name="attend_prev",
    )(safe, *held)


def finish_kernel(step, sig_ref, state_ref, part_ref, got_ref, gain_ref, final_ref, fresh_ref, est_ref, new_ref, *sent):
    state = state_ref[...]
    y = part_ref[...] + got_ref[...].astype(F32)
    scale = lax.rsqrt(jnp.mean(y * y, axis=1, keepdims=True) + EPS)
    velocity = dot((y * scale * gain_ref[...]).astype(BF), final_ref[...])
    est_ref[...] = state - sig_ref[2 * step] * velocity
    new = jnp.where(slot_of(step) == 0, fresh_ref[step], state + sig_ref[2 * step + 1] * velocity)
    new_ref[...] = new
    for sent_ref in sent:
        for chip in range(CHIPS):
            sent_ref[chip] = new.astype(BF)


def finish(step, sig, state, part, got, gain, final_weight, fresh):
    out = jax.ShapeDtypeStruct(state.shape, F32)
    shapes = [out, out]
    if step + 1 < STEPS:
        shapes.append(pltpu.VMEM((CHIPS,) + state.shape, BF))
    return pl.pallas_call(
        functools.partial(finish_kernel, step),
        out_shape=shapes,
        in_specs=[SMEM] + [VMEM] * 6,
        out_specs=[VMEM] * len(shapes),
        compiler_params=pltpu.CompilerParams(vmem_limit_bytes=12 * 2**20),
        name="finish",
    )(sig, *[in_vmem(v) for v in (state, part, got, gain, final_weight, fresh)])


def leave_kernel(queue_ref, second_ref, first_ref, est_ref, out_ref, sems):
    pairs = ((first_ref, est_ref.at[0, 0]), (second_ref, est_ref.at[1, 0]), (queue_ref, out_ref.at[0]))
    copies = [pltpu.make_async_copy(src, dst, sems.at[i]) for i, (src, dst) in enumerate(pairs)]
    for copy in copies:
        copy.start()
    for copy in copies:
        copy.wait()


def leave(first, second, queue):
    return pl.pallas_call(
        leave_kernel,
        out_shape=(
            jax.ShapeDtypeStruct((STEPS, 1) + first.shape, F32),
            jax.ShapeDtypeStruct((1,) + queue.shape, F32),
        ),
        in_specs=[VMEM] * 3,
        out_specs=(ANY, ANY),
        scratch_shapes=[pltpu.SemaphoreType.DMA((3,))],
        name="leave",
    )(in_vmem(queue), in_vmem(second), in_vmem(first))


def passed_along(x, by):
    peers = lax.axis_size("frame")
    return lax.ppermute(x, "frame", [(i, (i + by) % peers) for i in range(peers)])


def swapped(x):
    return lax.ppermute(x, "core", [(0, 1), (1, 0)])


def spread(x):
    return lax.all_to_all(x, ("y", "far"), 0, 0, tiled=True)


def shards(
    latents,
    fresh_noise,
    level_index,
    plan,
    frame_ids,
    in_weight,
    cond_gain,
    norm_gain,
    qkv_weight,
    qk_gain,
    out_weight,
    final_gain,
    final_weight,
):
    half = in_weight.shape[1] // 2
    freq = jnp.asarray(np.exp(-math.log(10000.0) * np.arange(half, dtype=np.float32) / half), F32)
    state = latents[0]
    partner = swapped(state)
    sent, gram_hi, gram_lo, cond, qk, safe, sig = fold(
        level_index,
        plan,
        frame_ids,
        freq[None],
        jnp.swapaxes(qkv_weight, 1, 2),
        in_weight,
        cond_gain,
        norm_gain[None],
        qk_gain,
        latents,
    )
    gram = (gram_hi, gram_lo)
    sent, partner = lax.optimization_barrier((sent, partner))
    pay = spread(sent)
    mine = pay[:, PAY - TOK :, :]
    results = []
    for step in range(STEPS):
        other = swapped(mine)
        before = passed_along(mine, 1)
        ready = list(prepared_own(step, pay, mine, gram, qk, partner))
        if step == 0:
            sums, *keys, weights = attend_own(step, safe, pay, mine, other, gram, qk, ready, out_weight)
            queried = ready.pop()
        else:
            sums, *keys, queried = attend_own(step, safe, pay, mine, other, gram, qk, ready, out_weight)
        begun = [sums, queried, *ready, *keys]
        before, *begun = lax.optimization_barrier((before, *begun))
        before_other = swapped(before)
        ready = prepared(step, begun[2], before, gram)
        part, part_other = attend_prev(
            step, safe, pay, before_other, gram, begun, ready, weights, state, in_weight, cond
        )
        got = swapped(part_other)
        estimate, state, *sent = finish(step, sig, state, part, got, final_gain[None], final_weight, fresh_noise)
        results.append(estimate)
        if sent:
            mine = spread(sent[0])
    queue = passed_along(state, -2)
    return leave(results[0], passed_along(results[1], -1), queue)


def solution(mesh):
    split = Mesh(mesh.devices.reshape(8, 4, 2, 2), ("frame", "y", "far", "core"))
    space = ("y", "far", "core")
    in_specs = (
        P("frame", space, None),
        P(None, space, None),
        P(),
        P(),
        P(),
        P(),
        P(),
        P(),
        P(None, None, space),
        P(),
        P(),
        P(),
        P(),
    )
    out_specs = (P(None, "frame", space, None), P("frame", space, None))
    return jax.shard_map(shards, mesh=split, in_specs=in_specs, out_specs=out_specs, check_vma=False)
```

```python
import functools
import math

import jax
import jax.numpy as jnp
import numpy as np
from jax import lax
from jax.experimental import pallas as pl
from jax.experimental.pallas import tpu as pltpu
from jax.sharding import Mesh
from jax.sharding import PartitionSpec as P

HEAD = 64
STEPS = 2
FEAT = 128
WIDE = 256
CHIPS = 8
TOK = 64
COLS = 192
PACK = 48
PAY = 3 * COLS + PACK + TOK
HEADS = CHIPS * 3
GROUPS = HEADS // 4
SIDE = CHIPS * TOK
ONE = 136
EPS = 1e-06
SAFE = 60.0

BF = jnp.bfloat16
F32 = jnp.float32
VMEM = pl.BlockSpec(memory_space=pltpu.VMEM)
SMEM = pl.BlockSpec(memory_space=pltpu.SMEM)
ANY = pl.BlockSpec(memory_space=pl.ANY)


def dot(a, b):
    return jnp.dot(a, b, preferred_element_type=F32)


def dot_t(a, b):
    return lax.dot_general(a, b, (((1,), (1,)), ((), ())), preferred_element_type=F32)


def halves(x):
    high = x.astype(BF)
    return high, (x - high.astype(F32)).astype(BF)


def in_vmem(x):
    return pltpu.with_memory_space_constraint(x, pltpu.VMEM)


def cost(products, bytes_moved=0):
    return pl.CostEstimate(flops=2 * products, transcendentals=0, bytes_accessed=bytes_moved)


def in_hbm(x):
    return pltpu.with_memory_space_constraint(x, pltpu.HBM)


def lanes(shape):
    return lax.broadcasted_iota(jnp.int32, shape, len(shape) - 1)


def rows(shape):
    return lax.broadcasted_iota(jnp.int32, shape, len(shape) - 2)


def slot_of(step):
    count = lax.axis_size("frame")
    return lax.rem(lax.axis_index("frame") + count - step, count)


def fold_kernel(
    level_hbm,
    plan_hbm,
    ids_hbm,
    freq_hbm,
    qkv_hbm,
    in_hbm,
    cond_gain_hbm,
    gain_hbm,
    qk_gain_hbm,
    state_hbm,
    pay_ref,
    gram_hi_ref,
    gram_lo_ref,
    cond_ref,
    qk_ref,
    safe_ref,
    sig_ref,
    level_ref,
    plan_ref,
    ids_ref,
    freq_ref,
    w_ref,
    in_ref,
    cond_gain_ref,
    gain_ref,
    qk_gain_ref,
    state_ref,
    sems,
):
    pairs = (
        (level_hbm, level_ref),
        (plan_hbm, plan_ref),
        (ids_hbm, ids_ref),
        (freq_hbm, freq_ref),
        (in_hbm, in_ref),
        (qkv_hbm, w_ref),
        (cond_gain_hbm, cond_gain_ref),
        (gain_hbm, gain_ref),
        (qk_gain_hbm, qk_gain_ref),
        (state_hbm, state_ref),
    )
    copies = [pltpu.make_async_copy(src, dst, sems.at[i]) for i, (src, dst) in enumerate(pairs)]
    for copy in copies:
        copy.start()
    for i in (0, 1, 2, 3):
        copies[i].wait()

    freq = freq_ref[...]
    row = rows((8, freq.shape[1]))
    angle = jnp.zeros((8, freq.shape[1]), F32)
    for step in range(STEPS):
        slot = slot_of(step)
        before = jnp.maximum(slot - 1, 0)
        stamp_now = plan_ref[level_ref[slot]].astype(F32)
        stamp_prev = plan_ref[level_ref[before]].astype(F32)
        sigma = stamp_now / 1000.0
        sig_ref[2 * step] = sigma
        sig_ref[2 * step + 1] = jnp.where(slot > 0, stamp_prev / 1000.0, 0.0) - sigma
        angle = jnp.where(row == 2 * step, stamp_now, angle)
        angle = jnp.where(row == 2 * step + 1, stamp_prev, angle)
        angle = jnp.where(row == 2 * step + 4, ids_ref[slot + step].astype(F32), angle)
        angle = jnp.where(row == 2 * step + 5, ids_ref[before + step].astype(F32), angle)
    angle = angle * freq
    wave = jnp.concatenate([jnp.cos(angle), jnp.sin(angle)], axis=1)

    for i in (4, 6, 7, 8, 9):
        copies[i].wait()
    product = qk_gain_ref[0:1, :] * qk_gain_ref[1:2, :]
    safe_ref[0] = (HEAD**0.5 * jnp.max(jnp.abs(product)) <= SAFE).astype(jnp.int32)
    product = product * (math.log2(math.e) / math.sqrt(HEAD))
    qk_ref[...] = jnp.concatenate([product] * 4, axis=1)

    cond = cond_gain_ref[0:1, :] * wave[0:4] + cond_gain_ref[1:2, :] * wave[4:8]
    cond = jnp.concatenate([cond, jnp.zeros_like(cond)], axis=0)
    cond_ref[...] = cond

    embed = in_ref[...]
    none = jnp.zeros((112, embed.shape[1]), BF)
    gain = gain_ref[...]
    emb = (embed.astype(F32) * gain).astype(BF)
    cg_hi, cg_lo = halves(cond * gain)
    right = jnp.concatenate([emb, jnp.concatenate([cg_hi, cg_lo], axis=0), none], axis=0)
    copies[5].wait()
    full = dot_t(w_ref[...].reshape(3 * COLS, embed.shape[1]), right)
    mat = full[:, 0:FEAT].astype(BF)
    bias = full[:, FEAT:WIDE]
    bias = bias + pltpu.roll(bias, FEAT - 8, 1)
    lane = lanes(bias.shape)
    bias = jnp.where(lane < 4, bias, 0.0)
    high = bias.astype(BF).astype(F32)
    bias = high + pltpu.roll(bias - high, 4, 1)
    packed = bias[0:PACK]
    for i in range(1, 12):
        packed = packed + pltpu.roll(bias[PACK * i : PACK * (i + 1)], 8 * i, 1)
    packed = packed.astype(BF)
    x = state_ref[0].astype(BF)
    for chip in range(CHIPS):
        pay_ref[chip, 0 : 3 * COLS] = mat
        pay_ref[chip, 3 * COLS : 3 * COLS + PACK] = packed
        pay_ref[chip, PAY - TOK : PAY] = x

    c_hi, c_lo = halves(cond)
    left = jnp.concatenate([embed, jnp.concatenate([c_hi, c_lo], axis=0)], axis=0)
    gram = dot_t(left, jnp.concatenate([left, none], axis=0))
    gram = jnp.concatenate([gram, jnp.zeros((112, WIDE), F32)], axis=0)
    lane, row = lanes(gram.shape), rows(gram.shape)
    gram = jnp.where(lane < FEAT + 8, gram + jnp.where(lane >= FEAT, pltpu.roll(gram, WIDE - 8, 1), 0.0), 0.0)
    gram = jnp.where(row < FEAT + 8, gram + jnp.where(row >= FEAT, pltpu.roll(gram, WIDE - 8, 0), 0.0), 0.0)
    g_hi, g_lo = halves(gram)
    gram_hi_ref[...] = g_hi
    gram_lo_ref[...] = g_lo


def fold(level_index, plan, frame_ids, freq, qkv, in_weight, cond_gain, gain, qk_gain, latents):
    width = in_weight.shape[1]
    args = (level_index, plan, frame_ids, freq, qkv, in_weight, cond_gain, gain, qk_gain, latents)
    return pl.pallas_call(
        fold_kernel,
        out_shape=(
            pltpu.VMEM((CHIPS, PAY, FEAT), BF),
            pltpu.VMEM((WIDE, WIDE), BF),
            pltpu.VMEM((WIDE, WIDE), BF),
            pltpu.VMEM((8, width), F32),
            pltpu.VMEM((1, WIDE), F32),
            jax.ShapeDtypeStruct((1,), jnp.int32),
            jax.ShapeDtypeStruct((2 * STEPS,), F32),
        ),
        in_specs=[ANY] * len(args),
        out_specs=(VMEM,) * 5 + (SMEM,) * 2,
        scratch_shapes=[pltpu.SMEM(v.shape, v.dtype) for v in args[:3]]
        + [pltpu.VMEM(v.shape, v.dtype) for v in args[3:]]
        + [pltpu.SemaphoreType.DMA((len(args),))],
        compiler_params=pltpu.CompilerParams(vmem_limit_bytes=20 * 2**20),
        name="fold",
    )(*[in_hbm(v) for v in args])


def unpack(pay_ref, ref, j):
    lane = lanes((PACK, FEAT))
    for m in range(CHIPS):
        packed = pay_ref[m, 3 * COLS : 3 * COLS + PACK, :].astype(F32)
        ref[m * COLS : (m + 1) * COLS, 0:FEAT] = pay_ref[m, j * COLS : (j + 1) * COLS, :]
        for i in range(4):
            shift = 8 * (4 * j + i)
            part = pltpu.roll(packed, FEAT - shift, 1) if shift else packed
            part = jnp.where(lane < 8, part, 0.0)
            ref[m * COLS + i * PACK : m * COLS + (i + 1) * PACK, FEAT:WIDE] = part.astype(BF)


def prepare(step, group, blocks, gram_hi_ref, gram_lo_ref, ak_ref, xkt_ref, val_ref, rk_ref):
    x = jnp.concatenate([ref[...].reshape(SIDE, FEAT) for ref in blocks], axis=0)
    count = x.shape[0]
    lane = lanes((count, FEAT))
    mark = jnp.logical_or(lane == 2 * step + group, lane == 4 + 2 * step + group)
    xk = jnp.concatenate([x, mark.astype(F32).astype(BF)], axis=1)
    row = rows((FEAT, count))
    mark = jnp.logical_or(row == 2 * step + group, row == 4 + 2 * step + group)
    xkt_ref[0:FEAT, :] = jnp.transpose(x)
    xkt_ref[FEAT:WIDE, :] = mark.astype(F32).astype(BF)
    xkt = xkt_ref[...]
    square = dot(gram_hi_ref[...], xkt) + dot(gram_lo_ref[...], xkt)
    m_row = jnp.sum(square * xkt.astype(F32), axis=0, keepdims=True) * (1.0 / 3072.0) + EPS
    r_col = jnp.transpose(jnp.broadcast_to(lax.rsqrt(m_row), (8, count)))[:, 0:1]
    val = jnp.where(lanes((count, WIDE)) == ONE, 1.0, xk.astype(F32) * r_col)
    if group == 1:
        val = jnp.where(slot_of(step) == 0, 0.0, val)
    val_ref[...] = val.astype(BF)
    for g in range(GROUPS):
        u = dot(ak_ref[g * WIDE : (g + 1) * WIDE, :], xkt_ref[...])
        u = jnp.sum((u * u).reshape(4, HEAD, count), axis=1)
        rk = lax.rsqrt(u * (1.0 / HEAD) + EPS * m_row)
        rk_ref[g] = jnp.concatenate([rk, rk], axis=0)


def queries(step, tokens, pay_ref, gram_hi_ref, gram_lo_ref, qk_ref, aq_ref, ak_ref, qc_ref):
    unpack(pay_ref, aq_ref, 0)
    xq = jnp.concatenate(tokens, axis=0)
    row = rows((FEAT, 2 * TOK))
    mark = jnp.logical_or(row == 2 * step, row == 4 + 2 * step)
    xqt = jnp.concatenate([jnp.transpose(xq), mark.astype(F32).astype(BF)], axis=0)
    square = dot(gram_hi_ref[...], xqt) + dot(gram_lo_ref[...], xqt)
    m_q = jnp.sum(square * xqt.astype(F32), axis=0, keepdims=True) * (1.0 / 3072.0) + EPS
    head_of = lanes((2 * TOK, WIDE)) // HEAD

    q = dot(aq_ref[...], xqt).reshape(HEADS, HEAD, 2 * TOK)
    q = q * lax.rsqrt(jnp.sum(q * q, axis=1, keepdims=True) * (1.0 / HEAD) + EPS * m_q[None])
    q = q.reshape(HEADS * HEAD, 2 * TOK)
    for g in range(GROUPS):
        span = slice(g * WIDE, (g + 1) * WIDE)
        some = jnp.transpose(q[span]) * qk_ref[...]
        some = jnp.concatenate([jnp.where(head_of == h, some, 0.0) for h in range(4)], axis=0)
        qc_ref[g] = dot(some.astype(BF), ak_ref[span, :]).astype(BF)


def prepare_own_kernel(step, *refs):
    refs = list(refs)
    pay_ref, block_ref, gram_hi_ref, gram_lo_ref = refs[:4]
    del refs[:4]
    if step == 0:
        qk_ref, partner_ref, qc_ref, aq_ref = refs.pop(0), refs.pop(0), refs.pop(4), refs.pop()
    ak_ref, xkt_ref, val_ref, rk_ref = refs
    unpack(pay_ref, ak_ref, 1)
    prepare(step, 0, (block_ref,), gram_hi_ref, gram_lo_ref, ak_ref, xkt_ref, val_ref, rk_ref)
    if step == 0:
        chip = lax.axis_index(("y", "far"))
        tokens = (block_ref[chip], partner_ref[...].astype(BF))
        queries(step, tokens, pay_ref, gram_hi_ref, gram_lo_ref, qk_ref, aq_ref, ak_ref, qc_ref)


def prepared_own(step, pay, block, gram, qk, partner):
    half = HEADS * HEAD
    held = [in_vmem(v) for v in (pay, block, *gram)]
    shapes = [pltpu.VMEM((half, WIDE), BF)] + side_shapes(SIDE)
    scratch = []
    if step == 0:
        held += [in_vmem(qk), in_vmem(partner)]
        shapes.append(pltpu.VMEM((GROUPS, 8 * TOK, WIDE), BF))
        scratch.append(pltpu.VMEM((half, WIDE), BF))
    return pl.pallas_call(
        functools.partial(prepare_own_kernel, step),
        out_shape=shapes,
        in_specs=[VMEM] * len(held),
        out_specs=[VMEM] * len(shapes),
        scratch_shapes=scratch,
        compiler_params=pltpu.CompilerParams(vmem_limit_bytes=12 * 2**20),
        cost_estimate=cost(HEADS * HEAD * WIDE * SIDE, 2 * CHIPS * PAY * FEAT),
        name="prepare_own",
    )(*held)


def prepare_kernel(
    step,
    ak_ref,
    block_ref,
    gram_hi_ref,
    gram_lo_ref,
    pay_ref,
    state_ref,
    in_ref,
    cond_ref,
    xkt_ref,
    val_ref,
    rk_ref,
    av_ref,
    hidden_ref,
):
    prepare(step, 1, (block_ref,), gram_hi_ref, gram_lo_ref, ak_ref, xkt_ref, val_ref, rk_ref)
    unpack(pay_ref, av_ref, 2)
    hidden_ref[...] = dot(state_ref[...].astype(BF), in_ref[...]) + cond_ref[2 * step : 2 * step + 1, :]


def side_shapes(count):
    return [
        pltpu.VMEM((WIDE, count), BF),
        pltpu.VMEM((count, WIDE), BF),
        pltpu.VMEM((GROUPS, 8, count), F32),
    ]


def prepared(step, ak, block, gram, pay, state, in_weight, cond):
    held = [in_vmem(v) for v in (ak, block, *gram, pay, state, in_weight, cond)]
    shapes = side_shapes(SIDE)
    shapes += [pltpu.VMEM((HEADS * HEAD, WIDE), BF), pltpu.VMEM((TOK, in_weight.shape[1]), F32)]
    return pl.pallas_call(
        functools.partial(prepare_kernel, step),
        out_shape=shapes,
        in_specs=[VMEM] * len(held),
        out_specs=[VMEM] * len(shapes),
        compiler_params=pltpu.CompilerParams(vmem_limit_bytes=10 * 2**20),
        cost_estimate=cost(HEADS * HEAD * WIDE * SIDE),
        name="prepare",
    )(*held)


def columns(sides):
    begin = 0
    for side in sides:
        count = side[0].shape[1]
        yield side, slice(begin, begin + count)
        begin += count


def weigh(g, qc_ref, sides, p_ref):
    for h in range(4):
        span = slice(2 * TOK * h, 2 * TOK * (h + 1))
        for (xkt_ref, _, rk_ref), keys in columns(sides):
            s = dot(qc_ref[g, span], xkt_ref[...]) * rk_ref[g, h : h + 1, :]
            p_ref[span, keys] = jnp.exp2(s).astype(BF)


def collect(g, h, sides, p_ref):
    span = slice(2 * TOK * h, 2 * TOK * (h + 1))
    parts = [dot(p_ref[span, keys], val_ref[...]) for (_, val_ref, _), keys in columns(sides)]
    return sum(parts[1:], parts[0])


def own_kernel(step, *refs):
    refs = list(refs)
    safe_ref, other_ref, gram_hi_ref, gram_lo_ref, ak_ref = refs[:5]
    sides = (refs[5:8],)
    del refs[:8]
    copies = []
    if step == 0:
        qc_ref, out_w_ref, w_ref, sem = refs.pop(0), refs.pop(0), refs.pop(4), refs.pop()
        core = lax.axis_index("core")
        for m in range(CHIPS):
            begin = pl.multiple_of((2 * m + core) * COLS, COLS)
            copies.append(
                pltpu.make_async_copy(out_w_ref.at[pl.ds(begin, COLS)], w_ref.at[pl.ds(m * COLS, COLS)], sem)
            )
        for copy in copies:
            copy.start()
    else:
        pay_ref, mine_ref, qk_ref, qc_ref, aq_ref = refs.pop(0), refs.pop(0), refs.pop(0), refs.pop(4), refs.pop()
    sum_ref, p_ref = refs.pop(0), refs.pop()
    sides += (tuple(refs),)
    prepare(step, 0, (other_ref,), gram_hi_ref, gram_lo_ref, ak_ref, *sides[1])
    if step > 0:
        chip = lax.axis_index(("y", "far"))
        tokens = (mine_ref[chip], other_ref[chip])
        queries(step, tokens, pay_ref, gram_hi_ref, gram_lo_ref, qk_ref, aq_ref, ak_ref, qc_ref)

    @pl.when(safe_ref[0] == 1)
    def _():
        def body(i, carry):
            for k in range(3):
                g = 3 * i + k
                weigh(g, qc_ref, sides, p_ref)
                for h in range(4):
                    sum_ref[g, 2 * TOK * h : 2 * TOK * (h + 1)] = collect(g, h, sides, p_ref)
            return carry

        lax.fori_loop(0, GROUPS // 3, body, 0)

    for copy in copies:
        copy.wait()


def attend_own(step, safe, pay, mine, other, gram, qk, ready, out_weight):
    group = (GROUPS, 8 * TOK, WIDE)
    half = HEADS * HEAD
    held = [in_vmem(v) for v in (other, *gram, *ready)]
    shapes = [pltpu.VMEM(group, F32)] + side_shapes(SIDE)
    scratch = [pltpu.VMEM((8 * TOK, 2 * SIDE), BF)]
    if step == 0:
        held.append(in_hbm(out_weight))
        shapes.append(pltpu.VMEM((half, out_weight.shape[1]), BF))
        scratch.append(pltpu.SemaphoreType.DMA)
    else:
        held += [in_vmem(v) for v in (pay, mine, qk)]
        shapes.append(pltpu.VMEM(group, BF))
        scratch.append(pltpu.VMEM((half, WIDE), BF))
    return pl.pallas_call(
        functools.partial(own_kernel, step),
        out_shape=shapes,
        in_specs=[SMEM] + [VMEM] * (len(held) - 1) + [ANY if step == 0 else VMEM],
        out_specs=[VMEM] * len(shapes),
        scratch_shapes=scratch,
        compiler_params=pltpu.CompilerParams(vmem_limit_bytes=14 * 2**20),
        cost_estimate=cost(HEADS * 2 * TOK * WIDE * 4 * SIDE),
        name="attend_own",
    )(safe, *held)


def prev_kernel(
    step,
    safe_ref,
    other_ref,
    gram_hi_ref,
    gram_lo_ref,
    sum_ref,
    qc_ref,
    ak_ref,
    xkt_a_ref,
    val_a_ref,
    rk_a_ref,
    xkt_b_ref,
    val_b_ref,
    rk_b_ref,
    xkt_c_ref,
    val_c_ref,
    rk_c_ref,
    av_ref,
    hidden_ref,
    w_ref,
    part_ref,
    part_other_ref,
    xkt_d_ref,
    val_d_ref,
    rk_d_ref,
    p_ref,
    s_ref,
    z_ref,
):
    own = ((xkt_a_ref, val_a_ref, rk_a_ref), (xkt_b_ref, val_b_ref, rk_b_ref))
    prev = ((xkt_c_ref, val_c_ref, rk_c_ref), (xkt_d_ref, val_d_ref, rk_d_ref))
    prepare(step, 1, (other_ref,), gram_hi_ref, gram_lo_ref, ak_ref, *prev[1])

    def settle(g, h, z):
        z_ref[g, 2 * TOK * h : 2 * TOK * (h + 1)] = (z * (1.0 / z[:, ONE : ONE + 1])).astype(BF)

    @pl.when(safe_ref[0] == 1)
    def _():
        def body(i, carry):
            for k in range(3):
                g = 3 * i + k
                weigh(g, qc_ref, prev, p_ref)
                for h in range(4):
                    settle(g, h, collect(g, h, prev, p_ref) + sum_ref[g, 2 * TOK * h : 2 * TOK * (h + 1)])
            return carry

        lax.fori_loop(0, GROUPS // 3, body, 0)

    @pl.when(safe_ref[0] != 1)
    def _():
        every = own + prev
        alone = slot_of(step) == 0

        def body(g, carry):
            for h in range(4):
                span = slice(2 * TOK * h, 2 * TOK * (h + 1))
                for (xkt_ref, _, rk_ref), keys in columns(every):
                    s = dot(qc_ref[g, span], xkt_ref[...]) * rk_ref[g, h : h + 1, :]
                    s_ref[:, keys] = jnp.where(alone, -1e30, s) if keys.start >= 2 * SIDE else s
                s = s_ref[...]
                p_ref[span, :] = jnp.exp2(s - jnp.max(s, axis=1, keepdims=True)).astype(BF)
                settle(g, h, collect(g, h, every, p_ref))
            return carry

        lax.fori_loop(0, GROUPS, body, 0)

    head_of = lanes((2 * TOK, WIDE)) // HEAD
    outs = []
    for g in range(GROUPS):
        o = dot_t(z_ref[g], av_ref[g * WIDE : (g + 1) * WIDE, :])
        picked = jnp.where(head_of == 0, o[0:128], 0.0)
        for h in range(1, 4):
            picked = jnp.where(head_of == h, o[128 * h : 128 * (h + 1)], picked)
        outs.append(picked.astype(BF))
    y = dot(jnp.concatenate(outs, axis=1), w_ref[...])
    part_ref[...] = hidden_ref[...] + y[0:TOK]
    part_other_ref[...] = y[TOK:].astype(BF)


def attend_prev(step, safe, other, gram, begun, ready, weights):
    width = weights.shape[1]
    held = [in_vmem(v) for v in (other, *gram, *begun, *ready, weights)]
    return pl.pallas_call(
        functools.partial(prev_kernel, step),
        out_shape=(pltpu.VMEM((TOK, width), F32), pltpu.VMEM((TOK, width), BF)),
        in_specs=[SMEM] + [VMEM] * len(held),
        out_specs=(VMEM, VMEM),
        scratch_shapes=side_shapes(SIDE)
        + [
            pltpu.VMEM((8 * TOK, 4 * SIDE), BF),
            pltpu.VMEM((2 * TOK, 4 * SIDE), F32),
            pltpu.VMEM((GROUPS, 8 * TOK, WIDE), BF),
        ],
        compiler_params=pltpu.CompilerParams(vmem_limit_bytes=16 * 2**20),
        cost_estimate=cost(HEADS * 2 * TOK * WIDE * 4 * SIDE),
        name="attend_prev",
    )(safe, *held)


def finish_kernel(step, sig_ref, state_ref, part_ref, got_ref, gain_ref, final_ref, fresh_ref, est_ref, new_ref, *sent):
    state = state_ref[...]
    y = part_ref[...] + got_ref[...].astype(F32)
    scale = lax.rsqrt(jnp.mean(y * y, axis=1, keepdims=True) + EPS)
    velocity = dot((y * scale * gain_ref[...]).astype(BF), final_ref[...])
    est_ref[...] = state - sig_ref[2 * step] * velocity
    new = jnp.where(slot_of(step) == 0, fresh_ref[step], state + sig_ref[2 * step + 1] * velocity)
    new_ref[...] = new
    for sent_ref in sent:
        for chip in range(CHIPS):
            sent_ref[chip] = new.astype(BF)


def finish(step, sig, state, part, got, gain, final_weight, fresh):
    out = jax.ShapeDtypeStruct(state.shape, F32)
    shapes = [out, out]
    if step + 1 < STEPS:
        shapes.append(pltpu.VMEM((CHIPS,) + state.shape, BF))
    return pl.pallas_call(
        functools.partial(finish_kernel, step),
        out_shape=shapes,
        in_specs=[SMEM] + [VMEM] * 6,
        out_specs=[VMEM] * len(shapes),
        compiler_params=pltpu.CompilerParams(vmem_limit_bytes=12 * 2**20),
        name="finish",
    )(sig, *[in_vmem(v) for v in (state, part, got, gain, final_weight, fresh)])


def leave_kernel(queue_ref, second_ref, first_ref, est_ref, out_ref, sems):
    pairs = ((first_ref, est_ref.at[0, 0]), (second_ref, est_ref.at[1, 0]), (queue_ref, out_ref.at[0]))
    copies = [pltpu.make_async_copy(src, dst, sems.at[i]) for i, (src, dst) in enumerate(pairs)]
    for copy in copies:
        copy.start()
    for copy in copies:
        copy.wait()


def leave(first, second, queue):
    return pl.pallas_call(
        leave_kernel,
        out_shape=(
            jax.ShapeDtypeStruct((STEPS, 1) + first.shape, F32),
            jax.ShapeDtypeStruct((1,) + queue.shape, F32),
        ),
        in_specs=[VMEM] * 3,
        out_specs=(ANY, ANY),
        scratch_shapes=[pltpu.SemaphoreType.DMA((3,))],
        name="leave",
    )(in_vmem(queue), in_vmem(second), in_vmem(first))


def passed_along(x, by):
    peers = lax.axis_size("frame")
    return lax.ppermute(x, "frame", [(i, (i + by) % peers) for i in range(peers)])


def swapped(x):
    return lax.ppermute(x, "core", [(0, 1), (1, 0)])


def spread(x):
    return lax.all_to_all(x, ("y", "far"), 0, 0, tiled=True)


def shards(
    latents,
    fresh_noise,
    level_index,
    plan,
    frame_ids,
    in_weight,
    cond_gain,
    norm_gain,
    qkv_weight,
    qk_gain,
    out_weight,
    final_gain,
    final_weight,
):
    half = in_weight.shape[1] // 2
    freq = jnp.asarray(np.exp(-math.log(10000.0) * np.arange(half, dtype=np.float32) / half), F32)
    state = latents[0]
    partner = swapped(state)
    sent, gram_hi, gram_lo, cond, qk, safe, sig = fold(
        level_index,
        plan,
        frame_ids,
        freq[None],
        jnp.swapaxes(qkv_weight, 1, 2),
        in_weight,
        cond_gain,
        norm_gain[None],
        qk_gain,
        latents,
    )
    gram = (gram_hi, gram_lo)
    sent, partner = lax.optimization_barrier((sent, partner))
    pay = spread(sent)
    mine = pay[:, PAY - TOK :, :]
    results = []
    for step in range(STEPS):
        other = swapped(mine)
        before = passed_along(mine, 1)
        ready = list(prepared_own(step, pay, mine, gram, qk, partner))
        if step == 0:
            sums, *keys, weights = attend_own(step, safe, pay, mine, other, gram, qk, ready, out_weight)
            queried = ready.pop()
        else:
            sums, *keys, queried = attend_own(step, safe, pay, mine, other, gram, qk, ready, out_weight)
        begun = [sums, queried, *ready, *keys]
        before, *begun = lax.optimization_barrier((before, *begun))
        before_other = swapped(before)
        ready = prepared(step, begun[2], before, gram, pay, state, in_weight, cond)
        part, part_other = attend_prev(step, safe, before_other, gram, begun, ready, weights)
        got = swapped(part_other)
        estimate, state, *sent = finish(step, sig, state, part, got, final_gain[None], final_weight, fresh_noise)
        results.append(estimate)
        if sent:
            mine = spread(sent[0])
    queue = passed_along(state, -2)
    return leave(results[0], passed_along(results[1], -1), queue)


def solution(mesh):
    split = Mesh(mesh.devices.reshape(8, 4, 2, 2), ("frame", "y", "far", "core"))
    space = ("y", "far", "core")
    in_specs = (
        P("frame", space, None),
        P(None, space, None),
        P(),
        P(),
        P(),
        P(),
        P(),
        P(),
        P(None, None, space),
        P(),
        P(),
        P(),
        P(),
    )
    out_specs = (P(None, "frame", space, None), P("frame", space, None))
    return jax.shard_map(shards, mesh=split, in_specs=in_specs, out_specs=out_specs, check_vma=False)
```

```python
import functools
import math

import jax
import jax.numpy as jnp
import numpy as np
from jax import lax
from jax.experimental import pallas as pl
from jax.experimental.pallas import tpu as pltpu
from jax.sharding import Mesh
from jax.sharding import PartitionSpec as P

HEAD = 64
STEPS = 2
FEAT = 128
WIDE = 256
CHIPS = 8
TOK = 64
COLS = 192
PACK = 48
PAY = 3 * COLS + PACK + TOK
HEADS = CHIPS * 3
GROUPS = HEADS // 4
SIDE = CHIPS * TOK
ONE = 136
EPS = 1e-06
SAFE = 60.0

BF = jnp.bfloat16
F32 = jnp.float32
VMEM = pl.BlockSpec(memory_space=pltpu.VMEM)
SMEM = pl.BlockSpec(memory_space=pltpu.SMEM)
ANY = pl.BlockSpec(memory_space=pl.ANY)


def dot(a, b):
    return jnp.dot(a, b, preferred_element_type=F32)


def dot_t(a, b):
    return lax.dot_general(a, b, (((1,), (1,)), ((), ())), preferred_element_type=F32)


def halves(x):
    high = x.astype(BF)
    return high, (x - high.astype(F32)).astype(BF)


def stacked_halves(x):
    high = x.astype(BF).astype(F32)
    return jnp.concatenate([high, x - high], axis=0).astype(BF)


def in_vmem(x):
    return pltpu.with_memory_space_constraint(x, pltpu.VMEM)


def cost(products, bytes_moved=0):
    return pl.CostEstimate(flops=2 * products, transcendentals=0, bytes_accessed=bytes_moved)


def in_hbm(x):
    return pltpu.with_memory_space_constraint(x, pltpu.HBM)


def lanes(shape):
    return lax.broadcasted_iota(jnp.int32, shape, len(shape) - 1)


def rows(shape):
    return lax.broadcasted_iota(jnp.int32, shape, len(shape) - 2)


def slot_of(step):
    count = lax.axis_size("frame")
    return lax.rem(lax.axis_index("frame") + count - step, count)


def fold_kernel(
    level_hbm,
    plan_hbm,
    ids_hbm,
    freq_hbm,
    qkv_hbm,
    in_hbm,
    cond_gain_hbm,
    gain_hbm,
    qk_gain_hbm,
    state_hbm,
    pay_ref,
    gram_hi_ref,
    gram_lo_ref,
    cond_ref,
    qk_ref,
    safe_ref,
    sig_ref,
    level_ref,
    plan_ref,
    ids_ref,
    freq_ref,
    w_ref,
    in_ref,
    cond_gain_ref,
    gain_ref,
    qk_gain_ref,
    state_ref,
    sems,
):
    pairs = (
        (level_hbm, level_ref),
        (plan_hbm, plan_ref),
        (ids_hbm, ids_ref),
        (freq_hbm, freq_ref),
        (in_hbm, in_ref),
        (qkv_hbm, w_ref),
        (cond_gain_hbm, cond_gain_ref),
        (gain_hbm, gain_ref),
        (qk_gain_hbm, qk_gain_ref),
        (state_hbm, state_ref),
    )
    copies = [pltpu.make_async_copy(src, dst, sems.at[i]) for i, (src, dst) in enumerate(pairs)]
    for copy in copies:
        copy.start()
    for i in (0, 1, 2, 3):
        copies[i].wait()

    freq = freq_ref[...]
    row = rows((8, freq.shape[1]))
    angle = jnp.zeros((8, freq.shape[1]), F32)
    for step in range(STEPS):
        slot = slot_of(step)
        before = jnp.maximum(slot - 1, 0)
        stamp_now = plan_ref[level_ref[slot]].astype(F32)
        stamp_prev = plan_ref[level_ref[before]].astype(F32)
        sigma = stamp_now / 1000.0
        sig_ref[2 * step] = sigma
        sig_ref[2 * step + 1] = jnp.where(slot > 0, stamp_prev / 1000.0, 0.0) - sigma
        angle = jnp.where(row == 2 * step, stamp_now, angle)
        angle = jnp.where(row == 2 * step + 1, stamp_prev, angle)
        angle = jnp.where(row == 2 * step + 4, ids_ref[slot + step].astype(F32), angle)
        angle = jnp.where(row == 2 * step + 5, ids_ref[before + step].astype(F32), angle)
    angle = angle * freq
    wave = jnp.concatenate([jnp.cos(angle), jnp.sin(angle)], axis=1)

    for i in (4, 6, 7, 8, 9):
        copies[i].wait()
    product = qk_gain_ref[0:1, :] * qk_gain_ref[1:2, :]
    safe_ref[0] = (HEAD**0.5 * jnp.max(jnp.abs(product)) <= SAFE).astype(jnp.int32)
    product = product * (math.log2(math.e) / math.sqrt(HEAD))
    qk_ref[...] = jnp.concatenate([product] * 4, axis=1)

    cond = cond_gain_ref[0:1, :] * wave[0:4] + cond_gain_ref[1:2, :] * wave[4:8]
    cond = jnp.concatenate([cond, jnp.zeros_like(cond)], axis=0)
    cond_ref[...] = cond

    embed = in_ref[...]
    none = jnp.zeros((112, embed.shape[1]), BF)
    gain = gain_ref[...]
    emb = (embed.astype(F32) * gain).astype(BF)
    right = jnp.concatenate([emb, stacked_halves(cond * gain), none], axis=0)
    copies[5].wait()
    full = dot_t(w_ref[...].reshape(3 * COLS, embed.shape[1]), right)
    mat = full[:, 0:FEAT].astype(BF)
    bias = full[:, FEAT:WIDE]
    bias = bias + pltpu.roll(bias, FEAT - 8, 1)
    lane = lanes(bias.shape)
    bias = jnp.where(lane < 4, bias, 0.0)
    high = bias.astype(BF).astype(F32)
    bias = high + pltpu.roll(bias - high, 4, 1)
    packed = bias[0:PACK]
    for i in range(1, 12):
        packed = packed + pltpu.roll(bias[PACK * i : PACK * (i + 1)], 8 * i, 1)
    packed = packed.astype(BF)
    x = state_ref[0].astype(BF)
    for chip in range(CHIPS):
        pay_ref[chip, 0 : 3 * COLS] = mat
        pay_ref[chip, 3 * COLS : 3 * COLS + PACK] = packed
        pay_ref[chip, PAY - TOK : PAY] = x

    left = jnp.concatenate([embed, stacked_halves(cond)], axis=0)
    gram = dot_t(left, jnp.concatenate([left, none], axis=0))
    gram = jnp.concatenate([gram, jnp.zeros((112, WIDE), F32)], axis=0)
    lane, row = lanes(gram.shape), rows(gram.shape)
    gram = jnp.where(lane < FEAT + 8, gram + jnp.where(lane >= FEAT, pltpu.roll(gram, WIDE - 8, 1), 0.0), 0.0)
    gram = jnp.where(row < FEAT + 8, gram + jnp.where(row >= FEAT, pltpu.roll(gram, WIDE - 8, 0), 0.0), 0.0)
    g_hi, g_lo = halves(gram)
    gram_hi_ref[...] = g_hi
    gram_lo_ref[...] = g_lo


def fold(level_index, plan, frame_ids, freq, qkv, in_weight, cond_gain, gain, qk_gain, latents):
    width = in_weight.shape[1]
    args = (level_index, plan, frame_ids, freq, qkv, in_weight, cond_gain, gain, qk_gain, latents)
    return pl.pallas_call(
        fold_kernel,
        out_shape=(
            pltpu.VMEM((CHIPS, PAY, FEAT), BF),
            pltpu.VMEM((WIDE, WIDE), BF),
            pltpu.VMEM((WIDE, WIDE), BF),
            pltpu.VMEM((8, width), F32),
            pltpu.VMEM((1, WIDE), F32),
            jax.ShapeDtypeStruct((1,), jnp.int32),
            jax.ShapeDtypeStruct((2 * STEPS,), F32),
        ),
        in_specs=[ANY] * len(args),
        out_specs=(VMEM,) * 5 + (SMEM,) * 2,
        scratch_shapes=[pltpu.SMEM(v.shape, v.dtype) for v in args[:3]]
        + [pltpu.VMEM(v.shape, v.dtype) for v in args[3:]]
        + [pltpu.SemaphoreType.DMA((len(args),))],
        compiler_params=pltpu.CompilerParams(vmem_limit_bytes=20 * 2**20),
        name="fold",
    )(*[in_hbm(v) for v in args])


def unpack(pay_ref, ref, j):
    lane = lanes((PACK, FEAT))
    for m in range(CHIPS):
        packed = pay_ref[m, 3 * COLS : 3 * COLS + PACK, :].astype(F32)
        ref[m * COLS : (m + 1) * COLS, 0:FEAT] = pay_ref[m, j * COLS : (j + 1) * COLS, :]
        for i in range(4):
            shift = 8 * (4 * j + i)
            part = pltpu.roll(packed, FEAT - shift, 1) if shift else packed
            part = jnp.where(lane < 8, part, 0.0)
            ref[m * COLS + i * PACK : m * COLS + (i + 1) * PACK, FEAT:WIDE] = part.astype(BF)


def prepare(step, group, blocks, gram_hi_ref, gram_lo_ref, ak_ref, xkt_ref, val_ref, rk_ref):
    x = jnp.concatenate([ref[...].reshape(SIDE, FEAT) for ref in blocks], axis=0)
    count = x.shape[0]
    lane = lanes((count, FEAT))
    mark = jnp.logical_or(lane == 2 * step + group, lane == 4 + 2 * step + group)
    xk = jnp.concatenate([x, mark.astype(F32).astype(BF)], axis=1)
    row = rows((FEAT, count))
    mark = jnp.logical_or(row == 2 * step + group, row == 4 + 2 * step + group)
    xkt_ref[0:FEAT, :] = jnp.transpose(x)
    xkt_ref[FEAT:WIDE, :] = mark.astype(F32).astype(BF)
    xkt = xkt_ref[...]
    square = dot(gram_hi_ref[...], xkt) + dot(gram_lo_ref[...], xkt)
    m_row = jnp.sum(square * xkt.astype(F32), axis=0, keepdims=True) * (1.0 / 3072.0) + EPS
    r_col = jnp.transpose(jnp.broadcast_to(lax.rsqrt(m_row), (8, count)))[:, 0:1]
    val = jnp.where(lanes((count, WIDE)) == ONE, 1.0, xk.astype(F32) * r_col)
    if group == 1:
        val = jnp.where(slot_of(step) == 0, 0.0, val)
    val_ref[...] = val.astype(BF)
    for g in range(GROUPS):
        u = dot(ak_ref[g * WIDE : (g + 1) * WIDE, :], xkt_ref[...])
        u = jnp.sum((u * u).reshape(4, HEAD, count), axis=1)
        rk = lax.rsqrt(u * (1.0 / HEAD) + EPS * m_row)
        rk_ref[g] = jnp.concatenate([rk, rk], axis=0)


def queries(step, tokens, pay_ref, gram_hi_ref, gram_lo_ref, qk_ref, aq_ref, ak_ref, qc_ref):
    unpack(pay_ref, aq_ref, 0)
    xq = jnp.concatenate(tokens, axis=0)
    row = rows((FEAT, 2 * TOK))
    mark = jnp.logical_or(row == 2 * step, row == 4 + 2 * step)
    xqt = jnp.concatenate([jnp.transpose(xq), mark.astype(F32).astype(BF)], axis=0)
    square = dot(gram_hi_ref[...], xqt) + dot(gram_lo_ref[...], xqt)
    m_q = jnp.sum(square * xqt.astype(F32), axis=0, keepdims=True) * (1.0 / 3072.0) + EPS
    head_of = lanes((2 * TOK, WIDE)) // HEAD

    q = dot(aq_ref[...], xqt).reshape(HEADS, HEAD, 2 * TOK)
    q = q * lax.rsqrt(jnp.sum(q * q, axis=1, keepdims=True) * (1.0 / HEAD) + EPS * m_q[None])
    q = q.reshape(HEADS * HEAD, 2 * TOK)
    for g in range(GROUPS):
        span = slice(g * WIDE, (g + 1) * WIDE)
        some = jnp.transpose(q[span]) * qk_ref[...]
        some = jnp.concatenate([jnp.where(head_of == h, some, 0.0) for h in range(4)], axis=0)
        qc_ref[g] = dot(some.astype(BF), ak_ref[span, :]).astype(BF)


def prepare_own_kernel(step, *refs):
    refs = list(refs)
    pay_ref, block_ref, gram_hi_ref, gram_lo_ref = refs[:4]
    del refs[:4]
    if step == 0:
        qk_ref, partner_ref, qc_ref, aq_ref = refs.pop(0), refs.pop(0), refs.pop(4), refs.pop()
    ak_ref, xkt_ref, val_ref, rk_ref = refs
    unpack(pay_ref, ak_ref, 1)
    prepare(step, 0, (block_ref,), gram_hi_ref, gram_lo_ref, ak_ref, xkt_ref, val_ref, rk_ref)
    if step == 0:
        chip = lax.axis_index(("y", "far"))
        tokens = (block_ref[chip], partner_ref[...].astype(BF))
        queries(step, tokens, pay_ref, gram_hi_ref, gram_lo_ref, qk_ref, aq_ref, ak_ref, qc_ref)


def prepared_own(step, pay, block, gram, qk, partner):
    half = HEADS * HEAD
    held = [in_vmem(v) for v in (pay, block, *gram)]
    shapes = [pltpu.VMEM((half, WIDE), BF)] + side_shapes(SIDE)
    scratch = []
    if step == 0:
        held += [in_vmem(qk), in_vmem(partner)]
        shapes.append(pltpu.VMEM((GROUPS, 8 * TOK, WIDE), BF))
        scratch.append(pltpu.VMEM((half, WIDE), BF))
    return pl.pallas_call(
        functools.partial(prepare_own_kernel, step),
        out_shape=shapes,
        in_specs=[VMEM] * len(held),
        out_specs=[VMEM] * len(shapes),
        scratch_shapes=scratch,
        compiler_params=pltpu.CompilerParams(vmem_limit_bytes=12 * 2**20),
        cost_estimate=cost(HEADS * HEAD * WIDE * SIDE, 2 * CHIPS * PAY * FEAT),
        name="prepare_own",
    )(*held)


def prepare_kernel(
    step,
    ak_ref,
    block_ref,
    gram_hi_ref,
    gram_lo_ref,
    pay_ref,
    state_ref,
    in_ref,
    cond_ref,
    xkt_ref,
    val_ref,
    rk_ref,
    av_ref,
    hidden_ref,
):
    prepare(step, 1, (block_ref,), gram_hi_ref, gram_lo_ref, ak_ref, xkt_ref, val_ref, rk_ref)
    unpack(pay_ref, av_ref, 2)
    hidden_ref[...] = dot(state_ref[...].astype(BF), in_ref[...]) + cond_ref[2 * step : 2 * step + 1, :]


def side_shapes(count):
    return [
        pltpu.VMEM((WIDE, count), BF),
        pltpu.VMEM((count, WIDE), BF),
        pltpu.VMEM((GROUPS, 8, count), F32),
    ]


def prepared(step, ak, block, gram, pay, state, in_weight, cond):
    held = [in_vmem(v) for v in (ak, block, *gram, pay, state, in_weight, cond)]
    shapes = side_shapes(SIDE)
    shapes += [pltpu.VMEM((HEADS * HEAD, WIDE), BF), pltpu.VMEM((TOK, in_weight.shape[1]), F32)]
    return pl.pallas_call(
        functools.partial(prepare_kernel, step),
        out_shape=shapes,
        in_specs=[VMEM] * len(held),
        out_specs=[VMEM] * len(shapes),
        compiler_params=pltpu.CompilerParams(vmem_limit_bytes=10 * 2**20),
        cost_estimate=cost(HEADS * HEAD * WIDE * SIDE),
        name="prepare",
    )(*held)


def columns(sides):
    begin = 0
    for side in sides:
        count = side[0].shape[1]
        yield side, slice(begin, begin + count)
        begin += count


def weigh(g, qc_ref, sides, p_ref):
    for h in range(4):
        span = slice(2 * TOK * h, 2 * TOK * (h + 1))
        for (xkt_ref, _, rk_ref), keys in columns(sides):
            s = dot(qc_ref[g, span], xkt_ref[...]) * rk_ref[g, h : h + 1, :]
            p_ref[span, keys] = jnp.exp2(s).astype(BF)


def collect(g, h, sides, p_ref):
    span = slice(2 * TOK * h, 2 * TOK * (h + 1))
    parts = [dot(p_ref[span, keys], val_ref[...]) for (_, val_ref, _), keys in columns(sides)]
    return sum(parts[1:], parts[0])


def own_kernel(step, *refs):
    refs = list(refs)
    safe_ref, other_ref, gram_hi_ref, gram_lo_ref, ak_ref = refs[:5]
    sides = (refs[5:8],)
    del refs[:8]
    copies = []
    if step == 0:
        qc_ref, out_w_ref, w_ref, sem = refs.pop(0), refs.pop(0), refs.pop(4), refs.pop()
        core = lax.axis_index("core")
        for m in range(CHIPS):
            begin = pl.multiple_of((2 * m + core) * COLS, COLS)
            copies.append(
                pltpu.make_async_copy(out_w_ref.at[pl.ds(begin, COLS)], w_ref.at[pl.ds(m * COLS, COLS)], sem)
            )
        for copy in copies:
            copy.start()
    else:
        pay_ref, mine_ref, qk_ref, qc_ref, aq_ref = refs.pop(0), refs.pop(0), refs.pop(0), refs.pop(4), refs.pop()
    sum_ref, p_ref = refs.pop(0), refs.pop()
    sides += (tuple(refs),)
    prepare(step, 0, (other_ref,), gram_hi_ref, gram_lo_ref, ak_ref, *sides[1])
    if step > 0:
        chip = lax.axis_index(("y", "far"))
        tokens = (mine_ref[chip], other_ref[chip])
        queries(step, tokens, pay_ref, gram_hi_ref, gram_lo_ref, qk_ref, aq_ref, ak_ref, qc_ref)

    @pl.when(safe_ref[0] == 1)
    def _():
        def body(i, carry):
            for k in range(3):
                g = 3 * i + k
                weigh(g, qc_ref, sides, p_ref)
                for h in range(4):
                    sum_ref[g, 2 * TOK * h : 2 * TOK * (h + 1)] = collect(g, h, sides, p_ref)
            return carry

        lax.fori_loop(0, GROUPS // 3, body, 0)

    for copy in copies:
        copy.wait()


def attend_own(step, safe, pay, mine, other, gram, qk, ready, out_weight):
    group = (GROUPS, 8 * TOK, WIDE)
    half = HEADS * HEAD
    held = [in_vmem(v) for v in (other, *gram, *ready)]
    shapes = [pltpu.VMEM(group, F32)] + side_shapes(SIDE)
    scratch = [pltpu.VMEM((8 * TOK, 2 * SIDE), BF)]
    if step == 0:
        held.append(in_hbm(out_weight))
        shapes.append(pltpu.VMEM((half, out_weight.shape[1]), BF))
        scratch.append(pltpu.SemaphoreType.DMA)
    else:
        held += [in_vmem(v) for v in (pay, mine, qk)]
        shapes.append(pltpu.VMEM(group, BF))
        scratch.append(pltpu.VMEM((half, WIDE), BF))
    return pl.pallas_call(
        functools.partial(own_kernel, step),
        out_shape=shapes,
        in_specs=[SMEM] + [VMEM] * (len(held) - 1) + [ANY if step == 0 else VMEM],
        out_specs=[VMEM] * len(shapes),
        scratch_shapes=scratch,
        compiler_params=pltpu.CompilerParams(vmem_limit_bytes=14 * 2**20),
        cost_estimate=cost(HEADS * 2 * TOK * WIDE * 4 * SIDE),
        name="attend_own",
    )(safe, *held)


def prev_kernel(
    step,
    safe_ref,
    other_ref,
    gram_hi_ref,
    gram_lo_ref,
    sum_ref,
    qc_ref,
    ak_ref,
    xkt_a_ref,
    val_a_ref,
    rk_a_ref,
    xkt_b_ref,
    val_b_ref,
    rk_b_ref,
    xkt_c_ref,
    val_c_ref,
    rk_c_ref,
    av_ref,
    hidden_ref,
    w_ref,
    part_ref,
    part_other_ref,
    xkt_d_ref,
    val_d_ref,
    rk_d_ref,
    p_ref,
    s_ref,
    z_ref,
):
    own = ((xkt_a_ref, val_a_ref, rk_a_ref), (xkt_b_ref, val_b_ref, rk_b_ref))
    prev = ((xkt_c_ref, val_c_ref, rk_c_ref), (xkt_d_ref, val_d_ref, rk_d_ref))
    prepare(step, 1, (other_ref,), gram_hi_ref, gram_lo_ref, ak_ref, *prev[1])

    def settle(g, h, z):
        z_ref[g, 2 * TOK * h : 2 * TOK * (h + 1)] = (z * (1.0 / z[:, ONE : ONE + 1])).astype(BF)

    @pl.when(safe_ref[0] == 1)
    def _():
        def body(i, carry):
            for k in range(3):
                g = 3 * i + k
                weigh(g, qc_ref, prev, p_ref)
                for h in range(4):
                    settle(g, h, collect(g, h, prev, p_ref) + sum_ref[g, 2 * TOK * h : 2 * TOK * (h + 1)])
            return carry

        lax.fori_loop(0, GROUPS // 3, body, 0)

    @pl.when(safe_ref[0] != 1)
    def _():
        every = own + prev
        alone = slot_of(step) == 0

        def body(g, carry):
            for h in range(4):
                span = slice(2 * TOK * h, 2 * TOK * (h + 1))
                for (xkt_ref, _, rk_ref), keys in columns(every):
                    s = dot(qc_ref[g, span], xkt_ref[...]) * rk_ref[g, h : h + 1, :]
                    s_ref[:, keys] = jnp.where(alone, -1e30, s) if keys.start >= 2 * SIDE else s
                s = s_ref[...]
                p_ref[span, :] = jnp.exp2(s - jnp.max(s, axis=1, keepdims=True)).astype(BF)
                settle(g, h, collect(g, h, every, p_ref))
            return carry

        lax.fori_loop(0, GROUPS, body, 0)

    head_of = lanes((2 * TOK, WIDE)) // HEAD
    outs = []
    for g in range(GROUPS):
        o = dot_t(z_ref[g], av_ref[g * WIDE : (g + 1) * WIDE, :])
        picked = jnp.where(head_of == 0, o[0:128], 0.0)
        for h in range(1, 4):
            picked = jnp.where(head_of == h, o[128 * h : 128 * (h + 1)], picked)
        outs.append(picked.astype(BF))
    y = dot(jnp.concatenate(outs, axis=1), w_ref[...])
    part_ref[...] = hidden_ref[...] + y[0:TOK]
    part_other_ref[...] = y[TOK:].astype(BF)


def attend_prev(step, safe, other, gram, begun, ready, weights):
    width = weights.shape[1]
    held = [in_vmem(v) for v in (other, *gram, *begun, *ready, weights)]
    return pl.pallas_call(
        functools.partial(prev_kernel, step),
        out_shape=(pltpu.VMEM((TOK, width), F32), pltpu.VMEM((TOK, width), BF)),
        in_specs=[SMEM] + [VMEM] * len(held),
        out_specs=(VMEM, VMEM),
        scratch_shapes=side_shapes(SIDE)
        + [
            pltpu.VMEM((8 * TOK, 4 * SIDE), BF),
            pltpu.VMEM((2 * TOK, 4 * SIDE), F32),
            pltpu.VMEM((GROUPS, 8 * TOK, WIDE), BF),
        ],
        compiler_params=pltpu.CompilerParams(vmem_limit_bytes=16 * 2**20),
        cost_estimate=cost(HEADS * 2 * TOK * WIDE * 4 * SIDE),
        name="attend_prev",
    )(safe, *held)


def finish_kernel(step, sig_ref, state_ref, part_ref, got_ref, gain_ref, final_ref, fresh_ref, est_ref, new_ref, *sent):
    state = state_ref[...]
    y = part_ref[...] + got_ref[...].astype(F32)
    scale = lax.rsqrt(jnp.mean(y * y, axis=1, keepdims=True) + EPS)
    velocity = dot((y * scale * gain_ref[...]).astype(BF), final_ref[...])
    est_ref[...] = state - sig_ref[2 * step] * velocity
    new = jnp.where(slot_of(step) == 0, fresh_ref[step], state + sig_ref[2 * step + 1] * velocity)
    new_ref[...] = new
    for sent_ref in sent:
        for chip in range(CHIPS):
            sent_ref[chip] = new.astype(BF)


def finish(step, sig, state, part, got, gain, final_weight, fresh):
    out = jax.ShapeDtypeStruct(state.shape, F32)
    shapes = [out, out]
    if step + 1 < STEPS:
        shapes.append(pltpu.VMEM((CHIPS,) + state.shape, BF))
    return pl.pallas_call(
        functools.partial(finish_kernel, step),
        out_shape=shapes,
        in_specs=[SMEM] + [VMEM] * 6,
        out_specs=[VMEM] * len(shapes),
        compiler_params=pltpu.CompilerParams(vmem_limit_bytes=12 * 2**20),
        name="finish",
    )(sig, *[in_vmem(v) for v in (state, part, got, gain, final_weight, fresh)])


def leave_kernel(queue_ref, second_ref, first_ref, est_ref, out_ref, sems):
    pairs = ((first_ref, est_ref.at[0, 0]), (second_ref, est_ref.at[1, 0]), (queue_ref, out_ref.at[0]))
    copies = [pltpu.make_async_copy(src, dst, sems.at[i]) for i, (src, dst) in enumerate(pairs)]
    for copy in copies:
        copy.start()
    for copy in copies:
        copy.wait()


def leave(first, second, queue):
    return pl.pallas_call(
        leave_kernel,
        out_shape=(
            jax.ShapeDtypeStruct((STEPS, 1) + first.shape, F32),
            jax.ShapeDtypeStruct((1,) + queue.shape, F32),
        ),
        in_specs=[VMEM] * 3,
        out_specs=(ANY, ANY),
        scratch_shapes=[pltpu.SemaphoreType.DMA((3,))],
        name="leave",
    )(in_vmem(queue), in_vmem(second), in_vmem(first))


def passed_along(x, by):
    peers = lax.axis_size("frame")
    return lax.ppermute(x, "frame", [(i, (i + by) % peers) for i in range(peers)])


def swapped(x):
    return lax.ppermute(x, "core", [(0, 1), (1, 0)])


def spread(x):
    return lax.all_to_all(x, ("y", "far"), 0, 0, tiled=True)


def shards(
    latents,
    fresh_noise,
    level_index,
    plan,
    frame_ids,
    in_weight,
    cond_gain,
    norm_gain,
    qkv_weight,
    qk_gain,
    out_weight,
    final_gain,
    final_weight,
):
    half = in_weight.shape[1] // 2
    freq = jnp.asarray(np.exp(-math.log(10000.0) * np.arange(half, dtype=np.float32) / half), F32)
    state = latents[0]
    partner = swapped(state)
    sent, gram_hi, gram_lo, cond, qk, safe, sig = fold(
        level_index,
        plan,
        frame_ids,
        freq[None],
        jnp.swapaxes(qkv_weight, 1, 2),
        in_weight,
        cond_gain,
        norm_gain[None],
        qk_gain,
        latents,
    )
    gram = (gram_hi, gram_lo)
    sent, partner = lax.optimization_barrier((sent, partner))
    pay = spread(sent)
    mine = pay[:, PAY - TOK :, :]
    results = []
    for step in range(STEPS):
        other = swapped(mine)
        before = passed_along(mine, 1)
        ready = list(prepared_own(step, pay, mine, gram, qk, partner))
        if step == 0:
            sums, *keys, weights = attend_own(step, safe, pay, mine, other, gram, qk, ready, out_weight)
            queried = ready.pop()
        else:
            sums, *keys, queried = attend_own(step, safe, pay, mine, other, gram, qk, ready, out_weight)
        begun = [sums, queried, *ready, *keys]
        before, *begun = lax.optimization_barrier((before, *begun))
        before_other = swapped(before)
        ready = prepared(step, begun[2], before, gram, pay, state, in_weight, cond)
        part, part_other = attend_prev(step, safe, before_other, gram, begun, ready, weights)
        got = swapped(part_other)
        estimate, state, *sent = finish(step, sig, state, part, got, final_gain[None], final_weight, fresh_noise)
        results.append(estimate)
        if sent:
            mine = spread(sent[0])
    queue = passed_along(state, -2)
    return leave(results[0], passed_along(results[1], -1), queue)


def solution(mesh):
    split = Mesh(mesh.devices.reshape(8, 4, 2, 2), ("frame", "y", "far", "core"))
    space = ("y", "far", "core")
    in_specs = (
        P("frame", space, None),
        P(None, space, None),
        P(),
        P(),
        P(),
        P(),
        P(),
        P(),
        P(None, None, space),
        P(),
        P(),
        P(),
        P(),
    )
    out_specs = (P(None, "frame", space, None), P("frame", space, None))
    return jax.shard_map(shards, mesh=split, in_specs=in_specs, out_specs=out_specs, check_vma=False)
```
